32 devices in a mesh: section: 4 (over y, x), dp: 8 (over z, core).
Axes of the slice: x: 2, y: 2, z: 4, core: 2. Of those that a mesh axis runs over, the one named last changes fastest.
Arguments:
- arrive: bfloat16 [4, 512, 4096], P('section', 'dp'), may hold values from -6 to 6
- entering: bfloat16 [2, 512, 4096], P(None, 'dp'), may hold values from -6 to 6
- stash: bfloat16 [4, 3, 512, 4096], P('section', None, 'dp'), may hold values from -6 to 6
- back_arrive: bfloat16 [4, 512, 4096], P('section', 'dp'), may hold values from -6 to 6
- head_grad: bfloat16 [2, 512, 4096], P(None, 'dp'), may hold values from -6 to 6
- norm_gain: float32 [4, 4096], P('section'), may hold values from 0.5 to 1.5
- router: float32 [4, 4096], P('section'), may hold values from -0.09375 to 0.09375
- w_up: bfloat16 [4, 4096, 8192], P('section', None, 'dp'), may hold values from -0.09375 to 0.09375
- w_down: bfloat16 [4, 8192, 4096], P('section', 'dp'), may hold values from -0.0625 to 0.0625
- routes: int32 [4, 3, 2, 96], P('section', None, None, 'dp'), may hold values from -1 to 63, as said below
Outputs:
- fwd_out: bfloat16 [4, 3, 512, 4096], P('section', None, 'dp')
- bwd_out: bfloat16 [4, 3, 512, 4096], P('section', None, 'dp')
- router_grad: float32 [4, 4096], P('section')
The draws below stay inside these ranges and needn't reach their ends.
Inputs may be any that keep to these rules, and one draw needn't show every extreme that they name: `routes`: in each list, the 12 slots of each device name 1 to 12 distinct rows of that device's 64 tokens, filled slots first and -1 after them; in every list some device fills all 12 slots.
All inputs are finite; a program needn't handle non-finite values.
Results may differ from the reference program's by a relative error of at most 0.015.
Values may be sent and summed in bfloat16 or wider, within the bound.
No kernel may reach another device: no remote copies, remote signals or barrier semaphores. Data moves between devices by JAX's collectives and lax.ppermute only.
A program may use at most 128 MiB of HBM per device.

```python
import jax
import jax.numpy as jnp
from jax import lax

D = 4096
FF = 8192
TOK_MB = 64
TICKS = 3
SECTIONS = 4
TOKENS = 512
CAP = 12
SLOTS = 96
SHARE = 1024
N_DP = 8


def draw_routes(key, part):
    key = jax.random.fold_in(key, 11)
    key_count, key_top, key_order = jax.random.split(key, 3)
    counts = jax.random.randint(key_count, (SECTIONS, TICKS, 2, N_DP), 1, CAP + 1)
    fullest = jax.random.randint(key_top, (SECTIONS, TICKS, 2, 1), 0, N_DP)
    device_ids = jnp.arange(N_DP, dtype=jnp.int32)
    counts = jnp.where(device_ids == fullest, CAP, counts)
    scores = jax.random.randint(key_order, (SECTIONS, TICKS, 2, N_DP, TOK_MB), 0, 2 ** 20) * TOK_MB
    scores = scores + jnp.arange(TOK_MB, dtype=jnp.int32)
    order = jnp.argsort(scores, axis=-1)[..., :CAP].astype(jnp.int32)
    slot_ids = jnp.arange(CAP, dtype=jnp.int32)
    lists = jnp.where(slot_ids < counts[..., None], order, -1)
    return lists.reshape(SECTIONS, TICKS, 2, N_DP * CAP).astype(jnp.int32)


def steps_of(own_key, dims, pieces, least, top_value):
    factor_of, own = 1.0, jax.random.fold_in(own_key, 6)
    for position, blocks in pieces:
        draws = jnp.exp(jax.random.uniform(jax.random.fold_in(own, position), (blocks,), jnp.float32, least / len(pieces), top_value / len(pieces)))
        factor_of = factor_of * jnp.repeat(draws, dims[position] // blocks).reshape([-1 if axis == position else 1 for axis in range(len(dims))])
    return factor_of


def gaussian(stream_key, extent, scale, reach, shards=(), held_as=jnp.bfloat16):
    drawn = scale * jax.random.normal(stream_key, extent, jnp.float32)
    if shards:
        drawn = drawn * steps_of(stream_key, extent, shards, -0.22, 0.18)
    return jnp.clip(drawn, -reach, reach).astype(held_as)


def setup_inputs(seed: int = 0) -> dict:
    splits = jax.random.split(jax.random.key(seed), 11)
    arrive = gaussian(splits[0], (SECTIONS, TOKENS, D), 1.0, 6.0, ((0, 4), (1, 8)))
    entering = gaussian(splits[1], (TICKS - 1, TOKENS, D), 1.0, 6.0, ((1, 8),))
    stash = gaussian(splits[2], (SECTIONS, TICKS, TOKENS, D), 1.0, 6.0, ((0, 4), (2, 8)))
    back_arrive = gaussian(splits[3], (SECTIONS, TOKENS, D), 1.0, 6.0, ((0, 4), (1, 8)))
    head_grad = gaussian(splits[4], (TICKS - 1, TOKENS, D), 1.0, 6.0, ((1, 8),))
    norm_gain = jnp.clip(1.0 + 0.1 * jax.random.normal(splits[5], (SECTIONS, D), jnp.float32), 0.5, 1.5)
    router = gaussian(splits[6], (SECTIONS, D), D ** -0.5, 0.09375, ((0, 4),), jnp.float32)
    w_up = gaussian(splits[7], (SECTIONS, D, FF), D ** -0.5, 0.09375, ((0, 4), (2, 8)))
    w_down = gaussian(splits[8], (SECTIONS, FF, D), FF ** -0.5, 0.0625, ((0, 4), (1, 8)))
    routes = draw_routes(jax.random.fold_in(splits[10], 71), 0)
    return dict(arrive=arrive, entering=entering, stash=stash, back_arrive=back_arrive, head_grad=head_grad, norm_gain=norm_gain, router=router, w_up=w_up, w_down=w_down, routes=routes)


EPS = 1e-05

def take_rows(activity, route):
    slot_owner = jnp.arange(SLOTS, dtype=jnp.int32) // CAP
    valid_slot = route >= 0
    row_index = (slot_owner * TOK_MB + jnp.where(valid_slot, route, 0)).astype(jnp.int32)
    store_index = jnp.where(valid_slot, row_index, TOKENS).astype(jnp.int32)
    picked = activity[row_index].astype(jnp.float32) * valid_slot[:, None].astype(jnp.float32)
    return (picked, row_index, store_index, valid_slot)

def normalize(picked, gain, router_vec):
    inv_rms = lax.rsqrt(lax.optimization_barrier(jnp.mean(picked * picked, axis=-1, keepdims=True)) + EPS)
    normed = (picked * inv_rms * gain).astype(jnp.bfloat16)
    gate_value = jax.nn.sigmoid(jnp.dot(normed.astype(jnp.float32), router_vec, precision=lax.Precision.HIGHEST))
    return (inv_rms, normed, gate_value)

def share_sum(parts):
    rounded = lax.optimization_barrier(parts.astype(jnp.bfloat16))
    return lax.optimization_barrier(jnp.sum(rounded.astype(jnp.float32), axis=0))

def up_hidden(normed, up_weight):
    up_proj = jnp.dot(normed, up_weight, preferred_element_type=jnp.float32)
    sigmoid_up = jax.nn.sigmoid(up_proj)
    hidden = (up_proj * sigmoid_up).astype(jnp.bfloat16)
    return (up_proj, sigmoid_up, hidden)

def block_forward(activity, route, gain, router_vec, up_weight, down_weight):
    picked, row_index, store_index, valid_slot = take_rows(activity, route)
    inv_rms, normed, gate_value = normalize(picked, gain, router_vec)
    up_proj, sigmoid_up, hidden = up_hidden(normed, up_weight)
    parts = jnp.einsum('snk,nkd->nsd', hidden.astype(jnp.float32).reshape(SLOTS, N_DP, SHARE), down_weight.astype(jnp.float32).reshape(N_DP, SHARE, D))
    block_out = share_sum(parts)
    renewed = (picked + gate_value[:, None] * block_out).astype(jnp.bfloat16)
    return activity.at[store_index].set(renewed, mode='drop')

def block_backward(saved, cotangent, route, gain, router_vec, up_weight, down_weight):
    picked, row_index, store_index, valid_slot = take_rows(saved, route)
    inv_rms, normed, gate_value = normalize(picked, gain, router_vec)
    up_proj, sigmoid_up, hidden = up_hidden(normed, up_weight)
    upstream = cotangent[row_index].astype(jnp.float32) * valid_slot[:, None].astype(jnp.float32)
    scaled = (gate_value[:, None] * upstream).astype(jnp.bfloat16)
    grad_hidden = jnp.dot(scaled, down_weight.T, preferred_element_type=jnp.float32)
    inner_parts = lax.optimization_barrier(jnp.sum((grad_hidden * hidden.astype(jnp.float32)).reshape(SLOTS, N_DP, SHARE), axis=-1)).T
    inner = share_sum(inner_parts)
    grad_up = (grad_hidden * sigmoid_up * (1.0 + up_proj * (1.0 - sigmoid_up))).astype(jnp.bfloat16)
    norm_parts = jnp.einsum('snk,dnk->nsd', grad_up.astype(jnp.float32).reshape(SLOTS, N_DP, SHARE), up_weight.astype(jnp.float32).reshape(D, N_DP, SHARE))
    grad_norm = share_sum(norm_parts)
    logit_grad = inner * (1.0 - gate_value)
    grad_normed = grad_norm + logit_grad[:, None] * router_vec
    scaled_grad = grad_normed * gain
    unit_rows = picked * inv_rms
    grad_rows = inv_rms * (scaled_grad - unit_rows * lax.optimization_barrier(jnp.mean(scaled_grad * unit_rows, axis=-1, keepdims=True)))
    renewed = (upstream + grad_rows).astype(jnp.bfloat16)
    result = cotangent.at[store_index].set(renewed, mode='drop')
    router_term = lax.optimization_barrier(jnp.sum(logit_grad[:, None] * normed.astype(jnp.float32), axis=0))
    return (result, router_term)

def one_section(operands):
    forward_in, backward_in, saved, route_fwd, route_bwd, gain, router_vec, up_weight, down_weight = operands
    forward_res = block_forward(forward_in, route_fwd, gain, router_vec, up_weight, down_weight)
    backward_res, router_term = block_backward(saved, backward_in, route_bwd, gain, router_vec, up_weight, down_weight)
    return (forward_res, backward_res, router_term)

def reference(arrive, entering, stash, back_arrive, head_grad, norm_gain, router, w_up, w_down, routes):
    forward_in = arrive
    backward_in = back_arrive
    forward_list = []
    backward_list = []
    router_total = jnp.zeros((SECTIONS, D), jnp.float32)
    for tick in range(TICKS):
        if tick > 0:
            forward_in = jnp.concatenate([entering[tick - 1][None], forward_prev[:-1]], axis=0)
            backward_in = jnp.concatenate([backward_prev[1:], head_grad[tick - 1][None]], axis=0)
        forward_prev, backward_prev, router_term = lax.map(one_section, (forward_in, backward_in, stash[:, tick], routes[:, tick, 0], routes[:, tick, 1], norm_gain, router, w_up, w_down))
        forward_list.append(forward_prev)
        backward_list.append(backward_prev)
        router_total = router_total + router_term
    return (jnp.stack(forward_list, axis=1), jnp.stack(backward_list, axis=1), router_total / float(TICKS * SLOTS))
```

```python
import jax
import jax.numpy as jnp
from jax import lax
from jax.sharding import PartitionSpec as P

EPS = 1e-05
CORES = 2


def shift_section(block, step):
    count = lax.axis_size("section")
    route = [(i - step, i) for i in range(count) if 0 <= i - step < count]
    return lax.ppermute(block, "section", route)


def swap_core(block):
    count = lax.axis_size("dp")
    return lax.ppermute(block, "dp", [(i, i ^ 1) for i in range(count)])


def shift_chip(block, step):
    count = lax.axis_size("dp")
    return lax.ppermute(block, "dp", [(i, (i + CORES * step) % count) for i in range(count)])


def gather_rows(rows):
    chips = lax.axis_size("dp") // CORES
    count, width = rows.shape
    half = width // 2
    packed = jnp.concatenate([rows[:, :half], rows[:, half:]], axis=0)
    own_core = jnp.stack([packed] + [shift_chip(packed, j) for j in range(1, chips)], axis=0)
    other_core = swap_core(own_core)
    both = jnp.stack([own_core, other_core], axis=0)
    both = both.reshape(CORES * chips, 2, count, half).swapaxes(1, 2)
    return both.reshape(CORES * chips * count, width)


def scatter_sum(parts):
    chips = lax.axis_size("dp") // CORES
    width = parts.shape[1]
    half = width // 2
    count = parts.shape[0] // (CORES * chips)
    parts = parts.reshape(CORES, chips, count, 2, half).swapaxes(2, 3)
    parts = parts.reshape(CORES, chips, 2 * count, half)
    crossed = swap_core(parts[1].astype(jnp.bfloat16))
    summed = parts[0] + crossed.astype(jnp.float32)
    total = summed[0]
    for j in range(1, chips):
        total = total + shift_chip(summed[j].astype(jnp.bfloat16), -j).astype(jnp.float32)
    return jnp.concatenate([total[:count], total[count:]], axis=1)


def one_hot(route, size):
    return (route[:, None] == jnp.arange(size, dtype=route.dtype)[None, :]).astype(jnp.bfloat16)


def pick(activity, hot):
    return jnp.dot(hot, activity, preferred_element_type=jnp.float32)


def put(activity, hot, rows):
    taken = jnp.sum(hot.astype(jnp.float32), axis=0) > 0.5
    moved = lax.dot_general(
        hot, rows, (((0,), (0,)), ((), ())), preferred_element_type=jnp.float32
    ).astype(jnp.bfloat16)
    return jnp.where(taken[:, None], moved, activity)


def normalize(picked, gain):
    inv_rms = lax.rsqrt(jnp.mean(picked * picked, axis=-1, keepdims=True) + EPS)
    return inv_rms, (picked * inv_rms * gain).astype(jnp.bfloat16)


def gate_of(normed, router_vec):
    return jax.nn.sigmoid(
        jnp.dot(normed.astype(jnp.float32), router_vec, precision=lax.Precision.HIGHEST)
    )


def per_device(
    arrive, entering, stash, back_arrive, head_grad, norm_gain, router, w_up, w_down, routes
):
    section = lax.axis_index("section")
    last = lax.axis_size("section") - 1
    dp_count = lax.axis_size("dp")
    gain = norm_gain[0]
    router_vec = router[0]
    up_weight = w_up[0]
    down_weight = w_down[0]
    slots = routes.shape[3]
    tokens = arrive.shape[1]
    width = arrive.shape[2]
    ticks = stash.shape[1]
    contract_last = (((1,), (1,)), ((), ()))

    hot_f = [one_hot(routes[0, k, 0], tokens) for k in range(ticks)]
    hot_b = [one_hot(routes[0, k, 1], tokens) for k in range(ticks)]
    route_behind = shift_section(routes[0, :, 0], 1)
    route_ahead = shift_section(routes[0, :, 1], -1)
    route_behind = jnp.where(section == 0, -1, route_behind)
    route_ahead = jnp.where(section == last, -1, route_ahead)
    hot_behind = [one_hot(route_behind[k], tokens) for k in range(ticks)]
    hot_ahead = [one_hot(route_ahead[k], tokens) for k in range(ticks)]

    forward_in = arrive[0]
    backward_in = back_arrive[0]
    forward_rows = pick(forward_in, hot_f[0])
    backward_rows = pick(backward_in, hot_b[0]).astype(jnp.bfloat16)

    saved = jnp.stack([pick(stash[0, k], hot_b[k]) for k in range(ticks)], axis=0)
    saved_rms, saved_normed = normalize(saved, gain)

    forward_rms, forward_normed = normalize(forward_rows, gain)
    forward_all = gather_rows(forward_normed)
    saved_all = gather_rows(saved_normed.reshape(ticks * slots, width))
    saved_gate = gate_of(saved_all, router_vec).reshape(dp_count, ticks, slots)
    saved_up = jnp.dot(saved_all, up_weight, preferred_element_type=jnp.float32)
    saved_up = saved_up.reshape(dp_count, ticks, slots, -1)
    saved_all = saved_all.reshape(dp_count, ticks, slots, width)

    forward_list = []
    backward_list = []
    logit_list = []
    for k in range(ticks):
        if k + 1 < ticks:
            forward_base = shift_section(forward_in, 1)
            backward_base = shift_section(backward_in, -1)

        if k > 0:
            forward_rms, forward_normed = normalize(forward_rows, gain)
            forward_all = gather_rows(forward_normed)
        gate = gate_of(forward_normed, router_vec)
        up = jnp.dot(forward_all, up_weight, preferred_element_type=jnp.float32)
        hidden = (up * jax.nn.sigmoid(up)).astype(jnp.bfloat16)
        block = scatter_sum(jnp.dot(hidden, down_weight, preferred_element_type=jnp.float32))
        forward_new = (forward_rows + gate[:, None] * block).astype(jnp.bfloat16)
        forward_list.append(put(forward_in, hot_f[k], forward_new))

        gate_all = saved_gate[:, k].reshape(dp_count * slots, 1)
        up_b = saved_up[:, k].reshape(dp_count * slots, -1)
        upstream_all = gather_rows(backward_rows)
        grad_hidden = gate_all * lax.dot_general(
            upstream_all, down_weight, contract_last, preferred_element_type=jnp.float32
        )
        sig = jax.nn.sigmoid(up_b)
        inner = jnp.sum(grad_hidden * (up_b * sig), axis=-1, keepdims=True)
        logit = inner * (1.0 - gate_all)
        logit_list.append(logit)
        grad_up = (grad_hidden * sig * (1.0 + up_b * (1.0 - sig))).astype(jnp.bfloat16)
        grad_part = lax.dot_general(
            grad_up, up_weight, contract_last, preferred_element_type=jnp.float32
        )
        grad_normed = scatter_sum(grad_part + logit * router_vec)
        scaled_grad = grad_normed * gain
        unit = saved[k] * saved_rms[k]
        grad_rows = saved_rms[k] * (
            scaled_grad - unit * jnp.mean(scaled_grad * unit, axis=-1, keepdims=True)
        )
        backward_new = (backward_rows.astype(jnp.float32) + grad_rows).astype(jnp.bfloat16)
        backward_list.append(put(backward_in, hot_b[k], backward_new))

        if k + 1 < ticks:
            forward_moved = shift_section(forward_new, 1)
            backward_moved = shift_section(backward_new, -1)
            match_f = routes[0, k + 1, 0][:, None] == route_behind[k][None, :]
            match_f = match_f & (route_behind[k] >= 0)[None, :]
            match_b = routes[0, k + 1, 1][:, None] == route_ahead[k][None, :]
            match_b = match_b & (route_ahead[k] >= 0)[None, :]
            source_f = jnp.where(section == 0, entering[k], forward_base)
            source_b = jnp.where(section == last, head_grad[k], backward_base)
            forward_rows = jnp.where(
                jnp.any(match_f, axis=1, keepdims=True),
                jnp.dot(
                    match_f.astype(jnp.bfloat16), forward_moved, preferred_element_type=jnp.float32
                ),
                pick(source_f, hot_f[k + 1]),
            )
            backward_rows = jnp.where(
                jnp.any(match_b, axis=1, keepdims=True),
                jnp.dot(
                    match_b.astype(jnp.bfloat16), backward_moved, preferred_element_type=jnp.float32
                ),
                pick(source_b, hot_b[k + 1]),
            ).astype(jnp.bfloat16)
            forward_in = put(source_f, hot_behind[k], forward_moved)
            backward_in = put(source_b, hot_ahead[k], backward_moved)

    logits = jnp.stack(logit_list, axis=0).reshape(ticks, dp_count, slots).swapaxes(0, 1)
    router_sum = jnp.einsum(
        "dts,dtsw->w", logits, saved_all.astype(jnp.float32), precision=lax.Precision.HIGHEST
    )[None]
    chips = dp_count // CORES
    router_sum = router_sum + swap_core(router_sum)
    by_distance = jnp.concatenate(
        [router_sum] + [shift_chip(router_sum, j) for j in range(1, chips)], axis=0
    )
    chip = lax.axis_index("dp") // CORES
    total = jnp.zeros_like(router_sum)
    for j in range(chips):
        total = total + lax.dynamic_slice_in_dim(by_distance, (chip - j) % chips, 1, 0)
    scale = 1.0 / float(ticks * slots * dp_count)
    return (
        jnp.stack(forward_list, axis=0)[None],
        jnp.stack(backward_list, axis=0)[None],
        total * scale,
    )


def solution(mesh):
    in_specs = (
        P("section", "dp", None),
        P(None, "dp", None),
        P("section", None, "dp", None),
        P("section", "dp", None),
        P(None, "dp", None),
        P("section", None),
        P("section", None),
        P("section", None, "dp"),
        P("section", "dp", None),
        P("section", None, None, "dp"),
    )
    out_specs = (P("section", None, "dp", None), P("section", None, "dp", None), P("section", None))
    return jax.shard_map(
        per_device, mesh=mesh, in_specs=in_specs, out_specs=out_specs, check_vma=False
    )
```

```python
import functools

import jax
import jax.numpy as jnp
from jax import lax
from jax.experimental import pallas as pl
from jax.experimental.pallas import tpu as pltpu
from jax.sharding import PartitionSpec as P

EPS = 1e-05
CORES = 2
CHUNK = 256
BF16 = jnp.bfloat16
F32 = jnp.float32
NN = (((1,), (0,)), ((), ()))
NT = (((1,), (1,)), ((), ()))
VMEM = pl.BlockSpec(memory_space=pltpu.VMEM)
SMEM = pl.BlockSpec(memory_space=pltpu.SMEM)


def shift_section(block, step):
    count = lax.axis_size("section")
    route = [(i - step, i) for i in range(count) if 0 <= i - step < count]
    return lax.ppermute(block, "section", route)


def swap_core(block):
    count = lax.axis_size("dp")
    return lax.ppermute(block, "dp", [(i, i ^ 1) for i in range(count)])


def shift_chip(block, step):
    count = lax.axis_size("dp")
    return lax.ppermute(block, "dp", [(i, (i + CORES * step) % count) for i in range(count)])


def gather_rows(packed):
    chips = lax.axis_size("dp") // CORES
    own = [packed] + [shift_chip(packed, j) for j in range(1, chips)]
    return own + [swap_core(block) for block in own]


def dot(a, b, dims=NN):
    return lax.dot_general(a, b, dims, preferred_element_type=F32)


def halves(column):
    rows = column.shape[0]
    wide = jnp.broadcast_to(column, (rows, 128))
    return (wide + pltpu.roll(wide, rows // 2, 0))[:, :1]


def top_rows(rows, period):
    return lax.rem(lax.broadcasted_iota(jnp.int32, (rows, 1), 0), period) < period // 2


def pick(activity, route_column):
    rows, half = route_column.shape[0], activity.shape[1] // 2
    tokens = activity.shape[0]
    hit = route_column == lax.broadcasted_iota(jnp.int32, (rows, tokens), 1)
    top = top_rows(rows, rows)
    left = jnp.where(hit & top, 1.0, 0.0).astype(BF16)
    right = jnp.where(hit & jnp.logical_not(top), 1.0, 0.0).astype(BF16)
    return dot(left, activity[:, :half]) + dot(right, activity[:, half:])


def put(activity, rows, route_row):
    tokens, half = activity.shape[0], activity.shape[1] // 2
    count = route_row.shape[1]
    hit = route_row == lax.broadcasted_iota(jnp.int32, (tokens, count), 0)
    first = lax.broadcasted_iota(jnp.int32, (tokens, count), 1) < count // 2
    left = jnp.where(hit & first, 1.0, 0.0)
    right = jnp.where(hit & jnp.logical_not(first), 1.0, 0.0)
    taken = jnp.sum(left, axis=1, keepdims=True) > 0.5
    new_left = jnp.where(taken, dot(left.astype(BF16), rows), activity[:, :half].astype(F32))
    new_right = jnp.where(taken, dot(right.astype(BF16), rows), activity[:, half:].astype(F32))
    return new_left.astype(BF16), new_right.astype(BF16)


def by_half(vector, rows):
    half = vector.shape[1] // 2
    return jnp.where(top_rows(rows, rows), vector[:, :half], vector[:, half:])


def inverse_rms(rows):
    width = 2 * rows.shape[1]
    mean = halves(jnp.sum(rows * rows, axis=1, keepdims=True)) / width
    return lax.rsqrt(mean + EPS)


def normalize(rows, gain, router):
    normed = (rows * inverse_rms(rows) * by_half(gain, rows.shape[0])).astype(BF16)
    logit = jnp.sum(normed.astype(F32) * by_half(router, rows.shape[0]), axis=1, keepdims=True)
    return normed, jax.nn.sigmoid(halves(logit))


def stack_blocks(refs, out):
    out[...] = jnp.concatenate([ref[...].astype(F32) for ref in refs], axis=0).astype(BF16)


def join_halves(left, right, period):
    rows = left.shape[0]
    top = top_rows(rows, period)
    return jnp.where(
        top,
        left + pltpu.roll(right, rows - period // 2, 0),
        right + pltpu.roll(left, period // 2, 0),
    )


def first_forward_kernel(act, column, gain, router, rows_out, normed_out, gate_out):
    rows = pick(act[...], column[...])
    normed, gate = normalize(rows, gain[...], router[...])
    rows_out[...] = rows.astype(BF16)
    normed_out[...] = normed
    gate_out[...] = jnp.broadcast_to(gate, gate_out.shape)


def first_backward_kernel(ticks, act, stash, columns, gain, rows_out, saved_out, normed_out):
    rows_out[...] = pick(act[...], columns[0]).astype(BF16)
    for k in range(ticks):
        rows = pick(stash[k], columns[k])
        saved_out[k] = rows.astype(BF16)
        count = rows.shape[0]
        normed_out[k] = (rows * inverse_rms(rows) * by_half(gain[...], count)).astype(BF16)


def source_kernel(flag, moved, fresh, column, source_out, rows_out):
    source = jnp.where(flag[0] == 1, fresh[...], moved[...])
    source_out[...] = source
    rows_out[...] = pick(source, column[...]).astype(BF16)


def select(base, moved, column, behind_row):
    rows = column.shape[0]
    hit = column == behind_row
    same = top_rows(rows, rows) == (lax.broadcasted_iota(jnp.int32, (rows, rows), 1) < rows // 2)
    match = jnp.where(hit & same, 1.0, 0.0)
    found = jnp.max(match, axis=1, keepdims=True) > 0.5
    return jnp.where(found, dot(match.astype(BF16), moved), base.astype(F32))


def next_forward_kernel(
    base, moved, column, behind_row, gain, router, rows_out, normed_out, gate_out
):
    rows = select(base[...], moved[...], column[...], behind_row[...])
    normed, gate = normalize(rows, gain[...], router[...])
    rows_out[...] = rows.astype(BF16)
    normed_out[...] = normed
    gate_out[...] = jnp.broadcast_to(gate, gate_out.shape)


def next_backward_kernel(base, moved, column, ahead_row, rows_out):
    rows_out[...] = select(base[...], moved[...], column[...], ahead_row[...]).astype(BF16)


def land_kernel(source, moved, row, out):
    half = source.shape[1] // 2
    left, right = put(source[...], moved[...], row[...])
    out[:, :half] = left
    out[:, half:] = right


def output_kernel(act, rows, row, *outs):
    out = outs[-1]
    half = act.shape[1] // 2
    left, right = put(act[...], rows[...], row[...])
    out[0, 0, :, :half] = left
    out[0, 0, :, half:] = right


def forward_kernel(count, *refs):
    blocks = refs[:count]
    up, down, own_out, cross_out, rows, total = refs[count:]
    step, steps = pl.program_id(0), pl.num_programs(0)
    period, half = blocks[0].shape

    @pl.when(step == 0)
    def _():
        stack_blocks(blocks, rows)
        total[...] = jnp.zeros_like(total)

    x = rows[...]
    top = top_rows(x.shape[0], period)
    u = join_halves(dot(x, up[:half, :]), dot(x, up[half:, :]), period)
    hidden = u * jax.nn.sigmoid(u)
    left = jnp.where(top, hidden, 0.0).astype(BF16)
    right = jnp.where(top, 0.0, hidden).astype(BF16)
    total[...] += dot(left, down[:, :half]) + dot(right, down[:, half:])

    @pl.when(step == steps - 1)
    def _():
        write_blocks(total, own_out, cross_out)


def write_blocks(total, own_out, cross_out):
    chips, period, _ = own_out.shape
    for j in range(chips):
        own_out[j] = total[j * period : (j + 1) * period, :]
        low = (chips + j) * period
        cross_out[j] = total[low : low + period, :].astype(BF16)


def backward_kernel(count, *refs):
    normed_blocks = refs[:count]
    grad_blocks = refs[count : 2 * count]
    up, down, router, term_in, own_out, cross_out, term_out, x_n, x_g, total, gate, inner = refs[
        2 * count :
    ]
    step, steps = pl.program_id(0), pl.num_programs(0)
    period, half = grad_blocks[0].shape
    all_rows = x_n.shape[0]
    top = top_rows(all_rows, period)

    @pl.when(step == 0)
    def _():
        stack_blocks(normed_blocks, x_n)
        stack_blocks(grad_blocks, x_g)
        total[...] = jnp.zeros_like(total)
        inner[...] = jnp.zeros_like(inner)
        vector = jnp.where(top, router[:, :half], router[:, half:])
        logit = jnp.sum(x_n[...].astype(F32) * vector, axis=1, keepdims=True)
        wide = jnp.broadcast_to(logit, gate.shape)
        gate[...] = jax.nn.sigmoid(join_halves(wide, wide, period))

    x = x_n[...]
    g = x_g[...]
    u = join_halves(dot(x, up[:half, :]), dot(x, up[half:, :]), period)
    grad_hidden = join_halves(dot(g, down[:, :half], NT), dot(g, down[:, half:], NT), period)
    grad_hidden = grad_hidden * gate[:, :1]
    sig = jax.nn.sigmoid(u)
    hidden = (u * sig).astype(BF16).astype(F32)
    inner[...] += jnp.sum(grad_hidden * hidden, axis=1, keepdims=True)
    grad_up = grad_hidden * sig * (1.0 + u * (1.0 - sig))
    left = jnp.where(top, grad_up, 0.0).astype(BF16)
    right = jnp.where(top, 0.0, grad_up).astype(BF16)
    total[...] += dot(left, up[:half, :], NT) + dot(right, up[half:, :], NT)

    @pl.when(step == steps - 1)
    def _():
        logit = inner[...] * (1.0 - gate[...])
        vector = jnp.where(top, router[:, :half], router[:, half:])
        total[...] += logit[:, :1] * vector
        write_blocks(total, own_out, cross_out)
        wide = logit.T[:1]
        first = lax.rem(lax.broadcasted_iota(jnp.int32, (1, all_rows), 1), period) < period // 2
        pieces = []
        rest = wide
        for _ in range(3):
            piece = rest.astype(BF16).astype(F32)
            pieces.append(piece)
            rest = rest - piece
        sums = []
        for side in (first, jnp.logical_not(first)):
            stacked = jnp.concatenate(
                [jnp.where(side, p, 0.0) for p in pieces]
                + [jnp.zeros((5, all_rows), F32)],
                axis=0,
            )
            sums.append(jnp.sum(dot(stacked.astype(BF16), x), axis=0, keepdims=True))
        term_out[...] = term_in[...] + jnp.concatenate(sums, axis=0)


def pair_kernel(own, crossed, own_out, *outs):
    own_out[...] = own[0] + crossed[0].astype(F32)
    for j, out in enumerate(outs):
        out[...] = (own[j + 1] + crossed[j + 1].astype(F32)).astype(BF16)


def forward_end_kernel(rows, gate, own, *refs):
    out = refs[-1]
    block = own[...]
    for ref in refs[:-1]:
        block = block + ref[...].astype(F32)
    out[...] = (rows[...].astype(F32) + gate[:, :1] * block).astype(BF16)


def backward_end_kernel(upstream, saved, gain, own, *refs):
    out = refs[-1]
    grad_normed = own[...]
    for ref in refs[:-1]:
        grad_normed = grad_normed + ref[...].astype(F32)
    picked = saved[...].astype(F32)
    inv_rms = inverse_rms(picked)
    scaled_grad = grad_normed * by_half(gain[...], picked.shape[0])
    unit = picked * inv_rms
    mean = halves(jnp.sum(scaled_grad * unit, axis=1, keepdims=True)) / (2 * picked.shape[1])
    grad_rows = inv_rms * (scaled_grad - unit * mean)
    out[...] = (upstream[...].astype(F32) + grad_rows).astype(BF16)


def call(kernel, outs, *operands, smem=0, **more):
    return pl.pallas_call(
        kernel,
        out_shape=outs,
        in_specs=[SMEM] * smem + [VMEM] * (len(operands) - smem),
        out_specs=jax.tree.map(lambda _: VMEM, outs),
        **more,
    )(*operands)


def shaped(shape, dtype=BF16):
    return jax.ShapeDtypeStruct(tuple(shape), dtype)


def whole(shape):
    return pl.BlockSpec(tuple(shape), lambda i: (0,) * len(shape))


def weight_call(kernel, blocks, extra, outs, scratch, up, down, matmuls):
    width, hidden = up.shape
    chunk = min(CHUNK, hidden)
    rows = len(blocks) * blocks[0].shape[0]
    return pl.pallas_call(
        kernel,
        grid=(hidden // chunk,),
        out_shape=outs,
        in_specs=[whole(b.shape) for b in blocks]
        + [
            pl.BlockSpec((width, chunk), lambda i: (0, i)),
            pl.BlockSpec((chunk, width), lambda i: (i, 0)),
        ]
        + [whole(e.shape) for e in extra],
        out_specs=[whole(o.shape) for o in outs],
        scratch_shapes=scratch,
        compiler_params=pltpu.CompilerParams(vmem_limit_bytes=40 * 2**20),
        cost_estimate=pl.CostEstimate(
            flops=2 * matmuls * rows * width * hidden,
            bytes_accessed=4 * width * hidden,
            transcendentals=rows * hidden,
        ),
    )(*blocks, up, down, *extra)


def scatter_sum(own, cross):
    chips, period, half = own.shape
    crossed = swap_core(cross)
    sums = call(
        pair_kernel,
        [shaped((period, half), F32)] + [shaped((period, half))] * (chips - 1),
        own,
        crossed,
    )
    return [sums[0]] + [shift_chip(sums[j], -j) for j in range(1, chips)]


def per_device(
    arrive, entering, stash, back_arrive, head_grad, norm_gain, router, w_up, w_down, routes
):
    section = lax.axis_index("section")
    last = lax.axis_size("section") - 1
    dp_count = lax.axis_size("dp")
    chips = dp_count // CORES
    up, down = w_up[0], w_down[0]
    slots = routes.shape[3]
    tokens, width = arrive.shape[1:]
    half = width // 2
    ticks = stash.shape[1]
    period = 2 * slots

    route = routes[0]
    twice = jnp.concatenate([route, route], axis=-1)
    columns = twice[..., None]
    columns_f = [columns[k, 0] for k in range(ticks)]
    columns_b = columns[:, 1]
    rows_of = twice[:, :, None, :]
    behind = jnp.where(section == 0, -2, shift_section(twice[:, 0], 1))
    ahead = jnp.where(section == last, -2, shift_section(twice[:, 1], -1))
    behind = jnp.where(behind < 0, -2, behind)[:, None, :]
    ahead = jnp.where(ahead < 0, -2, ahead)[:, None, :]
    at_first = (section == 0).astype(jnp.int32).reshape(1)
    at_last = (section == last).astype(jnp.int32).reshape(1)

    packed = shaped((period, half))
    gate_shape = shaped((period, 128), F32)
    part_outs = [shaped((chips, period, half), F32), shaped((chips, period, half))]
    all_rows = dp_count * period
    scratch_rows = pltpu.VMEM((all_rows, half), BF16)
    scratch_total = pltpu.VMEM((all_rows, half), F32)
    scratch_column = pltpu.VMEM((all_rows, 128), F32)

    forward_in, backward_in = arrive[0], back_arrive[0]
    forward_rows, forward_normed, gate = call(
        first_forward_kernel,
        [packed, packed, gate_shape],
        forward_in,
        columns_f[0],
        norm_gain,
        router,
    )
    backward_rows, saved, saved_normed = call(
        functools.partial(first_backward_kernel, ticks),
        [packed, shaped((ticks, period, half)), shaped((ticks, period, half))],
        backward_in,
        stash[0],
        columns_b,
        norm_gain,
    )
    term = jnp.zeros((2, half), F32)
    forward_out = backward_out = None
    out_shape = shaped((1, ticks, tokens, width))

    def write_out(result, k, act, rows, row):
        before = [] if result is None else [result]
        return pl.pallas_call(
            output_kernel,
            grid=(1,),
            out_shape=out_shape,
            in_specs=[whole(act.shape), whole(rows.shape), whole(row.shape)]
            + [pl.BlockSpec(memory_space=pl.ANY)] * len(before),
            out_specs=pl.BlockSpec((1, 1, tokens, width), lambda i: (0, k, 0, 0)),
            input_output_aliases={3: 0} if before else {},
        )(act, rows, row, *before)

    for k in range(ticks):
        if k + 1 < ticks:
            forward_base = shift_section(forward_in, 1)
            backward_base = shift_section(backward_in, -1)

        blocks = gather_rows(forward_normed)
        own, cross = weight_call(
            functools.partial(forward_kernel, dp_count),
            blocks,
            [],
            part_outs,
            [scratch_rows, scratch_total],
            up,
            down,
            2,
        )
        terms = scatter_sum(own, cross)
        forward_new = call(forward_end_kernel, packed, forward_rows, gate, *terms)

        blocks = gather_rows(saved_normed[k]) + gather_rows(backward_rows)
        own, cross, term = weight_call(
            functools.partial(backward_kernel, dp_count),
            blocks,
            [router, term],
            part_outs + [shaped((2, half), F32)],
            [scratch_rows, scratch_rows, scratch_total, scratch_column, scratch_column],
            up,
            down,
            3,
        )
        terms = scatter_sum(own, cross)
        backward_new = call(
            backward_end_kernel, packed, backward_rows, saved[k], norm_gain, *terms
        )

        forward_out = write_out(forward_out, k, forward_in, forward_new, rows_of[k, 0])
        backward_out = write_out(backward_out, k, backward_in, backward_new, rows_of[k, 1])

        if k + 1 < ticks:
            full = shaped((tokens, width))
            source, base = call(
                source_kernel,
                [full, packed],
                at_first,
                forward_base,
                entering[k],
                columns_f[k + 1],
                smem=1,
            )
            moved = shift_section(forward_new, 1)
            forward_rows, forward_normed, gate = call(
                next_forward_kernel,
                [packed, packed, gate_shape],
                base,
                moved,
                columns_f[k + 1],
                behind[k],
                norm_gain,
                router,
            )
            forward_in = call(land_kernel, full, source, moved, behind[k])

            source, base = call(
                source_kernel,
                [full, packed],
                at_last,
                backward_base,
                head_grad[k],
                columns_b[k + 1],
                smem=1,
            )
            moved = shift_section(backward_new, -1)
            backward_rows = call(
                next_backward_kernel, packed, base, moved, columns_b[k + 1], ahead[k]
            )
            backward_in = call(land_kernel, full, source, moved, ahead[k])

    pair = term + swap_core(term)
    by_distance = jnp.stack([pair] + [shift_chip(pair, j) for j in range(1, chips)], axis=0)
    chip = lax.axis_index("dp") // CORES
    total = jnp.zeros_like(pair)
    for j in range(chips):
        total = total + lax.dynamic_index_in_dim(by_distance, (chip - j) % chips, 0, False)
    scale = 1.0 / float(ticks * slots * dp_count)
    return forward_out, backward_out, total.reshape(1, width) * scale


def solution(mesh):
    in_specs = (
        P("section", "dp", None),
        P(None, "dp", None),
        P("section", None, "dp", None),
        P("section", "dp", None),
        P(None, "dp", None),
        P("section", None),
        P("section", None),
        P("section", None, "dp"),
        P("section", "dp", None),
        P("section", None, None, "dp"),
    )
    out_specs = (P("section", None, "dp", None), P("section", None, "dp", None), P("section", None))
    return jax.shard_map(
        per_device, mesh=mesh, in_specs=in_specs, out_specs=out_specs, check_vma=False
    )
```

```python
import functools

import jax
import jax.numpy as jnp
from jax import lax
from jax.experimental import pallas as pl
from jax.experimental.pallas import tpu as pltpu
from jax.sharding import PartitionSpec as P

EPS = 1e-05
CORES = 2
CHUNK = 256
WEIGHTS_LIMIT = 26
BF16 = jnp.bfloat16
F32 = jnp.float32
NN = (((1,), (0,)), ((), ()))
NT = (((1,), (1,)), ((), ()))
VMEM = pl.BlockSpec(memory_space=pltpu.VMEM)
SMEM = pl.BlockSpec(memory_space=pltpu.SMEM)


def shift_section(block, step):
    count = lax.axis_size("section")
    route = [(i - step, i) for i in range(count) if 0 <= i - step < count]
    return lax.ppermute(block, "section", route)


def swap_core(block):
    count = lax.axis_size("dp")
    return lax.ppermute(block, "dp", [(i, i ^ 1) for i in range(count)])


def shift_chip(block, step):
    count = lax.axis_size("dp")
    return lax.ppermute(block, "dp", [(i, (i + CORES * step) % count) for i in range(count)])


def swap_chips(blocks):
    count = lax.axis_size("dp")
    groups = [[c + CORES * j for j in range(count // CORES)] for c in range(CORES)]
    return lax.all_to_all(blocks, "dp", 0, 0, axis_index_groups=groups)


def gather_rows(copies):
    own = swap_chips(copies)
    return [own, swap_core(own)]


def dot(a, b, dims=NN):
    return lax.dot_general(a, b, dims, preferred_element_type=F32)


def halves(column):
    rows = column.shape[0]
    wide = jnp.broadcast_to(column, (rows, 128))
    return (wide + pltpu.roll(wide, rows // 2, 0))[:, :1]


def top_rows(rows, period):
    return lax.rem(lax.broadcasted_iota(jnp.int32, (rows, 1), 0), period) < period // 2


def pick(activity, route_column):
    rows, half = route_column.shape[0], activity.shape[1] // 2
    tokens = activity.shape[0]
    hit = route_column == lax.broadcasted_iota(jnp.int32, (rows, tokens), 1)
    top = top_rows(rows, rows)
    left = jnp.where(hit & top, 1.0, 0.0).astype(BF16)
    right = jnp.where(hit & jnp.logical_not(top), 1.0, 0.0).astype(BF16)
    return dot(left, activity[:, :half]) + dot(right, activity[:, half:])


def put(activity, rows, route_row):
    tokens, half = activity.shape[0], activity.shape[1] // 2
    count = route_row.shape[1]
    hit = route_row == lax.broadcasted_iota(jnp.int32, (tokens, count), 0)
    first = lax.broadcasted_iota(jnp.int32, (tokens, count), 1) < count // 2
    left = jnp.where(hit & first, 1.0, 0.0)
    right = jnp.where(hit & jnp.logical_not(first), 1.0, 0.0)
    taken = jnp.sum(left, axis=1, keepdims=True) > 0.5
    new_left = jnp.where(taken, dot(left.astype(BF16), rows), activity[:, :half].astype(F32))
    new_right = jnp.where(taken, dot(right.astype(BF16), rows), activity[:, half:].astype(F32))
    return new_left.astype(BF16), new_right.astype(BF16)


def by_half(vector, rows):
    half = vector.shape[1] // 2
    return jnp.where(top_rows(rows, rows), vector[:, :half], vector[:, half:])


def inverse_rms(rows):
    width = 2 * rows.shape[1]
    mean = halves(jnp.sum(rows * rows, axis=1, keepdims=True)) / width
    return lax.rsqrt(mean + EPS)


def normalize(rows, gain, router):
    normed = (rows * inverse_rms(rows) * by_half(gain, rows.shape[0])).astype(BF16)
    logit = jnp.sum(normed.astype(F32) * by_half(router, rows.shape[0]), axis=1, keepdims=True)
    return normed, jax.nn.sigmoid(halves(logit))


def stack_blocks(refs, place, out):
    blocks = [ref[(j, *place)].astype(F32) for ref in refs for j in range(ref.shape[0])]
    out[...] = jnp.concatenate(blocks, axis=0).astype(BF16)


def copies_of(out, rows, place=()):
    for j in range(out.shape[0]):
        out[(j, *place)] = rows


def join_halves(left, right, period):
    rows = left.shape[0]
    top = top_rows(rows, period)
    return jnp.where(
        top,
        left + pltpu.roll(right, rows - period // 2, 0),
        right + pltpu.roll(left, period // 2, 0),
    )


def first_forward_kernel(act, column, gain, router, rows_out, normed_out, gate_out):
    rows = pick(act[...], column[...])
    normed, gate = normalize(rows, gain[...], router[...])
    rows_out[...] = rows.astype(BF16)
    copies_of(normed_out, normed)
    gate_out[...] = jnp.broadcast_to(gate, gate_out.shape)


def first_backward_kernel(ticks, act, stash, columns, gain, rows_out, saved_out, copies_out):
    upstream = pick(act[...], columns[0]).astype(BF16)
    rows_out[...] = upstream
    copies_of(copies_out, upstream, (ticks,))
    for k in range(ticks):
        rows = pick(stash[k], columns[k])
        saved_out[k] = rows.astype(BF16)
        count = rows.shape[0]
        normed = (rows * inverse_rms(rows) * by_half(gain[...], count)).astype(BF16)
        copies_of(copies_out, normed, (k,))


def source_kernel(flag, moved, fresh, column, source_out, rows_out):
    source = jnp.where(flag[0] == 1, fresh[...], moved[...])
    source_out[...] = source
    rows_out[...] = pick(source, column[...]).astype(BF16)


def select(base, moved, column, behind_row):
    rows = column.shape[0]
    hit = column == behind_row
    same = top_rows(rows, rows) == (lax.broadcasted_iota(jnp.int32, (rows, rows), 1) < rows // 2)
    match = jnp.where(hit & same, 1.0, 0.0)
    found = jnp.max(match, axis=1, keepdims=True) > 0.5
    return jnp.where(found, dot(match.astype(BF16), moved), base.astype(F32))


def next_forward_kernel(
    base, moved, column, behind_row, gain, router, rows_out, normed_out, gate_out
):
    rows = select(base[...], moved[...], column[...], behind_row[...])
    normed, gate = normalize(rows, gain[...], router[...])
    rows_out[...] = rows.astype(BF16)
    copies_of(normed_out, normed)
    gate_out[...] = jnp.broadcast_to(gate, gate_out.shape)


def next_backward_kernel(base, moved, column, ahead_row, rows_out, copies_out):
    rows = select(base[...], moved[...], column[...], ahead_row[...]).astype(BF16)
    rows_out[...] = rows
    copies_of(copies_out, rows)


def land_kernel(source, moved, row, out):
    half = source.shape[1] // 2
    left, right = put(source[...], moved[...], row[...])
    out[:, :half] = left
    out[:, half:] = right


def output_kernel(act, rows, row, *outs):
    out = outs[-1]
    half = act.shape[1] // 2
    left, right = put(act[...], rows[...], row[...])
    out[0, 0, :, :half] = left
    out[0, 0, :, half:] = right


def forward_kernel(near, far, up, down, own_out, cross_out, rows, total):
    period, half = near.shape[1:]
    hidden_count = up.shape[1]
    chunk = min(CHUNK, hidden_count)
    stack_blocks([near, far], (), rows)
    x = rows[...]
    top = top_rows(x.shape[0], period)
    for low in range(0, hidden_count, chunk):
        n = slice(low, low + chunk)
        u = join_halves(dot(x, up[:half, n]), dot(x, up[half:, n]), period)
        hidden = u * jax.nn.sigmoid(u)
        left = jnp.where(top, hidden, 0.0).astype(BF16)
        right = jnp.where(top, 0.0, hidden).astype(BF16)
        part = dot(left, down[n, :half]) + dot(right, down[n, half:])
        total[...] = part if low == 0 else total[...] + part
    write_blocks(total, own_out, cross_out)


def write_blocks(total, own_out, cross_out):
    chips, period, _ = own_out.shape
    for j in range(chips):
        own_out[j] = total[j * period : (j + 1) * period, :]
        low = (chips + j) * period
        cross_out[j] = total[low : low + period, :].astype(BF16)


def backward_kernel(
    normed_place,
    grad_place,
    near_n,
    far_n,
    near_g,
    far_g,
    up,
    down,
    router,
    term_in,
    own_out,
    cross_out,
    term_out,
    x_n,
    x_g,
    total,
):
    period, half = own_out.shape[1:]
    all_rows = x_n.shape[0]
    hidden_count = up.shape[1]
    chunk = min(CHUNK, hidden_count)
    top = top_rows(all_rows, period)
    stack_blocks([near_n, far_n], normed_place, x_n)
    stack_blocks([near_g, far_g], grad_place, x_g)
    x = x_n[...]
    g = x_g[...]
    vector = jnp.where(top, router[:, :half], router[:, half:])
    logit = jnp.sum(x.astype(F32) * vector, axis=1, keepdims=True)
    wide = jnp.broadcast_to(logit, (all_rows, 128))
    gate = jax.nn.sigmoid(join_halves(wide, wide, period))
    inner = jnp.zeros((all_rows, 1), F32)
    for low in range(0, hidden_count, chunk):
        n = slice(low, low + chunk)
        u = join_halves(dot(x, up[:half, n]), dot(x, up[half:, n]), period)
        grad_hidden = join_halves(
            dot(g, down[n, :half], NT), dot(g, down[n, half:], NT), period
        )
        grad_hidden = grad_hidden * gate[:, :1]
        sig = jax.nn.sigmoid(u)
        hidden = (u * sig).astype(BF16).astype(F32)
        inner = inner + jnp.sum(grad_hidden * hidden, axis=1, keepdims=True)
        grad_up = grad_hidden * sig * (1.0 + u * (1.0 - sig))
        left = jnp.where(top, grad_up, 0.0).astype(BF16)
        right = jnp.where(top, 0.0, grad_up).astype(BF16)
        part = dot(left, up[:half, n], NT) + dot(right, up[half:, n], NT)
        total[...] = part if low == 0 else total[...] + part

    logit = inner * (1.0 - gate)
    total[...] += logit[:, :1] * vector
    write_blocks(total, own_out, cross_out)
    rest = logit.T[:1]
    first = lax.rem(lax.broadcasted_iota(jnp.int32, (1, all_rows), 1), period) < period // 2
    pieces = []
    for _ in range(3):
        piece = rest.astype(BF16).astype(F32)
        pieces.append(piece)
        rest = rest - piece
    sums = []
    for side in (first, jnp.logical_not(first)):
        stacked = jnp.concatenate(
            [jnp.where(side, p, 0.0) for p in pieces] + [jnp.zeros((5, all_rows), F32)], axis=0
        )
        sums.append(jnp.sum(dot(stacked.astype(BF16), x), axis=0, keepdims=True))
    term_out[...] = term_in[...] + jnp.concatenate(sums, axis=0)


def pair_kernel(own, crossed, out):
    out[...] = (own[...] + crossed[...].astype(F32)).astype(BF16)


def forward_end_kernel(rows, gate, terms, out):
    block = jnp.sum(terms[...].astype(F32), axis=0)
    out[...] = (rows[...].astype(F32) + gate[:, :1] * block).astype(BF16)


def backward_end_kernel(tick, upstream, saved, gain, terms, out):
    grad_normed = jnp.sum(terms[...].astype(F32), axis=0)
    picked = saved[tick].astype(F32)
    inv_rms = inverse_rms(picked)
    scaled_grad = grad_normed * by_half(gain[...], picked.shape[0])
    unit = picked * inv_rms
    mean = halves(jnp.sum(scaled_grad * unit, axis=1, keepdims=True)) / (2 * picked.shape[1])
    grad_rows = inv_rms * (scaled_grad - unit * mean)
    out[...] = (upstream[...].astype(F32) + grad_rows).astype(BF16)


def call(kernel, outs, *operands, smem=0, limit=8, scratch=(), cost=None):
    return pl.pallas_call(
        kernel,
        out_shape=outs,
        in_specs=[SMEM] * smem + [VMEM] * (len(operands) - smem),
        out_specs=jax.tree.map(lambda _: VMEM, outs),
        scratch_shapes=scratch,
        compiler_params=pltpu.CompilerParams(vmem_limit_bytes=limit * 2**20),
        cost_estimate=cost,
    )(*operands)


def shaped(shape, dtype=BF16):
    return jax.ShapeDtypeStruct(tuple(shape), dtype)


def whole(shape):
    return pl.BlockSpec(tuple(shape), lambda i: (0,) * len(shape))


def cost_of(matmuls, rows, weight):
    size = weight.shape[0] * weight.shape[1]
    return pl.CostEstimate(
        flops=4 * matmuls * rows * size,
        bytes_accessed=4 * size,
        transcendentals=rows * weight.shape[1],
    )


def scatter_sum(own, cross):
    return swap_chips(call(pair_kernel, shaped(own.shape), own, swap_core(cross)))


def per_device(
    arrive, entering, stash, back_arrive, head_grad, norm_gain, router, w_up, w_down, routes
):
    section = lax.axis_index("section")
    last = lax.axis_size("section") - 1
    dp_count = lax.axis_size("dp")
    chips = dp_count // CORES
    up, down = w_up[0], w_down[0]
    slots = routes.shape[3]
    tokens, width = arrive.shape[1:]
    half = width // 2
    ticks = stash.shape[1]
    period = 2 * slots

    route = routes[0]
    twice = jnp.concatenate([route, route], axis=-1)
    columns = twice[..., None]
    columns_f = [columns[k, 0] for k in range(ticks)]
    columns_b = columns[:, 1]
    rows_of = twice[:, :, None, :]
    behind = jnp.where(section == 0, -2, shift_section(twice[:, 0], 1))
    ahead = jnp.where(section == last, -2, shift_section(twice[:, 1], -1))
    behind = jnp.where(behind < 0, -2, behind)[:, None, :]
    ahead = jnp.where(ahead < 0, -2, ahead)[:, None, :]
    at_first = (section == 0).astype(jnp.int32).reshape(1)
    at_last = (section == last).astype(jnp.int32).reshape(1)

    packed = shaped((period, half))
    gate_shape = shaped((period, 128), F32)
    copies = shaped((chips, period, half))
    part_outs = [shaped((chips, period, half), F32), shaped((chips, period, half))]
    all_rows = dp_count * period
    scratch_rows = pltpu.VMEM((all_rows, half), BF16)
    scratch_total = pltpu.VMEM((all_rows, half), F32)

    forward_in, backward_in = arrive[0], back_arrive[0]
    forward_rows, forward_normed, gate = call(
        first_forward_kernel,
        [packed, copies, gate_shape],
        forward_in,
        columns_f[0],
        norm_gain,
        router,
    )
    backward_rows, saved, saved_copies = call(
        functools.partial(first_backward_kernel, ticks),
        [packed, shaped((ticks, period, half)), shaped((chips, ticks + 1, period, half))],
        backward_in,
        stash[0],
        columns_b,
        norm_gain,
        limit=16,
    )
    term = jnp.zeros((2, half), F32)
    forward_out = backward_out = None
    out_shape = shaped((1, ticks, tokens, width))

    def write_out(result, k, act, rows, row):
        before = [] if result is None else [result]
        return pl.pallas_call(
            output_kernel,
            grid=(1,),
            out_shape=out_shape,
            in_specs=[whole(act.shape), whole(rows.shape), whole(row.shape)]
            + [pl.BlockSpec(memory_space=pl.ANY)] * len(before),
            out_specs=pl.BlockSpec((1, 1, tokens, width), lambda i: (0, k, 0, 0)),
            input_output_aliases={3: 0} if before else {},
            compiler_params=pltpu.CompilerParams(vmem_limit_bytes=8 * 2**20),
        )(act, rows, row, *before)

    for k in range(ticks):
        if k + 1 < ticks:
            forward_base = shift_section(forward_in, 1)
            backward_base = shift_section(backward_in, -1)

        own, cross = call(
            forward_kernel,
            part_outs,
            *gather_rows(forward_normed),
            up,
            down,
            limit=WEIGHTS_LIMIT,
            scratch=[scratch_rows, scratch_total],
            cost=cost_of(2, all_rows, up),
        )
        terms = scatter_sum(own, cross)
        forward_new = call(forward_end_kernel, packed, forward_rows, gate, terms)

        if k == 0:
            saved_all = gather_rows(saved_copies)
            grads, place = saved_all, (ticks,)
        else:
            grads, place = gather_rows(backward_copies), ()
        own, cross, term = call(
            functools.partial(backward_kernel, (k,), place),
            part_outs + [shaped((2, half), F32)],
            *saved_all,
            *grads,
            up,
            down,
            router,
            term,
            limit=WEIGHTS_LIMIT,
            scratch=[scratch_rows, scratch_rows, scratch_total],
            cost=cost_of(3, all_rows, up),
        )
        terms = scatter_sum(own, cross)
        backward_new = call(
            functools.partial(backward_end_kernel, k),
            packed,
            backward_rows,
            saved,
            norm_gain,
            terms,
        )

        forward_out = write_out(forward_out, k, forward_in, forward_new, rows_of[k, 0])
        backward_out = write_out(backward_out, k, backward_in, backward_new, rows_of[k, 1])

        if k + 1 < ticks:
            full = shaped((tokens, width))
            source, base = call(
                source_kernel,
                [full, packed],
                at_first,
                forward_base,
                entering[k],
                columns_f[k + 1],
                smem=1,
            )
            moved = shift_section(forward_new, 1)
            forward_rows, forward_normed, gate = call(
                next_forward_kernel,
                [packed, copies, gate_shape],
                base,
                moved,
                columns_f[k + 1],
                behind[k],
                norm_gain,
                router,
            )
            forward_in = call(land_kernel, full, source, moved, behind[k])

            source, base = call(
                source_kernel,
                [full, packed],
                at_last,
                backward_base,
                head_grad[k],
                columns_b[k + 1],
                smem=1,
            )
            moved = shift_section(backward_new, -1)
            backward_rows, backward_copies = call(
                next_backward_kernel,
                [packed, copies],
                base,
                moved,
                columns_b[k + 1],
                ahead[k],
            )
            backward_in = call(land_kernel, full, source, moved, ahead[k])

    pair = term + swap_core(term)
    by_distance = jnp.stack([pair] + [shift_chip(pair, j) for j in range(1, chips)], axis=0)
    chip = lax.axis_index("dp") // CORES
    total = jnp.zeros_like(pair)
    for j in range(chips):
        total = total + lax.dynamic_index_in_dim(by_distance, (chip - j) % chips, 0, False)
    scale = 1.0 / float(ticks * slots * dp_count)
    return forward_out, backward_out, total.reshape(1, width) * scale


def solution(mesh):
    in_specs = (
        P("section", "dp", None),
        P(None, "dp", None),
        P("section", None, "dp", None),
        P("section", "dp", None),
        P(None, "dp", None),
        P("section", None),
        P("section", None),
        P("section", None, "dp"),
        P("section", "dp", None),
        P("section", None, None, "dp"),
    )
    out_specs = (P("section", None, "dp", None), P("section", None, "dp", None), P("section", None))
    return jax.shard_map(
        per_device, mesh=mesh, in_specs=in_specs, out_specs=out_specs, check_vma=False
    )
```

```python
import functools

import jax
import jax.numpy as jnp
from jax import lax
from jax.experimental import pallas as pl
from jax.experimental.pallas import tpu as pltpu
from jax.sharding import PartitionSpec as P

EPS = 1e-05
CORES = 2
CHUNK = 256
LANES = 128
WEIGHTS_LIMIT = 26
BF16 = jnp.bfloat16
F32 = jnp.float32
NN = (((1,), (0,)), ((), ()))
NT = (((1,), (1,)), ((), ()))
VMEM = pl.BlockSpec(memory_space=pltpu.VMEM)
SMEM = pl.BlockSpec(memory_space=pltpu.SMEM)
ANY = pl.BlockSpec(memory_space=pl.ANY)


def shift_section(block, step):
    count = lax.axis_size("section")
    route = [(i - step, i) for i in range(count) if 0 <= i - step < count]
    return lax.ppermute(block, "section", route)


def swap_core(block):
    count = lax.axis_size("dp")
    return lax.ppermute(block, "dp", [(i, i ^ 1) for i in range(count)])


def shift_chip(block, step):
    count = lax.axis_size("dp")
    return lax.ppermute(block, "dp", [(i, (i + CORES * step) % count) for i in range(count)])


def spread(block):
    return [block] + [shift_chip(block, j) for j in range(1, lax.axis_size("dp") // CORES)]


def collect(blocks):
    return [blocks[0]] + [shift_chip(b, -j) for j, b in enumerate(blocks) if j > 0]


def dot(a, b, dims=NN):
    return lax.dot_general(a, b, dims, preferred_element_type=F32)


def halves(column):
    rows = column.shape[0]
    wide = jnp.broadcast_to(column, (rows, 128))
    return (wide + pltpu.roll(wide, rows // 2, 0))[:, :1]


def column_of(route):
    slots = route.shape[1]
    row = lax.rem(lax.broadcasted_iota(jnp.int32, (2 * slots, slots), 0), slots)
    same = row == lax.broadcasted_iota(jnp.int32, (2 * slots, slots), 1)
    return jnp.sum(jnp.where(same, route, 0), axis=1, keepdims=True)


def row_of(column):
    count = column.shape[0]
    shape = (count, count)
    same = lax.broadcasted_iota(jnp.int32, shape, 0) == lax.broadcasted_iota(jnp.int32, shape, 1)
    return jnp.sum(jnp.where(same, column, 0), axis=0, keepdims=True)


def arrived(moved):
    half = moved.shape[1] - LANES
    place = row_of(moved[:, half : half + 1].astype(F32).astype(jnp.int32)) - 1
    return moved[:, :half], jnp.where(place < 0, -2, place)


def send_off(out, rows, route):
    half = rows.shape[1]
    out[:, :half] = rows
    place = (column_of(route) + 1).astype(F32).astype(BF16)
    out[:, half:] = jnp.broadcast_to(place, (rows.shape[0], LANES))


def top_rows(rows, period):
    return lax.rem(lax.broadcasted_iota(jnp.int32, (rows, 1), 0), period) < period // 2


def pick(activity, route_column):
    rows, half = route_column.shape[0], activity.shape[1] // 2
    tokens = activity.shape[0]
    hit = route_column == lax.broadcasted_iota(jnp.int32, (rows, tokens), 1)
    top = top_rows(rows, rows)
    left = jnp.where(hit & top, 1.0, 0.0).astype(BF16)
    right = jnp.where(hit & jnp.logical_not(top), 1.0, 0.0).astype(BF16)
    return dot(left, activity[:, :half]) + dot(right, activity[:, half:])


def put(activity, rows, route_row):
    tokens, half = activity.shape[0], activity.shape[1] // 2
    count = route_row.shape[1]
    hit = route_row == lax.broadcasted_iota(jnp.int32, (tokens, count), 0)
    first = lax.broadcasted_iota(jnp.int32, (tokens, count), 1) < count // 2
    left = jnp.where(hit & first, 1.0, 0.0)
    right = jnp.where(hit & jnp.logical_not(first), 1.0, 0.0)
    taken = jnp.sum(left, axis=1, keepdims=True) > 0.5
    new_left = jnp.where(taken, dot(left.astype(BF16), rows), activity[:, :half].astype(F32))
    new_right = jnp.where(taken, dot(right.astype(BF16), rows), activity[:, half:].astype(F32))
    return new_left.astype(BF16), new_right.astype(BF16)


def by_half(vector, rows):
    half = vector.shape[1] // 2
    return jnp.where(top_rows(rows, rows), vector[:, :half], vector[:, half:])


def inverse_rms(rows):
    width = 2 * rows.shape[1]
    mean = halves(jnp.sum(rows * rows, axis=1, keepdims=True)) / width
    return lax.rsqrt(mean + EPS)


def normalize(rows, gain, router):
    normed = (rows * inverse_rms(rows) * by_half(gain, rows.shape[0])).astype(BF16)
    logit = jnp.sum(normed.astype(F32) * by_half(router, rows.shape[0]), axis=1, keepdims=True)
    return normed, jax.nn.sigmoid(halves(logit))


def stack_blocks(refs, place, out):
    blocks = [ref[(j, *place)].astype(F32) for ref in refs for j in range(ref.shape[0])]
    out[...] = jnp.concatenate(blocks, axis=0).astype(BF16)


def join_halves(left, right, period):
    rows = left.shape[0]
    top = top_rows(rows, period)
    return jnp.where(
        top,
        left + pltpu.roll(right, rows - period // 2, 0),
        right + pltpu.roll(left, period // 2, 0),
    )


def first_forward_kernel(flags, act, routes, gain, router, normed_out, rows_out, gate_out, where_out):
    rows = pick(act[...], column_of(routes[0, 0, 0:1]))
    normed, gate = normalize(rows, gain[...], router[...])
    rows_out[...] = rows.astype(BF16)
    normed_out[...] = normed
    gate_out[...] = jnp.broadcast_to(gate, gate_out.shape)
    line = lax.broadcasted_iota(jnp.int32, where_out.shape, 0)
    where_out[...] = jnp.where(line == 0, flags[0], jnp.where(line == 1, flags[1], flags[2]))


def first_backward_kernel(act, stash, routes, gain, first_out, later_out, rows_out, saved_out):
    ticks = stash.shape[0]
    upstream = pick(act[...], column_of(routes[0, 0, 1:2])).astype(BF16)
    rows_out[...] = upstream
    first_out[1] = upstream
    for k in range(ticks):
        rows = pick(stash[k], column_of(routes[0, k, 1:2]))
        saved_out[k] = rows.astype(BF16)
        count = rows.shape[0]
        normed = (rows * inverse_rms(rows) * by_half(gain[...], count)).astype(BF16)
        if k == 0:
            first_out[0] = normed
        else:
            later_out[k - 1] = normed


def source_kernel(tick, way, place, moved, fresh, routes, source_out, rows_out):
    source = jnp.where(place[way : way + 1, :1] == 1, fresh[tick - 1], moved[...])
    source_out[...] = source
    rows_out[...] = pick(source, column_of(routes[0, tick, way : way + 1])).astype(BF16)


def select(base, packet, route):
    moved, behind_row = arrived(packet)
    column = column_of(route)
    rows = column.shape[0]
    hit = column == behind_row
    same = top_rows(rows, rows) == (lax.broadcasted_iota(jnp.int32, (rows, rows), 1) < rows // 2)
    match = jnp.where(hit & same, 1.0, 0.0)
    found = jnp.max(match, axis=1, keepdims=True) > 0.5
    return jnp.where(found, dot(match.astype(BF16), moved), base.astype(F32))


def next_forward_kernel(tick, base, moved, routes, gain, router, normed_out, rows_out, gate_out):
    rows = select(base[...], moved[...], routes[0, tick, 0:1])
    normed, gate = normalize(rows, gain[...], router[...])
    rows_out[...] = rows.astype(BF16)
    normed_out[...] = normed
    gate_out[...] = jnp.broadcast_to(gate, gate_out.shape)


def next_backward_kernel(tick, base, moved, routes, rows_out):
    rows_out[...] = select(base[...], moved[...], routes[0, tick, 1:2]).astype(BF16)


def land_kernel(source, moved, out):
    half = source.shape[1] // 2
    rows, places = arrived(moved[...])
    left, right = put(source[...], rows, places)
    out[:, :half] = left
    out[:, half:] = right


def output_kernel(act, moved, *outs):
    out = outs[-1]
    half = act.shape[1] // 2
    rows, places = arrived(moved[...])
    left, right = put(act[...], rows, places)
    out[0, 0, :, :half] = left
    out[0, 0, :, half:] = right


def stack_kernel(*refs):
    for j, ref in enumerate(refs[:-1]):
        refs[-1][j] = ref[...]


def forward_kernel(near, far, up, down, cross_out, own_out, rows, total):
    period, half = near.shape[1:]
    hidden_count = up.shape[1]
    chunk = min(CHUNK, hidden_count)
    stack_blocks([near, far], (), rows)
    x = rows[...]
    top = top_rows(x.shape[0], period)
    for low in range(0, hidden_count, chunk):
        n = slice(low, low + chunk)
        u = join_halves(dot(x, up[:half, n]), dot(x, up[half:, n]), period)
        hidden = u * jax.nn.sigmoid(u)
        left = jnp.where(top, hidden, 0.0).astype(BF16)
        right = jnp.where(top, 0.0, hidden).astype(BF16)
        part = dot(left, down[n, :half]) + dot(right, down[n, half:])
        total[...] = part if low == 0 else total[...] + part
    write_blocks(total, own_out, cross_out)


def write_blocks(total, own_out, cross_out):
    chips, period, _ = own_out.shape
    for j in range(chips):
        own_out[j] = total[j * period : (j + 1) * period, :]
        low = (chips + j) * period
        cross_out[j] = total[low : low + period, :].astype(BF16)


def backward_kernel(
    normed_place,
    grad_place,
    near_n,
    far_n,
    near_g,
    far_g,
    up,
    down,
    router,
    *refs,
):
    term_in = refs[:-6]
    cross_out, own_out, term_out, x_n, x_g, total = refs[-6:]
    period, half = own_out.shape[1:]
    all_rows = x_n.shape[0]
    hidden_count = up.shape[1]
    chunk = min(CHUNK, hidden_count)
    top = top_rows(all_rows, period)
    stack_blocks([near_n, far_n], normed_place, x_n)
    stack_blocks([near_g, far_g], grad_place, x_g)
    x = x_n[...]
    g = x_g[...]
    vector = jnp.where(top, router[:, :half], router[:, half:])
    logit = jnp.sum(x.astype(F32) * vector, axis=1, keepdims=True)
    wide = jnp.broadcast_to(logit, (all_rows, 128))
    gate = jax.nn.sigmoid(join_halves(wide, wide, period))
    inner = jnp.zeros((all_rows, 1), F32)
    for low in range(0, hidden_count, chunk):
        n = slice(low, low + chunk)
        u = join_halves(dot(x, up[:half, n]), dot(x, up[half:, n]), period)
        grad_hidden = join_halves(
            dot(g, down[n, :half], NT), dot(g, down[n, half:], NT), period
        )
        grad_hidden = grad_hidden * gate[:, :1]
        sig = jax.nn.sigmoid(u)
        hidden = (u * sig).astype(BF16).astype(F32)
        inner = inner + jnp.sum(grad_hidden * hidden, axis=1, keepdims=True)
        grad_up = grad_hidden * sig * (1.0 + u * (1.0 - sig))
        left = jnp.where(top, grad_up, 0.0).astype(BF16)
        right = jnp.where(top, 0.0, grad_up).astype(BF16)
        part = dot(left, up[:half, n], NT) + dot(right, up[half:, n], NT)
        total[...] = part if low == 0 else total[...] + part

    logit = inner * (1.0 - gate)
    total[...] += logit[:, :1] * vector
    write_blocks(total, own_out, cross_out)
    rest = logit.T[:1]
    first = lax.rem(lax.broadcasted_iota(jnp.int32, (1, all_rows), 1), period) < period // 2
    pieces = []
    for _ in range(3):
        piece = rest.astype(BF16).astype(F32)
        pieces.append(piece)
        rest = rest - piece
    sums = []
    for side in (first, jnp.logical_not(first)):
        stacked = jnp.concatenate(
            [jnp.where(side, p, 0.0) for p in pieces] + [jnp.zeros((5, all_rows), F32)], axis=0
        )
        sums.append(jnp.sum(dot(stacked.astype(BF16), x), axis=0, keepdims=True))
    term = jnp.concatenate(sums, axis=0)
    for before in term_in:
        term = term + before[...]
    term_out[...] = term


def pair_kernel(own, crossed, *outs):
    for j, out in enumerate(outs):
        out[...] = (own[j] + crossed[j].astype(F32)).astype(out.dtype)


def added(terms):
    total = terms[0][...]
    for term in terms[1:]:
        total = total + term[...].astype(F32)
    return total


def forward_end_kernel(tick, rows, gate, routes, *refs):
    block = added(refs[:-1])
    renewed = (rows[...].astype(F32) + gate[:, :1] * block).astype(BF16)
    send_off(refs[-1], renewed, routes[0, tick, 0:1])


def backward_end_kernel(tick, upstream, saved, gain, routes, *refs):
    grad_normed = added(refs[:-1])
    picked = saved[tick].astype(F32)
    inv_rms = inverse_rms(picked)
    scaled_grad = grad_normed * by_half(gain[...], picked.shape[0])
    unit = picked * inv_rms
    mean = halves(jnp.sum(scaled_grad * unit, axis=1, keepdims=True)) / (2 * picked.shape[1])
    grad_rows = inv_rms * (scaled_grad - unit * mean)
    renewed = (upstream[...].astype(F32) + grad_rows).astype(BF16)
    send_off(refs[-1], renewed, routes[0, tick, 1:2])


def term_pair_kernel(near, far, out):
    out[...] = near[...] + far[...]


def term_end_kernel(scale, place, *refs):
    out = refs[-1]
    chips = len(refs) - 1
    chip = place[2:3, :1]
    total = jnp.zeros(refs[0].shape, F32)
    for low in range(chips):
        for j in range(chips):
            total = total + jnp.where(lax.rem(chip - j + chips, chips) == low, refs[j][...], 0.0)
    half = refs[0].shape[1]
    out[:, :half] = total[0:1] * scale
    out[:, half:] = total[1:2] * scale


class Order:
    def __init__(self):
        self.token = []

    def __call__(self, kernel, outs, *operands, smem=0, limit=8, scratch=(), cost=None, **more):
        count = len(self.token)

        def body(*refs):
            kernel(*refs[count:])

        result = pl.pallas_call(
            body,
            out_shape=outs,
            in_specs=[ANY] * count + [SMEM] * smem + [VMEM] * (len(operands) - smem),
            out_specs=jax.tree.map(lambda _: VMEM, outs),
            scratch_shapes=scratch,
            compiler_params=pltpu.CompilerParams(vmem_limit_bytes=limit * 2**20),
            cost_estimate=cost,
            **more,
        )(*self.token, *operands)
        self.token = [result[0] if isinstance(result, (list, tuple)) else result]
        return result


def shaped(shape, dtype=BF16):
    return jax.ShapeDtypeStruct(tuple(shape), dtype)


def whole(shape):
    return pl.BlockSpec(tuple(shape), lambda i: (0,) * len(shape))


def cost_of(matmuls, rows, weight):
    size = weight.shape[0] * weight.shape[1]
    return pl.CostEstimate(
        flops=4 * matmuls * rows * size,
        bytes_accessed=4 * size,
        transcendentals=rows * weight.shape[1],
    )


def write_out(result, tick, ticks, act, moved):
    before = [] if result is None else [result]
    tokens, width = act.shape
    return pl.pallas_call(
        output_kernel,
        grid=(1,),
        out_shape=shaped((1, ticks, tokens, width)),
        in_specs=[whole(act.shape), whole(moved.shape)] + [ANY] * len(before),
        out_specs=pl.BlockSpec((1, 1, tokens, width), lambda i: (0, tick, 0, 0)),
        input_output_aliases={2: 0} if before else {},
        compiler_params=pltpu.CompilerParams(vmem_limit_bytes=8 * 2**20),
    )(act, moved, *before)


def per_device(
    arrive, entering, stash, back_arrive, head_grad, norm_gain, router, w_up, w_down, routes
):
    section = lax.axis_index("section")
    last = lax.axis_size("section") - 1
    dp_count = lax.axis_size("dp")
    chips = dp_count // CORES
    up, down = w_up[0], w_down[0]
    slots = routes.shape[3]
    tokens, width = arrive.shape[1:]
    half = width // 2
    ticks = stash.shape[1]
    period = 2 * slots
    flags = jnp.stack(
        [
            (section == 0).astype(jnp.int32),
            (section == last).astype(jnp.int32),
            lax.axis_index("dp") // CORES,
        ]
    )

    packed = shaped((period, half))
    packed_sum = shaped((period, half), F32)
    packet = shaped((period, half + LANES))
    full = shaped((tokens, width))
    gate_shape = shaped((period, LANES), F32)
    part_outs = [shaped((chips, period, half)), shaped((chips, period, half), F32)]
    all_rows = dp_count * period
    scratch_rows = pltpu.VMEM((all_rows, half), BF16)
    scratch_total = pltpu.VMEM((all_rows, half), F32)
    run = Order()

    def stacked(blocks):
        return run(stack_kernel, shaped((len(blocks), *blocks[0].shape)), *blocks)

    def pair(own, crossed):
        outs = [packed_sum] + [packed] * (chips - 1)
        return collect(run(pair_kernel, outs, own, crossed))

    forward_in, backward_in = arrive[0], back_arrive[0]
    forward_normed, forward_rows, gate, place = run(
        first_forward_kernel,
        [packed, packed, gate_shape, shaped((8, LANES), jnp.int32)],
        flags,
        forward_in,
        routes,
        norm_gain,
        router,
        smem=1,
    )
    forward_blocks = spread(forward_normed)
    saved_first, saved_later, backward_rows, saved = run(
        first_backward_kernel,
        [
            shaped((2, period, half)),
            shaped((ticks - 1, period, half)),
            packed,
            shaped((ticks, period, half)),
        ],
        backward_in,
        stash[0],
        routes,
        norm_gain,
        limit=16,
    )
    backward_blocks = spread(saved_first)
    term = []
    forward_out = backward_out = None
    forward_base = shift_section(forward_in, 1)
    backward_base = shift_section(backward_in, -1)

    for k in range(ticks):
        near = stacked(forward_blocks)
        far = swap_core(near)
        if k > 0:
            forward_source = forward_in
            forward_in = run(land_kernel, full, forward_source, forward_moved)
            backward_source = backward_in
            backward_in = run(land_kernel, full, backward_source, backward_moved)
            if k + 1 < ticks:
                forward_base = shift_section(forward_in, 1)
                backward_base = shift_section(backward_in, -1)
        cross, own = run(
            forward_kernel,
            part_outs,
            near,
            far,
            up,
            down,
            limit=WEIGHTS_LIMIT,
            scratch=[scratch_rows, scratch_total],
            cost=cost_of(2, all_rows, up),
        )
        crossed = swap_core(cross)

        near_g = stacked(backward_blocks)
        far_g = swap_core(near_g)
        if k == 0:
            near_n, far_n, normed_place, grad_place = near_g, far_g, (0,), (1,)
        else:
            if k == 1:
                near_n = stacked(later_blocks)
                far_n = swap_core(near_n)
            normed_place, grad_place = (k - 1,), ()
        terms = pair(own, crossed)

        cross, own, part = run(
            functools.partial(backward_kernel, normed_place, grad_place),
            part_outs + [shaped((2, half), F32)],
            near_n,
            far_n,
            near_g,
            far_g,
            up,
            down,
            router,
            *term,
            limit=WEIGHTS_LIMIT,
            scratch=[scratch_rows, scratch_rows, scratch_total],
            cost=cost_of(3, all_rows, up),
        )
        term = [part]
        crossed = swap_core(cross)
        forward_new = run(
            functools.partial(forward_end_kernel, k), packet, forward_rows, gate, routes, *terms
        )
        if k + 1 < ticks:
            forward_moved = shift_section(forward_new, 1)
        terms = pair(own, crossed)
        forward_out = write_out(forward_out, k, ticks, forward_in, forward_new)

        if k + 1 < ticks:
            forward_in, base = run(
                functools.partial(source_kernel, k + 1, 0),
                [full, packed],
                place,
                forward_base,
                entering,
                routes,
            )
            forward_normed, forward_rows, gate = run(
                functools.partial(next_forward_kernel, k + 1),
                [packed, packed, gate_shape],
                base,
                forward_moved,
                routes,
                norm_gain,
                router,
            )
            forward_blocks = spread(forward_normed)
        else:
            total = run(term_pair_kernel, shaped((2, half), F32), part, swap_core(part))
            total_blocks = spread(total)

        backward_new = run(
            functools.partial(backward_end_kernel, k),
            packet,
            backward_rows,
            saved,
            norm_gain,
            routes,
            *terms,
        )
        backward_out = write_out(backward_out, k, ticks, backward_in, backward_new)
        if k + 1 < ticks:
            backward_moved = shift_section(backward_new, -1)
            if k == 0:
                later_blocks = spread(saved_later)
            backward_in, base = run(
                functools.partial(source_kernel, k + 1, 1),
                [full, packed],
                place,
                backward_base,
                head_grad,
                routes,
            )
            backward_rows = run(
                functools.partial(next_backward_kernel, k + 1),
                packed,
                base,
                backward_moved,
                routes,
            )
            backward_blocks = spread(backward_rows)

    scale = 1.0 / float(ticks * slots * dp_count)
    router_grad = run(
        functools.partial(term_end_kernel, scale), shaped((1, width), F32), place, *total_blocks
    )
    return forward_out, backward_out, router_grad


def solution(mesh):
    in_specs = (
        P("section", "dp", None),
        P(None, "dp", None),
        P("section", None, "dp", None),
        P("section", "dp", None),
        P(None, "dp", None),
        P("section", None),
        P("section", None),
        P("section", None, "dp"),
        P("section", "dp", None),
        P("section", None, None, "dp"),
    )
    out_specs = (P("section", None, "dp", None), P("section", None, "dp", None), P("section", None))
    return jax.shard_map(
        per_device, mesh=mesh, in_specs=in_specs, out_specs=out_specs, check_vma=False
    )
```

```python
import functools

import jax
import jax.numpy as jnp
from jax import lax
from jax.experimental import pallas as pl
from jax.experimental.pallas import tpu as pltpu
from jax.sharding import PartitionSpec as P

EPS = 1e-05
CORES = 2
CHUNK = 256
LANES = 128
WEIGHTS_LIMIT = 26
BF16 = jnp.bfloat16
F32 = jnp.float32
NN = (((1,), (0,)), ((), ()))
NT = (((1,), (1,)), ((), ()))
VMEM = pl.BlockSpec(memory_space=pltpu.VMEM)
SMEM = pl.BlockSpec(memory_space=pltpu.SMEM)
ANY = pl.BlockSpec(memory_space=pl.ANY)
SMALL = pl.CostEstimate(flops=0, bytes_accessed=2 * 2**20, transcendentals=0)


def shift_section(block, step):
    count = lax.axis_size("section")
    route = [(i - step, i) for i in range(count) if 0 <= i - step < count]
    return lax.ppermute(block, "section", route)


def swap_core(block):
    count = lax.axis_size("dp")
    return lax.ppermute(block, "dp", [(i, i ^ 1) for i in range(count)])


def shift_chip(block, step):
    count = lax.axis_size("dp")
    return lax.ppermute(block, "dp", [(i, (i + CORES * step) % count) for i in range(count)])


def spread(block):
    return [block] + [shift_chip(block, j) for j in range(1, lax.axis_size("dp") // CORES)]


def collect(blocks):
    return [blocks[0]] + [shift_chip(b, -j) for j, b in enumerate(blocks) if j > 0]


def dot(a, b, dims=NN):
    return lax.dot_general(a, b, dims, preferred_element_type=F32)


def halves(column):
    rows = column.shape[0]
    wide = jnp.broadcast_to(column, (rows, 128))
    return (wide + pltpu.roll(wide, rows // 2, 0))[:, :1]


def column_of(route):
    slots = route.shape[1]
    row = lax.rem(lax.broadcasted_iota(jnp.int32, (2 * slots, slots), 0), slots)
    same = row == lax.broadcasted_iota(jnp.int32, (2 * slots, slots), 1)
    return jnp.sum(jnp.where(same, route, 0), axis=1, keepdims=True)


def row_of(column):
    count = column.shape[0]
    shape = (count, count)
    same = lax.broadcasted_iota(jnp.int32, shape, 0) == lax.broadcasted_iota(jnp.int32, shape, 1)
    return jnp.sum(jnp.where(same, column, 0), axis=0, keepdims=True)


def arrived(moved):
    half = moved.shape[1] - LANES
    place = row_of(moved[:, half : half + 1].astype(F32).astype(jnp.int32)) - 1
    return moved[:, :half], jnp.where(place < 0, -2, place)


def send_off(out, rows, route):
    half = rows.shape[1]
    out[:, :half] = rows
    place = (column_of(route) + 1).astype(F32).astype(BF16)
    out[:, half:] = jnp.broadcast_to(place, (rows.shape[0], LANES))


def top_rows(rows, period):
    return lax.rem(lax.broadcasted_iota(jnp.int32, (rows, 1), 0), period) < period // 2


def pick(activity, route_column):
    rows, half = route_column.shape[0], activity.shape[1] // 2
    tokens = activity.shape[0]
    hit = route_column == lax.broadcasted_iota(jnp.int32, (rows, tokens), 1)
    top = top_rows(rows, rows)
    left = jnp.where(hit & top, 1.0, 0.0).astype(BF16)
    right = jnp.where(hit & jnp.logical_not(top), 1.0, 0.0).astype(BF16)
    return dot(left, activity[:, :half]) + dot(right, activity[:, half:])


def put(activity, rows, route_row):
    tokens, half = activity.shape[0], activity.shape[1] // 2
    count = route_row.shape[1]
    hit = route_row == lax.broadcasted_iota(jnp.int32, (tokens, count), 0)
    first = lax.broadcasted_iota(jnp.int32, (tokens, count), 1) < count // 2
    left = jnp.where(hit & first, 1.0, 0.0)
    right = jnp.where(hit & jnp.logical_not(first), 1.0, 0.0)
    taken = jnp.sum(left, axis=1, keepdims=True) > 0.5
    new_left = jnp.where(taken, dot(left.astype(BF16), rows), activity[:, :half].astype(F32))
    new_right = jnp.where(taken, dot(right.astype(BF16), rows), activity[:, half:].astype(F32))
    return new_left.astype(BF16), new_right.astype(BF16)


def by_half(vector, rows):
    half = vector.shape[1] // 2
    return jnp.where(top_rows(rows, rows), vector[:, :half], vector[:, half:])


def inverse_rms(rows):
    width = 2 * rows.shape[1]
    mean = halves(jnp.sum(rows * rows, axis=1, keepdims=True)) / width
    return lax.rsqrt(mean + EPS)


def normalize(rows, gain, router):
    normed = (rows * inverse_rms(rows) * by_half(gain, rows.shape[0])).astype(BF16)
    logit = jnp.sum(normed.astype(F32) * by_half(router, rows.shape[0]), axis=1, keepdims=True)
    return normed, jax.nn.sigmoid(halves(logit))


def stack_blocks(refs, out):
    blocks = [ref[j].astype(F32) for ref in refs for j in range(ref.shape[0])]
    out[...] = jnp.concatenate(blocks, axis=0).astype(BF16)


def stack_gathered(flags, gathered, place, out):
    chips = gathered.shape[0] // CORES
    blocks = []
    for core in (flags[3], 1 - flags[3]):
        for j in range(chips):
            device = lax.rem(flags[2] + chips - j, chips) * CORES + core
            blocks.append(gathered[(device, *place)].astype(F32))
    out[...] = jnp.concatenate(blocks, axis=0).astype(BF16)


def join_halves(left, right, period):
    rows = left.shape[0]
    top = top_rows(rows, period)
    return jnp.where(
        top,
        left + pltpu.roll(right, rows - period // 2, 0),
        right + pltpu.roll(left, period // 2, 0),
    )


def first_forward_kernel(flags, act, routes, gain, router, normed_out, rows_out, gate_out, where_out):
    rows = pick(act[...], column_of(routes[0, 0, 0:1]))
    normed, gate = normalize(rows, gain[...], router[...])
    rows_out[...] = rows.astype(BF16)
    normed_out[...] = normed
    gate_out[...] = jnp.broadcast_to(gate, gate_out.shape)
    line = lax.broadcasted_iota(jnp.int32, where_out.shape, 0)
    where_out[...] = jnp.where(line == 0, flags[0], jnp.where(line == 1, flags[1], flags[2]))


def first_backward_kernel(act, stash, routes, gain, first_out, later_out, rows_out, saved_out):
    ticks = stash.shape[0]
    upstream = pick(act[...], column_of(routes[0, 0, 1:2])).astype(BF16)
    rows_out[...] = upstream
    for k in range(ticks):
        rows = pick(stash[k], column_of(routes[0, k, 1:2]))
        saved_out[k] = rows.astype(BF16)
        count = rows.shape[0]
        normed = (rows * inverse_rms(rows) * by_half(gain[...], count)).astype(BF16)
        if k == 0:
            first_out[...] = normed
        else:
            later_out[k - 1] = normed


def source_kernel(tick, way, place, moved, fresh, routes, source_out, rows_out):
    source = jnp.where(place[way : way + 1, :1] == 1, fresh[tick - 1], moved[...])
    source_out[...] = source
    rows_out[...] = pick(source, column_of(routes[0, tick, way : way + 1])).astype(BF16)


def select(base, packet, route):
    moved, behind_row = arrived(packet)
    column = column_of(route)
    rows = column.shape[0]
    hit = column == behind_row
    same = top_rows(rows, rows) == (lax.broadcasted_iota(jnp.int32, (rows, rows), 1) < rows // 2)
    match = jnp.where(hit & same, 1.0, 0.0)
    found = jnp.max(match, axis=1, keepdims=True) > 0.5
    return jnp.where(found, dot(match.astype(BF16), moved), base.astype(F32))


def next_forward_kernel(tick, base, moved, routes, gain, router, normed_out, rows_out, gate_out):
    rows = select(base[...], moved[...], routes[0, tick, 0:1])
    normed, gate = normalize(rows, gain[...], router[...])
    rows_out[...] = rows.astype(BF16)
    normed_out[...] = normed
    gate_out[...] = jnp.broadcast_to(gate, gate_out.shape)


def next_backward_kernel(tick, base, moved, routes, rows_out):
    rows_out[...] = select(base[...], moved[...], routes[0, tick, 1:2]).astype(BF16)


def land_kernel(source, moved, out):
    half = source.shape[1] // 2
    rows, places = arrived(moved[...])
    left, right = put(source[...], rows, places)
    out[:, :half] = left
    out[:, half:] = right


def output_kernel(token, act, moved, *outs):
    done, out = outs[-2:]
    done[...] = jnp.zeros_like(done)
    half = act.shape[1] // 2
    rows, places = arrived(moved[...])
    left, right = put(act[...], rows, places)
    out[0, 0, :, :half] = left
    out[0, 0, :, half:] = right


def stack_kernel(*refs):
    for j, ref in enumerate(refs[:-1]):
        refs[-1][j] = ref[...]


def forward_kernel(near, far, up, down, cross_out, own_out, rows, total):
    period, half = near.shape[1:]
    hidden_count = up.shape[1]
    chunk = min(CHUNK, hidden_count)
    stack_blocks([near, far], rows)
    x = rows[...]
    top = top_rows(x.shape[0], period)
    for low in range(0, hidden_count, chunk):
        n = slice(low, low + chunk)
        u = join_halves(dot(x, up[:half, n]), dot(x, up[half:, n]), period)
        hidden = u * jax.nn.sigmoid(u)
        left = jnp.where(top, hidden, 0.0).astype(BF16)
        right = jnp.where(top, 0.0, hidden).astype(BF16)
        part = dot(left, down[n, :half]) + dot(right, down[n, half:])
        total[...] = part if low == 0 else total[...] + part
    write_blocks(total, own_out, cross_out)


def write_blocks(total, own_out, cross_out):
    chips, period, _ = own_out.shape
    for j in range(chips):
        own_out[j] = total[j * period : (j + 1) * period, :]
        low = (chips + j) * period
        cross_out[j] = total[low : low + period, :].astype(BF16)


def backward_kernel(
    place,
    flags,
    gathered,
    near_g,
    far_g,
    up,
    down,
    router,
    *refs,
):
    term_in = refs[:-6]
    cross_out, own_out, term_out, x_n, x_g, total = refs[-6:]
    period, half = own_out.shape[1:]
    all_rows = x_n.shape[0]
    hidden_count = up.shape[1]
    chunk = min(CHUNK, hidden_count)
    top = top_rows(all_rows, period)
    stack_gathered(flags, gathered, place, x_n)
    stack_blocks([near_g, far_g], x_g)
    x = x_n[...]
    g = x_g[...]
    vector = jnp.where(top, router[:, :half], router[:, half:])
    logit = jnp.sum(x.astype(F32) * vector, axis=1, keepdims=True)
    wide = jnp.broadcast_to(logit, (all_rows, 128))
    gate = jax.nn.sigmoid(join_halves(wide, wide, period))
    inner = jnp.zeros((all_rows, 1), F32)
    for low in range(0, hidden_count, chunk):
        n = slice(low, low + chunk)
        u = join_halves(dot(x, up[:half, n]), dot(x, up[half:, n]), period)
        grad_hidden = join_halves(
            dot(g, down[n, :half], NT), dot(g, down[n, half:], NT), period
        )
        grad_hidden = grad_hidden * gate[:, :1]
        sig = jax.nn.sigmoid(u)
        hidden = (u * sig).astype(BF16).astype(F32)
        inner = inner + jnp.sum(grad_hidden * hidden, axis=1, keepdims=True)
        grad_up = grad_hidden * sig * (1.0 + u * (1.0 - sig))
        left = jnp.where(top, grad_up, 0.0).astype(BF16)
        right = jnp.where(top, 0.0, grad_up).astype(BF16)
        part = dot(left, up[:half, n], NT) + dot(right, up[half:, n], NT)
        total[...] = part if low == 0 else total[...] + part

    logit = inner * (1.0 - gate)
    total[...] += logit[:, :1] * vector
    write_blocks(total, own_out, cross_out)
    rest = logit.T[:1]
    first = lax.rem(lax.broadcasted_iota(jnp.int32, (1, all_rows), 1), period) < period // 2
    pieces = []
    for _ in range(3):
        piece = rest.astype(BF16).astype(F32)
        pieces.append(piece)
        rest = rest - piece
    sums = []
    for side in (first, jnp.logical_not(first)):
        stacked = jnp.concatenate(
            [jnp.where(side, p, 0.0) for p in pieces] + [jnp.zeros((5, all_rows), F32)], axis=0
        )
        sums.append(jnp.sum(dot(stacked.astype(BF16), x), axis=0, keepdims=True))
    term = jnp.concatenate(sums, axis=0)
    for before in term_in:
        term = term + before[...]
    term_out[...] = term


def pair_kernel(own, crossed, *outs):
    for j, out in enumerate(outs):
        out[...] = (own[j] + crossed[j].astype(F32)).astype(out.dtype)


def added(terms):
    total = terms[0][...]
    for term in terms[1:]:
        total = total + term[...].astype(F32)
    return total


def forward_end_kernel(tick, rows, gate, routes, *refs):
    block = added(refs[:-1])
    renewed = (rows[...].astype(F32) + gate[:, :1] * block).astype(BF16)
    send_off(refs[-1], renewed, routes[0, tick, 0:1])


def backward_end_kernel(tick, upstream, saved, gain, routes, *refs):
    grad_normed = added(refs[:-1])
    picked = saved[tick].astype(F32)
    inv_rms = inverse_rms(picked)
    scaled_grad = grad_normed * by_half(gain[...], picked.shape[0])
    unit = picked * inv_rms
    mean = halves(jnp.sum(scaled_grad * unit, axis=1, keepdims=True)) / (2 * picked.shape[1])
    grad_rows = inv_rms * (scaled_grad - unit * mean)
    renewed = (upstream[...].astype(F32) + grad_rows).astype(BF16)
    send_off(refs[-1], renewed, routes[0, tick, 1:2])


def term_pair_kernel(near, far, out):
    out[...] = near[...] + far[...]


def term_end_kernel(scale, place, *refs):
    out = refs[-1]
    chips = len(refs) - 1
    chip = place[2:3, :1]
    total = jnp.zeros(refs[0].shape, F32)
    for low in range(chips):
        for j in range(chips):
            total = total + jnp.where(lax.rem(chip - j + chips, chips) == low, refs[j][...], 0.0)
    half = refs[0].shape[1]
    out[:, :half] = total[0:1] * scale
    out[:, half:] = total[1:2] * scale


class Order:
    def __init__(self):
        self.token = []

    def __call__(self, kernel, outs, *operands, smem=0, limit=8, scratch=(), cost=None):
        count = len(self.token)

        def body(*refs):
            kernel(*refs[count:])

        result = pl.pallas_call(
            body,
            out_shape=outs,
            in_specs=[ANY] * count + [SMEM] * smem + [VMEM] * (len(operands) - smem),
            out_specs=jax.tree.map(lambda _: VMEM, outs),
            scratch_shapes=scratch,
            compiler_params=pltpu.CompilerParams(vmem_limit_bytes=limit * 2**20),
            cost_estimate=cost or SMALL,
        )(*self.token, *operands)
        self.token = [result[0] if isinstance(result, (list, tuple)) else result]
        return result

    def write(self, result, tick, ticks, act, moved):
        before = [] if result is None else [result]
        tokens, width = act.shape
        token, result = pl.pallas_call(
            output_kernel,
            grid=(1,),
            out_shape=[shaped((8, LANES), F32), shaped((1, ticks, tokens, width))],
            in_specs=[ANY, whole(act.shape), whole(moved.shape)] + [ANY] * len(before),
            out_specs=[
                whole((8, LANES)),
                pl.BlockSpec((1, 1, tokens, width), lambda i: (0, tick, 0, 0)),
            ],
            input_output_aliases={3: 1} if before else {},
            compiler_params=pltpu.CompilerParams(vmem_limit_bytes=8 * 2**20),
            cost_estimate=SMALL,
        )(*self.token, act, moved, *before)
        self.token = [token]
        return result


def shaped(shape, dtype=BF16):
    return jax.ShapeDtypeStruct(tuple(shape), dtype)


def whole(shape):
    return pl.BlockSpec(tuple(shape), lambda i: (0,) * len(shape))


def cost_of(matmuls, rows, weight):
    size = weight.shape[0] * weight.shape[1]
    return pl.CostEstimate(
        flops=4 * matmuls * rows * size,
        bytes_accessed=4 * size,
        transcendentals=rows * weight.shape[1],
    )


def per_device(
    arrive, entering, stash, back_arrive, head_grad, norm_gain, router, w_up, w_down, routes
):
    section = lax.axis_index("section")
    last = lax.axis_size("section") - 1
    dp_count = lax.axis_size("dp")
    chips = dp_count // CORES
    up, down = w_up[0], w_down[0]
    slots = routes.shape[3]
    tokens, width = arrive.shape[1:]
    half = width // 2
    ticks = stash.shape[1]
    period = 2 * slots
    flags = jnp.stack(
        [
            (section == 0).astype(jnp.int32),
            (section == last).astype(jnp.int32),
            lax.axis_index("dp") // CORES,
            lax.axis_index("dp") % CORES,
        ]
    )

    packed = shaped((period, half))
    packed_sum = shaped((period, half), F32)
    packet = shaped((period, half + LANES))
    full = shaped((tokens, width))
    gate_shape = shaped((period, LANES), F32)
    part_outs = [shaped((chips, period, half)), shaped((chips, period, half), F32)]
    all_rows = dp_count * period
    scratch_rows = pltpu.VMEM((all_rows, half), BF16)
    scratch_total = pltpu.VMEM((all_rows, half), F32)
    run = Order()

    def stacked(blocks):
        return run(stack_kernel, shaped((len(blocks), *blocks[0].shape)), *blocks)

    def pair(own, crossed):
        outs = [packed_sum] + [packed] * (chips - 1)
        return collect(run(pair_kernel, outs, own, crossed))

    forward_in, backward_in = arrive[0], back_arrive[0]
    forward_normed, forward_rows, gate, place = run(
        first_forward_kernel,
        [packed, packed, gate_shape, shaped((8, LANES), jnp.int32)],
        flags,
        forward_in,
        routes,
        norm_gain,
        router,
        smem=1,
    )
    forward_blocks = spread(forward_normed)
    saved_first, saved_later, backward_rows, saved = run(
        first_backward_kernel,
        [
            packed,
            shaped((ticks - 1, period, half)),
            packed,
            shaped((ticks, period, half)),
        ],
        backward_in,
        stash[0],
        routes,
        norm_gain,
        limit=16,
    )
    gathered_first = lax.all_gather(saved_first, "dp", axis=0)
    gathered_later = lax.all_gather(saved_later, "dp", axis=0)
    backward_blocks = spread(backward_rows)
    term = []
    forward_out = backward_out = None
    forward_base = shift_section(forward_in, 1)
    backward_base = shift_section(backward_in, -1)
    near = stacked(forward_blocks)
    far = swap_core(near)

    for k in range(ticks):
        more = k + 1 < ticks
        if k > 0:
            forward_in = run(land_kernel, full, forward_in, forward_moved)
            if more:
                forward_base = shift_section(forward_in, 1)
        cross, own = run(
            forward_kernel,
            part_outs,
            near,
            far,
            up,
            down,
            limit=WEIGHTS_LIMIT,
            scratch=[scratch_rows, scratch_total],
            cost=cost_of(2, all_rows, up),
        )
        crossed = swap_core(cross)
        near = stacked(backward_blocks)
        far = swap_core(near)
        terms = pair(own, crossed)
        if more:
            forward_next, forward_picked = run(
                functools.partial(source_kernel, k + 1, 0),
                [full, packed],
                place,
                forward_base,
                entering,
                routes,
            )
        if k > 0:
            backward_in = run(land_kernel, full, backward_in, backward_moved)
            if more:
                backward_base = shift_section(backward_in, -1)

        cross, own, part = run(
            functools.partial(backward_kernel, (k - 1,) if k else ()),
            part_outs + [shaped((2, half), F32)],
            flags,
            gathered_later if k else gathered_first,
            near,
            far,
            up,
            down,
            router,
            *term,
            smem=1,
            limit=WEIGHTS_LIMIT,
            scratch=[scratch_rows, scratch_rows, scratch_total],
            cost=cost_of(3, all_rows, up),
        )
        term = [part]
        crossed = swap_core(cross)
        forward_new = run(
            functools.partial(forward_end_kernel, k), packet, forward_rows, gate, routes, *terms
        )
        if more:
            forward_moved = shift_section(forward_new, 1)
        terms = pair(own, crossed)

        if more:
            backward_next, backward_picked = run(
                functools.partial(source_kernel, k + 1, 1),
                [full, packed],
                place,
                backward_base,
                head_grad,
                routes,
            )
            forward_normed, forward_rows, gate = run(
                functools.partial(next_forward_kernel, k + 1),
                [packed, packed, gate_shape],
                forward_picked,
                forward_moved,
                routes,
                norm_gain,
                router,
            )
            forward_blocks = spread(forward_normed)
        else:
            total = run(term_pair_kernel, shaped((2, half), F32), part, swap_core(part))
            total_blocks = spread(total)
        forward_out = run.write(forward_out, k, ticks, forward_in, forward_new)

        backward_new = run(
            functools.partial(backward_end_kernel, k),
            packet,
            backward_rows,
            saved,
            norm_gain,
            routes,
            *terms,
        )
        if more:
            backward_moved = shift_section(backward_new, -1)
            near = stacked(forward_blocks)
            far = swap_core(near)
            backward_rows = run(
                functools.partial(next_backward_kernel, k + 1),
                packed,
                backward_picked,
                backward_moved,
                routes,
            )
            backward_blocks = spread(backward_rows)
        backward_out = run.write(backward_out, k, ticks, backward_in, backward_new)
        if more:
            forward_in, backward_in = forward_next, backward_next

    scale = 1.0 / float(ticks * slots * dp_count)
    router_grad = run(
        functools.partial(term_end_kernel, scale), shaped((1, width), F32), place, *total_blocks
    )
    return forward_out, backward_out, router_grad


def solution(mesh):
    in_specs = (
        P("section", "dp", None),
        P(None, "dp", None),
        P("section", None, "dp", None),
        P("section", "dp", None),
        P(None, "dp", None),
        P("section", None),
        P("section", None),
        P("section", None, "dp"),
        P("section", "dp", None),
        P("section", None, None, "dp"),
    )
    out_specs = (P("section", None, "dp", None), P("section", None, "dp", None), P("section", None))
    return jax.shard_map(
        per_device, mesh=mesh, in_specs=in_specs, out_specs=out_specs, check_vma=False
    )
```

```python
import functools

import jax
import jax.numpy as jnp
from jax import lax
from jax.experimental import pallas as pl
from jax.experimental.pallas import tpu as pltpu
from jax.sharding import PartitionSpec as P

EPS = 1e-05
CORES = 2
CHUNK = 256
LANES = 128
WEIGHTS_LIMIT = 26
BF16 = jnp.bfloat16
F32 = jnp.float32
NN = (((1,), (0,)), ((), ()))
NT = (((1,), (1,)), ((), ()))
VMEM = pl.BlockSpec(memory_space=pltpu.VMEM)
SMEM = pl.BlockSpec(memory_space=pltpu.SMEM)
ANY = pl.BlockSpec(memory_space=pl.ANY)
SMALL = pl.CostEstimate(flops=0, bytes_accessed=2 * 2**20, transcendentals=0)


def shift_section(block, step):
    count = lax.axis_size("section")
    route = [(i - step, i) for i in range(count) if 0 <= i - step < count]
    return lax.ppermute(block, "section", route)


def swap_core(block):
    count = lax.axis_size("dp")
    return lax.ppermute(block, "dp", [(i, i ^ 1) for i in range(count)])


def shift_chip(block, step):
    count = lax.axis_size("dp")
    return lax.ppermute(block, "dp", [(i, (i + CORES * step) % count) for i in range(count)])


def spread(block):
    return [block] + [shift_chip(block, j) for j in range(1, lax.axis_size("dp") // CORES)]


def collect(blocks):
    return [blocks[0]] + [shift_chip(b, -j) for j, b in enumerate(blocks) if j > 0]


def dot(a, b, dims=NN):
    return lax.dot_general(a, b, dims, preferred_element_type=F32)


def halves(column):
    rows = column.shape[0]
    wide = jnp.broadcast_to(column, (rows, 128))
    return (wide + pltpu.roll(wide, rows // 2, 0))[:, :1]


def column_of(route):
    slots = route.shape[1]
    row = lax.rem(lax.broadcasted_iota(jnp.int32, (2 * slots, slots), 0), slots)
    same = row == lax.broadcasted_iota(jnp.int32, (2 * slots, slots), 1)
    return jnp.sum(jnp.where(same, route, 0), axis=1, keepdims=True)


def row_of(column):
    count = column.shape[0]
    shape = (count, count)
    same = lax.broadcasted_iota(jnp.int32, shape, 0) == lax.broadcasted_iota(jnp.int32, shape, 1)
    return jnp.sum(jnp.where(same, column, 0), axis=0, keepdims=True)


def arrived(moved):
    half = moved.shape[1] - LANES
    place = row_of(moved[:, half : half + 1].astype(F32).astype(jnp.int32)) - 1
    return moved[:, :half], jnp.where(place < 0, -2, place)


def send_off(out, rows, route):
    half = rows.shape[1]
    out[:, :half] = rows
    place = (column_of(route) + 1).astype(F32).astype(BF16)
    out[:, half:] = jnp.broadcast_to(place, (rows.shape[0], LANES))


def top_rows(rows, period):
    return lax.rem(lax.broadcasted_iota(jnp.int32, (rows, 1), 0), period) < period // 2


def pick(activity, route_column):
    rows, half = route_column.shape[0], activity.shape[1] // 2
    tokens = activity.shape[0]
    hit = route_column == lax.broadcasted_iota(jnp.int32, (rows, tokens), 1)
    top = top_rows(rows, rows)
    left = jnp.where(hit & top, 1.0, 0.0).astype(BF16)
    right = jnp.where(hit & jnp.logical_not(top), 1.0, 0.0).astype(BF16)
    return dot(left, activity[:, :half]) + dot(right, activity[:, half:])


def put(activity, rows, route_row):
    tokens, half = activity.shape[0], activity.shape[1] // 2
    count = route_row.shape[1]
    hit = route_row == lax.broadcasted_iota(jnp.int32, (tokens, count), 0)
    first = lax.broadcasted_iota(jnp.int32, (tokens, count), 1) < count // 2
    left = jnp.where(hit & first, 1.0, 0.0)
    right = jnp.where(hit & jnp.logical_not(first), 1.0, 0.0)
    taken = jnp.sum(left, axis=1, keepdims=True) > 0.5
    new_left = jnp.where(taken, dot(left.astype(BF16), rows), activity[:, :half].astype(F32))
    new_right = jnp.where(taken, dot(right.astype(BF16), rows), activity[:, half:].astype(F32))
    return new_left.astype(BF16), new_right.astype(BF16)


def by_half(vector, rows):
    half = vector.shape[1] // 2
    return jnp.where(top_rows(rows, rows), vector[:, :half], vector[:, half:])


def inverse_rms(rows):
    width = 2 * rows.shape[1]
    mean = halves(jnp.sum(rows * rows, axis=1, keepdims=True)) / width
    return lax.rsqrt(mean + EPS)


def normalize(rows, gain, router):
    normed = (rows * inverse_rms(rows) * by_half(gain, rows.shape[0])).astype(BF16)
    logit = jnp.sum(normed.astype(F32) * by_half(router, rows.shape[0]), axis=1, keepdims=True)
    return normed, jax.nn.sigmoid(halves(logit))


def stack_blocks(refs, place, out):
    blocks = [ref[(j, *place)].astype(F32) for ref in refs for j in range(ref.shape[0])]
    out[...] = jnp.concatenate(blocks, axis=0).astype(BF16)


def join_halves(left, right, period):
    rows = left.shape[0]
    top = top_rows(rows, period)
    return jnp.where(
        top,
        left + pltpu.roll(right, rows - period // 2, 0),
        right + pltpu.roll(left, period // 2, 0),
    )


def first_forward_kernel(flags, act, routes, gain, router, normed_out, rows_out, gate_out, where_out):
    rows = pick(act[...], column_of(routes[0, 0, 0:1]))
    normed, gate = normalize(rows, gain[...], router[...])
    rows_out[...] = rows.astype(BF16)
    normed_out[...] = normed
    gate_out[...] = jnp.broadcast_to(gate, gate_out.shape)
    line = lax.broadcasted_iota(jnp.int32, where_out.shape, 0)
    where_out[...] = jnp.where(line == 0, flags[0], jnp.where(line == 1, flags[1], flags[2]))


def first_backward_kernel(act, stash, routes, gain, first_out, later_out, rows_out, saved_out):
    ticks = stash.shape[0]
    upstream = pick(act[...], column_of(routes[0, 0, 1:2])).astype(BF16)
    rows_out[...] = upstream
    first_out[1] = upstream
    for k in range(ticks):
        rows = pick(stash[k], column_of(routes[0, k, 1:2]))
        saved_out[k] = rows.astype(BF16)
        count = rows.shape[0]
        normed = (rows * inverse_rms(rows) * by_half(gain[...], count)).astype(BF16)
        if k == 0:
            first_out[0] = normed
        else:
            later_out[k - 1] = normed


def source_kernel(tick, way, place, moved, fresh, routes, source_out, rows_out):
    source = jnp.where(place[way : way + 1, :1] == 1, fresh[tick - 1], moved[...])
    source_out[...] = source
    rows_out[...] = pick(source, column_of(routes[0, tick, way : way + 1])).astype(BF16)


def select(base, packet, route):
    moved, behind_row = arrived(packet)
    column = column_of(route)
    rows = column.shape[0]
    hit = column == behind_row
    same = top_rows(rows, rows) == (lax.broadcasted_iota(jnp.int32, (rows, rows), 1) < rows // 2)
    match = jnp.where(hit & same, 1.0, 0.0)
    found = jnp.max(match, axis=1, keepdims=True) > 0.5
    return jnp.where(found, dot(match.astype(BF16), moved), base.astype(F32))


def next_forward_kernel(tick, base, moved, routes, gain, router, normed_out, rows_out, gate_out):
    rows = select(base[...], moved[...], routes[0, tick, 0:1])
    normed, gate = normalize(rows, gain[...], router[...])
    rows_out[...] = rows.astype(BF16)
    normed_out[...] = normed
    gate_out[...] = jnp.broadcast_to(gate, gate_out.shape)


def next_backward_kernel(tick, base, moved, routes, rows_out):
    rows_out[...] = select(base[...], moved[...], routes[0, tick, 1:2]).astype(BF16)


def land_kernel(source, moved, out):
    half = source.shape[1] // 2
    rows, places = arrived(moved[...])
    left, right = put(source[...], rows, places)
    out[:, :half] = left
    out[:, half:] = right


def output_kernel(token, act, moved, *outs):
    done, out = outs[-2:]
    done[...] = jnp.zeros_like(done)
    half = act.shape[1] // 2
    rows, places = arrived(moved[...])
    left, right = put(act[...], rows, places)
    out[0, 0, :, :half] = left
    out[0, 0, :, half:] = right


def stack_kernel(*refs):
    for j, ref in enumerate(refs[:-1]):
        refs[-1][j] = ref[...]


def forward_kernel(near, far, up, down, cross_out, own_out, rows, total):
    period, half = near.shape[1:]
    hidden_count = up.shape[1]
    chunk = min(CHUNK, hidden_count)
    stack_blocks([near, far], (), rows)
    x = rows[...]
    top = top_rows(x.shape[0], period)
    for low in range(0, hidden_count, chunk):
        n = slice(low, low + chunk)
        u = join_halves(dot(x, up[:half, n]), dot(x, up[half:, n]), period)
        hidden = u * jax.nn.sigmoid(u)
        left = jnp.where(top, hidden, 0.0).astype(BF16)
        right = jnp.where(top, 0.0, hidden).astype(BF16)
        part = dot(left, down[n, :half]) + dot(right, down[n, half:])
        total[...] = part if low == 0 else total[...] + part
    write_blocks(total, own_out, cross_out)


def write_blocks(total, own_out, cross_out):
    chips, period, _ = own_out.shape
    for j in range(chips):
        own_out[j] = total[j * period : (j + 1) * period, :]
        low = (chips + j) * period
        cross_out[j] = total[low : low + period, :].astype(BF16)


def backward_kernel(
    normed_place,
    grad_place,
    near_n,
    far_n,
    near_g,
    far_g,
    up,
    down,
    router,
    *refs,
):
    term_in = refs[:-6]
    cross_out, own_out, term_out, x_n, x_g, total = refs[-6:]
    period, half = own_out.shape[1:]
    all_rows = x_n.shape[0]
    hidden_count = up.shape[1]
    chunk = min(CHUNK, hidden_count)
    top = top_rows(all_rows, period)
    stack_blocks([near_n, far_n], normed_place, x_n)
    stack_blocks([near_g, far_g], grad_place, x_g)
    x = x_n[...]
    g = x_g[...]
    vector = jnp.where(top, router[:, :half], router[:, half:])
    logit = jnp.sum(x.astype(F32) * vector, axis=1, keepdims=True)
    wide = jnp.broadcast_to(logit, (all_rows, 128))
    gate = jax.nn.sigmoid(join_halves(wide, wide, period))
    inner = jnp.zeros((all_rows, 1), F32)
    for low in range(0, hidden_count, chunk):
        n = slice(low, low + chunk)
        u = join_halves(dot(x, up[:half, n]), dot(x, up[half:, n]), period)
        grad_hidden = join_halves(
            dot(g, down[n, :half], NT), dot(g, down[n, half:], NT), period
        )
        grad_hidden = grad_hidden * gate[:, :1]
        sig = jax.nn.sigmoid(u)
        hidden = (u * sig).astype(BF16).astype(F32)
        inner = inner + jnp.sum(grad_hidden * hidden, axis=1, keepdims=True)
        grad_up = grad_hidden * sig * (1.0 + u * (1.0 - sig))
        left = jnp.where(top, grad_up, 0.0).astype(BF16)
        right = jnp.where(top, 0.0, grad_up).astype(BF16)
        part = dot(left, up[:half, n], NT) + dot(right, up[half:, n], NT)
        total[...] = part if low == 0 else total[...] + part

    logit = inner * (1.0 - gate)
    total[...] += logit[:, :1] * vector
    write_blocks(total, own_out, cross_out)
    rest = logit.T[:1]
    first = lax.rem(lax.broadcasted_iota(jnp.int32, (1, all_rows), 1), period) < period // 2
    pieces = []
    for _ in range(3):
        piece = rest.astype(BF16).astype(F32)
        pieces.append(piece)
        rest = rest - piece
    sums = []
    for side in (first, jnp.logical_not(first)):
        stacked = jnp.concatenate(
            [jnp.where(side, p, 0.0) for p in pieces] + [jnp.zeros((5, all_rows), F32)], axis=0
        )
        sums.append(jnp.sum(dot(stacked.astype(BF16), x), axis=0, keepdims=True))
    term = jnp.concatenate(sums, axis=0)
    for before in term_in:
        term = term + before[...]
    term_out[...] = term


def pair_kernel(own, crossed, *outs):
    for j, out in enumerate(outs):
        out[...] = (own[j] + crossed[j].astype(F32)).astype(out.dtype)


def added(terms):
    total = terms[0][...]
    for term in terms[1:]:
        total = total + term[...].astype(F32)
    return total


def forward_end_kernel(tick, rows, gate, routes, *refs):
    block = added(refs[:-1])
    renewed = (rows[...].astype(F32) + gate[:, :1] * block).astype(BF16)
    send_off(refs[-1], renewed, routes[0, tick, 0:1])


def backward_end_kernel(tick, upstream, saved, gain, routes, *refs):
    grad_normed = added(refs[:-1])
    picked = saved[tick].astype(F32)
    inv_rms = inverse_rms(picked)
    scaled_grad = grad_normed * by_half(gain[...], picked.shape[0])
    unit = picked * inv_rms
    mean = halves(jnp.sum(scaled_grad * unit, axis=1, keepdims=True)) / (2 * picked.shape[1])
    grad_rows = inv_rms * (scaled_grad - unit * mean)
    renewed = (upstream[...].astype(F32) + grad_rows).astype(BF16)
    send_off(refs[-1], renewed, routes[0, tick, 1:2])


def term_pair_kernel(near, far, out):
    out[...] = near[...] + far[...]


def term_end_kernel(scale, place, *refs):
    out = refs[-1]
    chips = len(refs) - 1
    chip = place[2:3, :1]
    total = jnp.zeros(refs[0].shape, F32)
    for low in range(chips):
        for j in range(chips):
            total = total + jnp.where(lax.rem(chip - j + chips, chips) == low, refs[j][...], 0.0)
    half = refs[0].shape[1]
    out[:, :half] = total[0:1] * scale
    out[:, half:] = total[1:2] * scale


class Order:
    def __init__(self):
        self.token = []

    def __call__(
        self, kernel, outs, *operands, smem=0, limit=8, scratch=(), cost=None, through=None
    ):
        count = len(self.token)
        passed = 0 if through is None else 1

        def body(*refs):
            kernel(*refs[count + passed : len(refs) - passed])

        in_specs = [ANY] * (count + passed)
        out_specs = jax.tree.map(lambda _: VMEM, outs)
        aliases = {}
        if passed:
            out_specs[-1] = ANY
            aliases = {count: len(outs) - 1}
            operands = (through, *operands)
        result = pl.pallas_call(
            body,
            out_shape=outs,
            in_specs=in_specs + [SMEM] * smem + [VMEM] * (len(operands) - smem - passed),
            out_specs=out_specs,
            input_output_aliases=aliases,
            scratch_shapes=scratch,
            compiler_params=pltpu.CompilerParams(vmem_limit_bytes=limit * 2**20),
            cost_estimate=cost or SMALL,
        )(*self.token, *operands)
        several = isinstance(result, (list, tuple))
        self.token = [result[-1 - passed] if several else result]
        return result

    def write(self, result, tick, ticks, act, moved):
        before = [] if result is None else [result]
        tokens, width = act.shape
        token, result = pl.pallas_call(
            output_kernel,
            grid=(1,),
            out_shape=[shaped((8, LANES), F32), shaped((1, ticks, tokens, width))],
            in_specs=[ANY, whole(act.shape), whole(moved.shape)] + [ANY] * len(before),
            out_specs=[
                whole((8, LANES)),
                pl.BlockSpec((1, 1, tokens, width), lambda i: (0, tick, 0, 0)),
            ],
            input_output_aliases={3: 1} if before else {},
            compiler_params=pltpu.CompilerParams(vmem_limit_bytes=8 * 2**20),
            cost_estimate=SMALL,
        )(*self.token, act, moved, *before)
        self.token = [token]
        return result


def shaped(shape, dtype=BF16):
    return jax.ShapeDtypeStruct(tuple(shape), dtype)


def whole(shape):
    return pl.BlockSpec(tuple(shape), lambda i: (0,) * len(shape))


def cost_of(matmuls, rows, weight):
    size = weight.shape[0] * weight.shape[1]
    return pl.CostEstimate(
        flops=4 * matmuls * rows * size,
        bytes_accessed=4 * size,
        transcendentals=rows * weight.shape[1],
    )


def per_device(
    arrive, entering, stash, back_arrive, head_grad, norm_gain, router, w_up, w_down, routes
):
    section = lax.axis_index("section")
    last = lax.axis_size("section") - 1
    dp_count = lax.axis_size("dp")
    chips = dp_count // CORES
    up, down = w_up[0], w_down[0]
    slots = routes.shape[3]
    tokens, width = arrive.shape[1:]
    half = width // 2
    ticks = stash.shape[1]
    period = 2 * slots
    flags = jnp.stack(
        [
            (section == 0).astype(jnp.int32),
            (section == last).astype(jnp.int32),
            lax.axis_index("dp") // CORES,
        ]
    )

    packed = shaped((period, half))
    packed_sum = shaped((period, half), F32)
    packet = shaped((period, half + LANES))
    full = shaped((tokens, width))
    gate_shape = shaped((period, LANES), F32)
    part_outs = [shaped((chips, period, half)), shaped((chips, period, half), F32)]
    all_rows = dp_count * period
    scratch_rows = pltpu.VMEM((all_rows, half), BF16)
    scratch_total = pltpu.VMEM((all_rows, half), F32)
    run = Order()

    def stacked(blocks):
        return run(stack_kernel, shaped((len(blocks), *blocks[0].shape)), *blocks)

    def pair(own, crossed):
        outs = [packed_sum] + [packed] * (chips - 1)
        return collect(run(pair_kernel, outs, own, crossed))

    forward_in, backward_in = arrive[0], back_arrive[0]
    forward_normed, forward_rows, gate, place = run(
        first_forward_kernel,
        [packed, packed, gate_shape, shaped((8, LANES), jnp.int32)],
        flags,
        forward_in,
        routes,
        norm_gain,
        router,
        smem=1,
    )
    forward_blocks = spread(forward_normed)
    saved_first, saved_later, backward_rows, saved = run(
        first_backward_kernel,
        [
            shaped((2, period, half)),
            shaped((ticks - 1, period, half)),
            packed,
            shaped((ticks, period, half)),
        ],
        backward_in,
        stash[0],
        routes,
        norm_gain,
        limit=16,
    )
    later_blocks = spread(saved_later)
    backward_blocks = spread(saved_first)
    term = []
    forward_out = backward_out = None
    forward_base = shift_section(forward_in, 1)
    backward_base = shift_section(backward_in, -1)
    near = stacked(forward_blocks)
    far = swap_core(near)

    for k in range(ticks):
        more = k + 1 < ticks
        if k > 0:
            forward_in = run(land_kernel, full, forward_in, forward_moved)
            if more:
                forward_base = shift_section(forward_in, 1)
        cross, own = run(
            forward_kernel,
            part_outs,
            near,
            far,
            up,
            down,
            limit=WEIGHTS_LIMIT,
            scratch=[scratch_rows, scratch_total],
            cost=cost_of(2, all_rows, up),
        )
        crossed = swap_core(cross)
        near = stacked(backward_blocks)
        far = swap_core(near)
        terms = pair(own, crossed)
        if more:
            forward_next, forward_picked = run(
                functools.partial(source_kernel, k + 1, 0),
                [full, packed],
                place,
                forward_base,
                entering,
                routes,
            )
        if k > 0:
            backward_in = run(land_kernel, full, backward_in, backward_moved)
            if more:
                backward_base = shift_section(backward_in, -1)

        if k == 0:
            near_n, far_n, normed_place, grad_place = near, far, (0,), (1,)
        else:
            near_n, far_n, normed_place, grad_place = near_later, far_later, (k - 1,), ()
        cross, own, part = run(
            functools.partial(backward_kernel, normed_place, grad_place),
            part_outs + [shaped((2, half), F32)],
            near_n,
            far_n,
            near,
            far,
            up,
            down,
            router,
            *term,
            limit=WEIGHTS_LIMIT,
            scratch=[scratch_rows, scratch_rows, scratch_total],
            cost=cost_of(3, all_rows, up),
        )
        term = [part]
        forward_new, cross = run(
            functools.partial(forward_end_kernel, k),
            [packet, shaped(cross.shape)],
            forward_rows,
            gate,
            routes,
            *terms,
            through=cross,
        )
        crossed = swap_core(cross)
        if more:
            forward_moved = shift_section(forward_new, 1)
        if k == 0:
            near_later = stacked(later_blocks)
            far_later = swap_core(near_later)
        terms = pair(own, crossed)

        if more:
            backward_next, backward_picked = run(
                functools.partial(source_kernel, k + 1, 1),
                [full, packed],
                place,
                backward_base,
                head_grad,
                routes,
            )
            forward_normed, forward_rows, gate = run(
                functools.partial(next_forward_kernel, k + 1),
                [packed, packed, gate_shape],
                forward_picked,
                forward_moved,
                routes,
                norm_gain,
                router,
            )
            forward_blocks = spread(forward_normed)
        else:
            total = run(term_pair_kernel, shaped((2, half), F32), part, swap_core(part))
            total_blocks = spread(total)
        forward_out = run.write(forward_out, k, ticks, forward_in, forward_new)

        backward_new = run(
            functools.partial(backward_end_kernel, k),
            packet,
            backward_rows,
            saved,
            norm_gain,
            routes,
            *terms,
        )
        if more:
            backward_moved = shift_section(backward_new, -1)
            near = stacked(forward_blocks)
            far = swap_core(near)
            backward_rows = run(
                functools.partial(next_backward_kernel, k + 1),
                packed,
                backward_picked,
                backward_moved,
                routes,
            )
            backward_blocks = spread(backward_rows)
        backward_out = run.write(backward_out, k, ticks, backward_in, backward_new)
        if more:
            forward_in, backward_in = forward_next, backward_next

    scale = 1.0 / float(ticks * slots * dp_count)
    router_grad = run(
        functools.partial(term_end_kernel, scale), shaped((1, width), F32), place, *total_blocks
    )
    return forward_out, backward_out, router_grad


def solution(mesh):
    in_specs = (
        P("section", "dp", None),
        P(None, "dp", None),
        P("section", None, "dp", None),
        P("section", "dp", None),
        P(None, "dp", None),
        P("section", None),
        P("section", None),
        P("section", None, "dp"),
        P("section", "dp", None),
        P("section", None, None, "dp"),
    )
    out_specs = (P("section", None, "dp", None), P("section", None, "dp", None), P("section", None))
    return jax.shard_map(
        per_device, mesh=mesh, in_specs=in_specs, out_specs=out_specs, check_vma=False
    )
```

```python
import functools

import jax
import jax.numpy as jnp
from jax import lax
from jax.experimental import pallas as pl
from jax.experimental.pallas import tpu as pltpu
from jax.sharding import PartitionSpec as P

EPS = 1e-05
CORES = 2
CHUNK = 256
LANES = 128
WEIGHTS_LIMIT = 26
BF16 = jnp.bfloat16
F32 = jnp.float32
NN = (((1,), (0,)), ((), ()))
NT = (((1,), (1,)), ((), ()))
VMEM = pl.BlockSpec(memory_space=pltpu.VMEM)
SMEM = pl.BlockSpec(memory_space=pltpu.SMEM)
ANY = pl.BlockSpec(memory_space=pl.ANY)
SMALL = pl.CostEstimate(flops=0, bytes_accessed=2 * 2**20, transcendentals=0)


def shift_section(block, step):
    count = lax.axis_size("section")
    return lax.ppermute(block, "section", [(i, (i + step) % count) for i in range(count)])


def swap_core(block):
    count = lax.axis_size("dp")
    return lax.ppermute(block, "dp", [(i, i ^ 1) for i in range(count)])


def shift_chip(block, step):
    count = lax.axis_size("dp")
    return lax.ppermute(block, "dp", [(i, (i + CORES * step) % count) for i in range(count)])


def spread(block):
    return [block] + [shift_chip(block, j) for j in range(1, lax.axis_size("dp") // CORES)]


def collect(blocks):
    return [blocks[0]] + [shift_chip(b, -j) for j, b in enumerate(blocks) if j > 0]


def dot(a, b, dims=NN):
    return lax.dot_general(a, b, dims, preferred_element_type=F32)


def halves(column):
    rows = column.shape[0]
    wide = jnp.broadcast_to(column, (rows, 128))
    return (wide + pltpu.roll(wide, rows // 2, 0))[:, :1]


def column_of(route):
    slots = route.shape[1]
    row = lax.rem(lax.broadcasted_iota(jnp.int32, (2 * slots, slots), 0), slots)
    same = row == lax.broadcasted_iota(jnp.int32, (2 * slots, slots), 1)
    return jnp.sum(jnp.where(same, route, 0), axis=1, keepdims=True)


def row_of(column):
    count = column.shape[0]
    shape = (count, count)
    same = lax.broadcasted_iota(jnp.int32, shape, 0) == lax.broadcasted_iota(jnp.int32, shape, 1)
    return jnp.sum(jnp.where(same, column, 0), axis=0, keepdims=True)


def arrived(moved, at_end=None):
    half = moved.shape[1] - LANES
    place = row_of(moved[:, half : half + 1].astype(F32).astype(jnp.int32)) - 1
    none = place < 0
    if at_end is not None:
        none = none | (at_end == 1)
    return moved[:, :half], jnp.where(none, -2, place)


def send_off(out, rows, route):
    half = rows.shape[1]
    out[:, :half] = rows
    place = (column_of(route) + 1).astype(F32).astype(BF16)
    out[:, half:] = jnp.broadcast_to(place, (rows.shape[0], LANES))


def top_rows(rows, period):
    return lax.rem(lax.broadcasted_iota(jnp.int32, (rows, 1), 0), period) < period // 2


def pick(activity, route_column):
    rows, half = route_column.shape[0], activity.shape[1] // 2
    tokens = activity.shape[0]
    hit = route_column == lax.broadcasted_iota(jnp.int32, (rows, tokens), 1)
    top = top_rows(rows, rows)
    left = jnp.where(hit & top, 1.0, 0.0).astype(BF16)
    right = jnp.where(hit & jnp.logical_not(top), 1.0, 0.0).astype(BF16)
    return dot(left, activity[:, :half]) + dot(right, activity[:, half:])


def put(activity, rows, route_row):
    tokens, half = activity.shape[0], activity.shape[1] // 2
    count = route_row.shape[1]
    hit = route_row == lax.broadcasted_iota(jnp.int32, (tokens, count), 0)
    first = lax.broadcasted_iota(jnp.int32, (tokens, count), 1) < count // 2
    left = jnp.where(hit & first, 1.0, 0.0)
    right = jnp.where(hit & jnp.logical_not(first), 1.0, 0.0)
    taken = jnp.sum(left, axis=1, keepdims=True) > 0.5
    new_left = jnp.where(taken, dot(left.astype(BF16), rows), activity[:, :half].astype(F32))
    new_right = jnp.where(taken, dot(right.astype(BF16), rows), activity[:, half:].astype(F32))
    return new_left.astype(BF16), new_right.astype(BF16)


def by_half(vector, rows):
    half = vector.shape[1] // 2
    return jnp.where(top_rows(rows, rows), vector[:, :half], vector[:, half:])


def inverse_rms(rows):
    width = 2 * rows.shape[1]
    mean = halves(jnp.sum(rows * rows, axis=1, keepdims=True)) / width
    return lax.rsqrt(mean + EPS)


def normalize(rows, gain, router):
    normed = (rows * inverse_rms(rows) * by_half(gain, rows.shape[0])).astype(BF16)
    logit = jnp.sum(normed.astype(F32) * by_half(router, rows.shape[0]), axis=1, keepdims=True)
    return normed, jax.nn.sigmoid(halves(logit))


def stack_blocks(refs, place, out):
    blocks = [ref[(j, *place)].astype(F32) for ref in refs for j in range(ref.shape[0])]
    out[...] = jnp.concatenate(blocks, axis=0).astype(BF16)


def join_halves(left, right, period):
    rows = left.shape[0]
    top = top_rows(rows, period)
    return jnp.where(
        top,
        left + pltpu.roll(right, rows - period // 2, 0),
        right + pltpu.roll(left, period // 2, 0),
    )


def first_forward_kernel(flags, act, routes, gain, router, normed_out, rows_out, gate_out, where_out):
    rows = pick(act[...], column_of(routes[0, 0, 0:1]))
    normed, gate = normalize(rows, gain[...], router[...])
    rows_out[...] = rows.astype(BF16)
    normed_out[...] = normed
    gate_out[...] = jnp.broadcast_to(gate, gate_out.shape)
    line = lax.broadcasted_iota(jnp.int32, where_out.shape, 0)
    where_out[...] = jnp.where(line == 0, flags[0], jnp.where(line == 1, flags[1], flags[2]))


def first_backward_kernel(act, stash, routes, gain, first_out, later_out, rows_out, saved_out):
    ticks = stash.shape[0]
    upstream = pick(act[...], column_of(routes[0, 0, 1:2])).astype(BF16)
    rows_out[...] = upstream
    first_out[1] = upstream
    for k in range(ticks):
        rows = pick(stash[k], column_of(routes[0, k, 1:2]))
        saved_out[k] = rows.astype(BF16)
        count = rows.shape[0]
        normed = (rows * inverse_rms(rows) * by_half(gain[...], count)).astype(BF16)
        if k == 0:
            first_out[0] = normed
        else:
            later_out[k - 1] = normed


def source_kernel(tick, way, place, moved, fresh, routes, source_out, rows_out):
    source = jnp.where(place[way : way + 1, :1] == 1, fresh[tick - 1], moved[...])
    source_out[...] = source
    rows_out[...] = pick(source, column_of(routes[0, tick, way : way + 1])).astype(BF16)


def select(base, packet, route, at_end):
    moved, behind_row = arrived(packet, at_end)
    column = column_of(route)
    rows = column.shape[0]
    hit = column == behind_row
    same = top_rows(rows, rows) == (lax.broadcasted_iota(jnp.int32, (rows, rows), 1) < rows // 2)
    match = jnp.where(hit & same, 1.0, 0.0)
    found = jnp.max(match, axis=1, keepdims=True) > 0.5
    return jnp.where(found, dot(match.astype(BF16), moved), base.astype(F32))


def next_forward_kernel(
    tick, base, moved, place, later, routes, gain, router, normed_out, rows_out, gate_out
):
    rows = select(base[...], moved[...], routes[0, tick, 0:1], place[0:1, :1])
    normed, gate = normalize(rows, gain[...], router[...])
    rows_out[...] = rows.astype(BF16)
    normed_out[0] = normed
    normed_out[1] = later[tick - 1]
    gate_out[...] = jnp.broadcast_to(gate, gate_out.shape)


def next_backward_kernel(tick, base, moved, place, routes, rows_out):
    rows = select(base[...], moved[...], routes[0, tick, 1:2], place[1:2, :1])
    rows_out[...] = rows.astype(BF16)


def land_kernel(way, source, moved, place, out):
    half = source.shape[1] // 2
    rows, places = arrived(moved[...], place[way : way + 1, :1])
    left, right = put(source[...], rows, places)
    out[:, :half] = left
    out[:, half:] = right


def output_kernel(token, act, moved, *outs):
    done, out = outs[-2:]
    done[...] = jnp.zeros_like(done)
    half = act.shape[1] // 2
    rows, places = arrived(moved[...])
    left, right = put(act[...], rows, places)
    out[0, 0, :, :half] = left
    out[0, 0, :, half:] = right


def stack_kernel(*refs):
    for j, ref in enumerate(refs[:-1]):
        refs[-1][j] = ref[...]


def forward_kernel(place, near, far, up, down, cross_out, own_out, rows, total):
    period, half = near.shape[-2:]
    hidden_count = up.shape[1]
    chunk = min(CHUNK, hidden_count)
    stack_blocks([near, far], place, rows)
    x = rows[...]
    top = top_rows(x.shape[0], period)
    for low in range(0, hidden_count, chunk):
        n = slice(low, low + chunk)
        u = join_halves(dot(x, up[:half, n]), dot(x, up[half:, n]), period)
        hidden = u * jax.nn.sigmoid(u)
        left = jnp.where(top, hidden, 0.0).astype(BF16)
        right = jnp.where(top, 0.0, hidden).astype(BF16)
        part = dot(left, down[n, :half]) + dot(right, down[n, half:])
        total[...] = part if low == 0 else total[...] + part
    write_blocks(total, own_out, cross_out)


def write_blocks(total, own_out, cross_out):
    chips, period, _ = own_out.shape
    for j in range(chips):
        own_out[j] = total[j * period : (j + 1) * period, :]
        low = (chips + j) * period
        cross_out[j] = total[low : low + period, :].astype(BF16)


def backward_kernel(
    normed_place,
    grad_place,
    near_n,
    far_n,
    near_g,
    far_g,
    up,
    down,
    router,
    *refs,
):
    term_in = refs[:-6]
    cross_out, own_out, term_out, x_n, x_g, total = refs[-6:]
    period, half = own_out.shape[1:]
    all_rows = x_n.shape[0]
    hidden_count = up.shape[1]
    chunk = min(CHUNK, hidden_count)
    top = top_rows(all_rows, period)
    stack_blocks([near_n, far_n], normed_place, x_n)
    stack_blocks([near_g, far_g], grad_place, x_g)
    x = x_n[...]
    g = x_g[...]
    vector = jnp.where(top, router[:, :half], router[:, half:])
    logit = jnp.sum(x.astype(F32) * vector, axis=1, keepdims=True)
    wide = jnp.broadcast_to(logit, (all_rows, 128))
    gate = jax.nn.sigmoid(join_halves(wide, wide, period))
    inner = jnp.zeros((all_rows, 1), F32)
    for low in range(0, hidden_count, chunk):
        n = slice(low, low + chunk)
        u = join_halves(dot(x, up[:half, n]), dot(x, up[half:, n]), period)
        grad_hidden = join_halves(
            dot(g, down[n, :half], NT), dot(g, down[n, half:], NT), period
        )
        grad_hidden = grad_hidden * gate[:, :1]
        sig = jax.nn.sigmoid(u)
        hidden = (u * sig).astype(BF16).astype(F32)
        inner = inner + jnp.sum(grad_hidden * hidden, axis=1, keepdims=True)
        grad_up = grad_hidden * sig * (1.0 + u * (1.0 - sig))
        left = jnp.where(top, grad_up, 0.0).astype(BF16)
        right = jnp.where(top, 0.0, grad_up).astype(BF16)
        part = dot(left, up[:half, n], NT) + dot(right, up[half:, n], NT)
        total[...] = part if low == 0 else total[...] + part

    logit = inner * (1.0 - gate)
    total[...] += logit[:, :1] * vector
    write_blocks(total, own_out, cross_out)
    rest = logit.T[:1]
    first = lax.rem(lax.broadcasted_iota(jnp.int32, (1, all_rows), 1), period) < period // 2
    pieces = []
    for _ in range(3):
        piece = rest.astype(BF16).astype(F32)
        pieces.append(piece)
        rest = rest - piece
    sums = []
    for side in (first, jnp.logical_not(first)):
        stacked = jnp.concatenate(
            [jnp.where(side, p, 0.0) for p in pieces] + [jnp.zeros((5, all_rows), F32)], axis=0
        )
        sums.append(jnp.sum(dot(stacked.astype(BF16), x), axis=0, keepdims=True))
    term = jnp.concatenate(sums, axis=0)
    for before in term_in:
        term = term + before[...]
    term_out[...] = term


def pair_kernel(own, crossed, *outs):
    for j, out in enumerate(outs):
        out[...] = (own[j] + crossed[j].astype(F32)).astype(out.dtype)


def added(terms):
    total = terms[0][...]
    for term in terms[1:]:
        total = total + term[...].astype(F32)
    return total


def forward_end_kernel(tick, rows, gate, routes, *refs):
    block = added(refs[:-1])
    renewed = (rows[...].astype(F32) + gate[:, :1] * block).astype(BF16)
    send_off(refs[-1], renewed, routes[0, tick, 0:1])


def backward_end_kernel(tick, upstream, saved, gain, routes, *refs):
    grad_normed = added(refs[:-1])
    picked = saved[tick].astype(F32)
    inv_rms = inverse_rms(picked)
    scaled_grad = grad_normed * by_half(gain[...], picked.shape[0])
    unit = picked * inv_rms
    mean = halves(jnp.sum(scaled_grad * unit, axis=1, keepdims=True)) / (2 * picked.shape[1])
    grad_rows = inv_rms * (scaled_grad - unit * mean)
    renewed = (upstream[...].astype(F32) + grad_rows).astype(BF16)
    send_off(refs[-1], renewed, routes[0, tick, 1:2])


def term_pair_kernel(near, far, out):
    out[...] = near[...] + far[...]


def term_end_kernel(scale, place, *refs):
    out = refs[-1]
    chips = len(refs) - 1
    chip = place[2:3, :1]
    total = jnp.zeros(refs[0].shape, F32)
    for low in range(chips):
        for j in range(chips):
            total = total + jnp.where(lax.rem(chip - j + chips, chips) == low, refs[j][...], 0.0)
    half = refs[0].shape[1]
    out[:, :half] = total[0:1] * scale
    out[:, half:] = total[1:2] * scale


class Order:
    def __init__(self):
        self.token = []

    def __call__(
        self, kernel, outs, *operands, smem=0, limit=8, scratch=(), cost=None, through=None
    ):
        count = len(self.token)
        passed = 0 if through is None else 1

        def body(*refs):
            kernel(*refs[count + passed : len(refs) - passed])

        in_specs = [ANY] * (count + passed)
        out_specs = jax.tree.map(lambda _: VMEM, outs)
        aliases = {}
        if passed:
            out_specs[-1] = ANY
            aliases = {count: len(outs) - 1}
            operands = (through, *operands)
        result = pl.pallas_call(
            body,
            out_shape=outs,
            in_specs=in_specs + [SMEM] * smem + [VMEM] * (len(operands) - smem - passed),
            out_specs=out_specs,
            input_output_aliases=aliases,
            scratch_shapes=scratch,
            compiler_params=pltpu.CompilerParams(vmem_limit_bytes=limit * 2**20),
            cost_estimate=cost or SMALL,
        )(*self.token, *operands)
        several = isinstance(result, (list, tuple))
        self.token = [result[-1 - passed] if several else result]
        return result

    def write(self, result, tick, ticks, act, moved):
        before = [] if result is None else [result]
        tokens, width = act.shape
        token, result = pl.pallas_call(
            output_kernel,
            grid=(1,),
            out_shape=[shaped((8, LANES), F32), shaped((1, ticks, tokens, width))],
            in_specs=[ANY, whole(act.shape), whole(moved.shape)] + [ANY] * len(before),
            out_specs=[
                whole((8, LANES)),
                pl.BlockSpec((1, 1, tokens, width), lambda i: (0, tick, 0, 0)),
            ],
            input_output_aliases={3: 1} if before else {},
            compiler_params=pltpu.CompilerParams(vmem_limit_bytes=8 * 2**20),
            cost_estimate=SMALL,
        )(*self.token, act, moved, *before)
        self.token = [token]
        return result


def shaped(shape, dtype=BF16):
    return jax.ShapeDtypeStruct(tuple(shape), dtype)


def whole(shape):
    return pl.BlockSpec(tuple(shape), lambda i: (0,) * len(shape))


def cost_of(matmuls, rows, weight):
    size = weight.shape[0] * weight.shape[1]
    return pl.CostEstimate(
        flops=4 * matmuls * rows * size,
        bytes_accessed=4 * size,
        transcendentals=rows * weight.shape[1],
    )


def per_device(
    arrive, entering, stash, back_arrive, head_grad, norm_gain, router, w_up, w_down, routes
):
    section = lax.axis_index("section")
    last = lax.axis_size("section") - 1
    dp_count = lax.axis_size("dp")
    chips = dp_count // CORES
    up, down = w_up[0], w_down[0]
    slots = routes.shape[3]
    tokens, width = arrive.shape[1:]
    half = width // 2
    ticks = stash.shape[1]
    period = 2 * slots
    flags = jnp.stack(
        [
            (section == 0).astype(jnp.int32),
            (section == last).astype(jnp.int32),
            lax.axis_index("dp") // CORES,
        ]
    )

    packed = shaped((period, half))
    packed_sum = shaped((period, half), F32)
    packet = shaped((period, half + LANES))
    full = shaped((tokens, width))
    gate_shape = shaped((period, LANES), F32)
    part_outs = [shaped((chips, period, half)), shaped((chips, period, half), F32)]
    all_rows = dp_count * period
    scratch_rows = pltpu.VMEM((all_rows, half), BF16)
    scratch_total = pltpu.VMEM((all_rows, half), F32)
    run = Order()

    def stacked(blocks):
        return run(stack_kernel, shaped((len(blocks), *blocks[0].shape)), *blocks)

    def pair(own, crossed):
        outs = [packed_sum] + [packed] * (chips - 1)
        return collect(run(pair_kernel, outs, own, crossed))

    forward_in, backward_in = arrive[0], back_arrive[0]
    forward_normed, forward_rows, gate, place = run(
        first_forward_kernel,
        [packed, packed, gate_shape, shaped((8, LANES), jnp.int32)],
        flags,
        forward_in,
        routes,
        norm_gain,
        router,
        smem=1,
    )
    forward_blocks = spread(forward_normed)
    saved_first, saved_later, backward_rows, saved = run(
        first_backward_kernel,
        [
            shaped((2, period, half)),
            shaped((ticks - 1, period, half)),
            packed,
            shaped((ticks, period, half)),
        ],
        backward_in,
        stash[0],
        routes,
        norm_gain,
        limit=16,
    )
    backward_blocks = spread(saved_first)
    term = []
    forward_out = backward_out = None
    forward_base = shift_section(forward_in, 1)
    backward_base = shift_section(backward_in, -1)
    near_f = stacked(forward_blocks)
    far_f = swap_core(near_f)

    for k in range(ticks):
        more = k + 1 < ticks
        if k > 0:
            forward_in = run(
                functools.partial(land_kernel, 0), full, forward_in, forward_moved, place
            )
            if more:
                forward_base = shift_section(forward_in, 1)
        cross, own = run(
            functools.partial(forward_kernel, (0,) if k else ()),
            part_outs,
            near_f,
            far_f,
            up,
            down,
            limit=WEIGHTS_LIMIT,
            scratch=[scratch_rows, scratch_total],
            cost=cost_of(2, all_rows, up),
        )
        crossed = swap_core(cross)
        near_b = stacked(backward_blocks)
        far_b = swap_core(near_b)
        terms = pair(own, crossed)
        if k > 0:
            backward_in = run(
                functools.partial(land_kernel, 1), full, backward_in, backward_moved, place
            )
            if more:
                backward_base = shift_section(backward_in, -1)

        near_n, far_n, normed_place = (near_f, far_f, (1,)) if k else (near_b, far_b, (0,))
        cross, own, part = run(
            functools.partial(backward_kernel, normed_place, () if k else (1,)),
            part_outs + [shaped((2, half), F32)],
            near_n,
            far_n,
            near_b,
            far_b,
            up,
            down,
            router,
            *term,
            limit=WEIGHTS_LIMIT,
            scratch=[scratch_rows, scratch_rows, scratch_total],
            cost=cost_of(3, all_rows, up),
        )
        term = [part]
        forward_new, cross = run(
            functools.partial(forward_end_kernel, k),
            [packet, shaped(cross.shape)],
            forward_rows,
            gate,
            routes,
            *terms,
            through=cross,
        )
        crossed = swap_core(cross)
        if more:
            forward_moved = shift_section(forward_new, 1)
            forward_next, forward_picked = run(
                functools.partial(source_kernel, k + 1, 0),
                [full, packed],
                place,
                forward_base,
                entering,
                routes,
            )
        else:
            total = run(term_pair_kernel, shaped((2, half), F32), part, swap_core(part))
        terms = pair(own, crossed)

        if more:
            backward_next, backward_picked = run(
                functools.partial(source_kernel, k + 1, 1),
                [full, packed],
                place,
                backward_base,
                head_grad,
                routes,
            )
            forward_normed, forward_rows, gate = run(
                functools.partial(next_forward_kernel, k + 1),
                [shaped((2, period, half)), packed, gate_shape],
                forward_picked,
                forward_moved,
                place,
                saved_later,
                routes,
                norm_gain,
                router,
            )
            forward_blocks = spread(forward_normed)
        else:
            total_blocks = spread(total)
        forward_out = run.write(forward_out, k, ticks, forward_in, forward_new)

        backward_new = run(
            functools.partial(backward_end_kernel, k),
            packet,
            backward_rows,
            saved,
            norm_gain,
            routes,
            *terms,
        )
        if more:
            backward_moved = shift_section(backward_new, -1)
            backward_rows = run(
                functools.partial(next_backward_kernel, k + 1),
                packed,
                backward_picked,
                backward_moved,
                place,
                routes,
            )
            backward_blocks = spread(backward_rows)
            near_f = stacked(forward_blocks)
            far_f = swap_core(near_f)
        backward_out = run.write(backward_out, k, ticks, backward_in, backward_new)
        if more:
            forward_in, backward_in = forward_next, backward_next

    scale = 1.0 / float(ticks * slots * dp_count)
    router_grad = run(
        functools.partial(term_end_kernel, scale), shaped((1, width), F32), place, *total_blocks
    )
    return forward_out, backward_out, router_grad


def solution(mesh):
    in_specs = (
        P("section", "dp", None),
        P(None, "dp", None),
        P("section", None, "dp", None),
        P("section", "dp", None),
        P(None, "dp", None),
        P("section", None),
        P("section", None),
        P("section", None, "dp"),
        P("section", "dp", None),
        P("section", None, None, "dp"),
    )
    out_specs = (P("section", None, "dp", None), P("section", None, "dp", None), P("section", None))
    return jax.shard_map(
        per_device, mesh=mesh, in_specs=in_specs, out_specs=out_specs, check_vma=False
    )
```

```python
import functools

import jax
import jax.numpy as jnp
from jax import lax
from jax.experimental import pallas as pl
from jax.experimental.pallas import tpu as pltpu
from jax.sharding import PartitionSpec as P

EPS = 1e-05
CORES = 2
CHUNK = 256
LANES = 128
WEIGHTS_LIMIT = 26
BF16 = jnp.bfloat16
F32 = jnp.float32
NN = (((1,), (0,)), ((), ()))
NT = (((1,), (1,)), ((), ()))
VMEM = pl.BlockSpec(memory_space=pltpu.VMEM)
SMEM = pl.BlockSpec(memory_space=pltpu.SMEM)
ANY = pl.BlockSpec(memory_space=pl.ANY)
SMALL = pl.CostEstimate(flops=0, bytes_accessed=2 * 2**20, transcendentals=0)


def shift_section(block, step):
    count = lax.axis_size("section")
    return lax.ppermute(block, "section", [(i, (i + step) % count) for i in range(count)])


def swap_core(block):
    count = lax.axis_size("dp")
    return lax.ppermute(block, "dp", [(i, i ^ 1) for i in range(count)])


def in_pairs(chips):
    return chips & (chips - 1) == 0


def swap_chip(block, j, way):
    count = lax.axis_size("dp")
    chips = count // CORES
    route = []
    for chip in range(chips):
        target = chip ^ j if in_pairs(chips) else (chip + way * j) % chips
        route += [(chip * CORES + core, target * CORES + core) for core in range(CORES)]
    return lax.ppermute(block, "dp", route)


def spread(block):
    return [block] + [swap_chip(block, j, 1) for j in range(1, lax.axis_size("dp") // CORES)]


def collect(blocks):
    return [blocks[0]] + [swap_chip(b, j, -1) for j, b in enumerate(blocks) if j > 0]


def dot(a, b, dims=NN):
    return lax.dot_general(a, b, dims, preferred_element_type=F32)


def halves(column):
    rows = column.shape[0]
    wide = jnp.broadcast_to(column, (rows, 128))
    return (wide + pltpu.roll(wide, rows // 2, 0))[:, :1]


def column_of(route):
    slots = route.shape[1]
    row = lax.rem(lax.broadcasted_iota(jnp.int32, (2 * slots, slots), 0), slots)
    same = row == lax.broadcasted_iota(jnp.int32, (2 * slots, slots), 1)
    return jnp.sum(jnp.where(same, route, 0), axis=1, keepdims=True)


def row_of(column):
    count = column.shape[0]
    shape = (count, count)
    same = lax.broadcasted_iota(jnp.int32, shape, 0) == lax.broadcasted_iota(jnp.int32, shape, 1)
    return jnp.sum(jnp.where(same, column, 0), axis=0, keepdims=True)


def arrived(moved, at_end=None):
    half = moved.shape[1] - LANES
    place = row_of(moved[:, half : half + 1].astype(F32).astype(jnp.int32)) - 1
    none = place < 0
    if at_end is not None:
        none = none | (at_end == 1)
    return moved[:, :half], jnp.where(none, -2, place)


def send_off(out, rows, route):
    half = rows.shape[1]
    out[:, :half] = rows
    place = (column_of(route) + 1).astype(F32).astype(BF16)
    out[:, half:] = jnp.broadcast_to(place, (rows.shape[0], LANES))


def top_rows(rows, period):
    return lax.rem(lax.broadcasted_iota(jnp.int32, (rows, 1), 0), period) < period // 2


def pick(activity, route_column):
    rows, half = route_column.shape[0], activity.shape[1] // 2
    tokens = activity.shape[0]
    hit = route_column == lax.broadcasted_iota(jnp.int32, (rows, tokens), 1)
    top = top_rows(rows, rows)
    left = jnp.where(hit & top, 1.0, 0.0).astype(BF16)
    right = jnp.where(hit & jnp.logical_not(top), 1.0, 0.0).astype(BF16)
    return dot(left, activity[:, :half]) + dot(right, activity[:, half:])


def put(activity, rows, route_row):
    tokens, half = activity.shape[0], activity.shape[1] // 2
    count = route_row.shape[1]
    hit = route_row == lax.broadcasted_iota(jnp.int32, (tokens, count), 0)
    first = lax.broadcasted_iota(jnp.int32, (tokens, count), 1) < count // 2
    left = jnp.where(hit & first, 1.0, 0.0)
    right = jnp.where(hit & jnp.logical_not(first), 1.0, 0.0)
    taken = jnp.sum(left, axis=1, keepdims=True) > 0.5
    new_left = jnp.where(taken, dot(left.astype(BF16), rows), activity[:, :half].astype(F32))
    new_right = jnp.where(taken, dot(right.astype(BF16), rows), activity[:, half:].astype(F32))
    return new_left.astype(BF16), new_right.astype(BF16)


def by_half(vector, rows):
    half = vector.shape[1] // 2
    return jnp.where(top_rows(rows, rows), vector[:, :half], vector[:, half:])


def inverse_rms(rows):
    width = 2 * rows.shape[1]
    mean = halves(jnp.sum(rows * rows, axis=1, keepdims=True)) / width
    return lax.rsqrt(mean + EPS)


def normalize(rows, gain, router):
    normed = (rows * inverse_rms(rows) * by_half(gain, rows.shape[0])).astype(BF16)
    logit = jnp.sum(normed.astype(F32) * by_half(router, rows.shape[0]), axis=1, keepdims=True)
    return normed, jax.nn.sigmoid(halves(logit))


def stack_blocks(refs, place, out):
    blocks = [ref[(j, *place)].astype(F32) for ref in refs for j in range(ref.shape[0])]
    out[...] = jnp.concatenate(blocks, axis=0).astype(BF16)


def join_halves(left, right, period):
    rows = left.shape[0]
    top = top_rows(rows, period)
    return jnp.where(
        top,
        left + pltpu.roll(right, rows - period // 2, 0),
        right + pltpu.roll(left, period // 2, 0),
    )


def first_forward_kernel(flags, act, routes, gain, router, normed_out, rows_out, gate_out, where_out):
    rows = pick(act[...], column_of(routes[0, 0, 0:1]))
    normed, gate = normalize(rows, gain[...], router[...])
    rows_out[...] = rows.astype(BF16)
    normed_out[...] = normed
    gate_out[...] = jnp.broadcast_to(gate, gate_out.shape)
    line = lax.broadcasted_iota(jnp.int32, where_out.shape, 0)
    where_out[...] = jnp.where(line == 0, flags[0], jnp.where(line == 1, flags[1], flags[2]))


def first_backward_kernel(act, stash, routes, gain, first_out, rows_out, saved_out):
    ticks = stash.shape[0]
    upstream = pick(act[...], column_of(routes[0, 0, 1:2])).astype(BF16)
    rows_out[...] = upstream
    first_out[1] = upstream
    for k in range(ticks):
        rows = pick(stash[k], column_of(routes[0, k, 1:2]))
        saved_out[k] = rows.astype(BF16)
        count = rows.shape[0]
        normed = (rows * inverse_rms(rows) * by_half(gain[...], count)).astype(BF16)
        first_out[k if k == 0 else k + 1] = normed


def source_kernel(tick, way, place, moved, fresh, routes, source_out, rows_out):
    source = jnp.where(place[way : way + 1, :1] == 1, fresh[tick - 1], moved[...])
    source_out[...] = source
    rows_out[...] = pick(source, column_of(routes[0, tick, way : way + 1])).astype(BF16)


def select(base, packet, route, at_end):
    moved, behind_row = arrived(packet, at_end)
    column = column_of(route)
    rows = column.shape[0]
    hit = column == behind_row
    same = top_rows(rows, rows) == (lax.broadcasted_iota(jnp.int32, (rows, rows), 1) < rows // 2)
    match = jnp.where(hit & same, 1.0, 0.0)
    found = jnp.max(match, axis=1, keepdims=True) > 0.5
    return jnp.where(found, dot(match.astype(BF16), moved), base.astype(F32))


def next_forward_kernel(
    tick, base, moved, place, routes, gain, router, normed_out, rows_out, gate_out
):
    rows = select(base[...], moved[...], routes[0, tick, 0:1], place[0:1, :1])
    normed, gate = normalize(rows, gain[...], router[...])
    rows_out[...] = rows.astype(BF16)
    normed_out[...] = normed
    gate_out[...] = jnp.broadcast_to(gate, gate_out.shape)


def next_backward_kernel(tick, base, moved, place, routes, rows_out):
    rows = select(base[...], moved[...], routes[0, tick, 1:2], place[1:2, :1])
    rows_out[...] = rows.astype(BF16)


def land_kernel(way, source, moved, place, out):
    half = source.shape[1] // 2
    rows, places = arrived(moved[...], place[way : way + 1, :1])
    left, right = put(source[...], rows, places)
    out[:, :half] = left
    out[:, half:] = right


def output_kernel(token, act, moved, *outs):
    done, out = outs[-2:]
    done[...] = jnp.zeros_like(done)
    half = act.shape[1] // 2
    rows, places = arrived(moved[...])
    left, right = put(act[...], rows, places)
    out[0, 0, :, :half] = left
    out[0, 0, :, half:] = right


def stack_kernel(*refs):
    for j, ref in enumerate(refs[:-1]):
        refs[-1][j] = ref[...]


def stack_first_kernel(*refs):
    first, later = refs[-2:]
    for j, ref in enumerate(refs[:-2]):
        first[j] = ref[:2]
        later[j] = ref[2:]


def forward_kernel(near, far, up, down, cross_out, own_out, rows, total):
    period, half = near.shape[-2:]
    hidden_count = up.shape[1]
    chunk = min(CHUNK, hidden_count)
    stack_blocks([near, far], (), rows)
    x = rows[...]
    top = top_rows(x.shape[0], period)
    for low in range(0, hidden_count, chunk):
        n = slice(low, low + chunk)
        u = join_halves(dot(x, up[:half, n]), dot(x, up[half:, n]), period)
        hidden = u * jax.nn.sigmoid(u)
        left = jnp.where(top, hidden, 0.0).astype(BF16)
        right = jnp.where(top, 0.0, hidden).astype(BF16)
        part = dot(left, down[n, :half]) + dot(right, down[n, half:])
        total[...] = part if low == 0 else total[...] + part
    write_blocks(total, own_out, cross_out)


def write_blocks(total, own_out, cross_out):
    chips, period, _ = own_out.shape
    for j in range(chips):
        own_out[j] = total[j * period : (j + 1) * period, :]
        low = (chips + j) * period
        cross_out[j] = total[low : low + period, :].astype(BF16)


def backward_kernel(
    normed_place,
    grad_place,
    near_n,
    far_n,
    near_g,
    far_g,
    up,
    down,
    router,
    *refs,
):
    term_in = refs[:-6]
    cross_out, own_out, term_out, x_n, x_g, total = refs[-6:]
    period, half = own_out.shape[1:]
    all_rows = x_n.shape[0]
    hidden_count = up.shape[1]
    chunk = min(CHUNK, hidden_count)
    top = top_rows(all_rows, period)
    stack_blocks([near_n, far_n], normed_place, x_n)
    stack_blocks([near_g, far_g], grad_place, x_g)
    x = x_n[...]
    g = x_g[...]
    vector = jnp.where(top, router[:, :half], router[:, half:])
    logit = jnp.sum(x.astype(F32) * vector, axis=1, keepdims=True)
    wide = jnp.broadcast_to(logit, (all_rows, 128))
    gate = jax.nn.sigmoid(join_halves(wide, wide, period))
    inner = jnp.zeros((all_rows, 1), F32)
    for low in range(0, hidden_count, chunk):
        n = slice(low, low + chunk)
        u = join_halves(dot(x, up[:half, n]), dot(x, up[half:, n]), period)
        grad_hidden = join_halves(
            dot(g, down[n, :half], NT), dot(g, down[n, half:], NT), period
        )
        grad_hidden = grad_hidden * gate[:, :1]
        sig = jax.nn.sigmoid(u)
        hidden = (u * sig).astype(BF16).astype(F32)
        inner = inner + jnp.sum(grad_hidden * hidden, axis=1, keepdims=True)
        grad_up = grad_hidden * sig * (1.0 + u * (1.0 - sig))
        left = jnp.where(top, grad_up, 0.0).astype(BF16)
        right = jnp.where(top, 0.0, grad_up).astype(BF16)
        part = dot(left, up[:half, n], NT) + dot(right, up[half:, n], NT)
        total[...] = part if low == 0 else total[...] + part

    logit = inner * (1.0 - gate)
    total[...] += logit[:, :1] * vector
    write_blocks(total, own_out, cross_out)
    rest = logit.T[:1]
    first = lax.rem(lax.broadcasted_iota(jnp.int32, (1, all_rows), 1), period) < period // 2
    pieces = []
    for _ in range(3):
        piece = rest.astype(BF16).astype(F32)
        pieces.append(piece)
        rest = rest - piece
    sums = []
    for side in (first, jnp.logical_not(first)):
        stacked = jnp.concatenate(
            [jnp.where(side, p, 0.0) for p in pieces] + [jnp.zeros((5, all_rows), F32)], axis=0
        )
        sums.append(jnp.sum(dot(stacked.astype(BF16), x), axis=0, keepdims=True))
    term = jnp.concatenate(sums, axis=0)
    for before in term_in:
        term = term + before[...]
    term_out[...] = term


def pair_kernel(own, crossed, *outs):
    for j, out in enumerate(outs):
        out[...] = (own[j] + crossed[j].astype(F32)).astype(out.dtype)


def added(terms):
    total = terms[0][...]
    for term in terms[1:]:
        total = total + term[...].astype(F32)
    return total


def forward_end_kernel(tick, rows, gate, routes, *refs):
    block = added(refs[:-1])
    renewed = (rows[...].astype(F32) + gate[:, :1] * block).astype(BF16)
    send_off(refs[-1], renewed, routes[0, tick, 0:1])


def backward_end_kernel(tick, upstream, saved, gain, routes, *refs):
    grad_normed = added(refs[:-1])
    picked = saved[tick].astype(F32)
    inv_rms = inverse_rms(picked)
    scaled_grad = grad_normed * by_half(gain[...], picked.shape[0])
    unit = picked * inv_rms
    mean = halves(jnp.sum(scaled_grad * unit, axis=1, keepdims=True)) / (2 * picked.shape[1])
    grad_rows = inv_rms * (scaled_grad - unit * mean)
    renewed = (upstream[...].astype(F32) + grad_rows).astype(BF16)
    send_off(refs[-1], renewed, routes[0, tick, 1:2])


def term_pair_kernel(near, far, out):
    out[...] = near[...] + far[...]


def term_end_kernel(scale, place, *refs):
    out = refs[-1]
    chips = len(refs) - 1
    chip = place[2:3, :1]
    total = jnp.zeros(refs[0].shape, F32)
    for low in range(chips):
        for j in range(chips):
            source = chip ^ j if in_pairs(chips) else lax.rem(chip - j + chips, chips)
            total = total + jnp.where(source == low, refs[j][...], 0.0)
    half = refs[0].shape[1]
    out[:, :half] = total[0:1] * scale
    out[:, half:] = total[1:2] * scale


class Order:
    def __init__(self):
        self.token = []

    def __call__(
        self, kernel, outs, *operands, smem=0, limit=8, scratch=(), cost=None, through=None
    ):
        count = len(self.token)
        passed = 0 if through is None else 1

        def body(*refs):
            kernel(*refs[count + passed : len(refs) - passed])

        in_specs = [ANY] * (count + passed)
        out_specs = jax.tree.map(lambda _: VMEM, outs)
        aliases = {}
        if passed:
            out_specs[-1] = ANY
            aliases = {count: len(outs) - 1}
            operands = (through, *operands)
        result = pl.pallas_call(
            body,
            out_shape=outs,
            in_specs=in_specs + [SMEM] * smem + [VMEM] * (len(operands) - smem - passed),
            out_specs=out_specs,
            input_output_aliases=aliases,
            scratch_shapes=scratch,
            compiler_params=pltpu.CompilerParams(vmem_limit_bytes=limit * 2**20),
            cost_estimate=cost or SMALL,
        )(*self.token, *operands)
        several = isinstance(result, (list, tuple))
        self.token = [result[-1 - passed] if several else result]
        return result

    def write(self, result, tick, ticks, act, moved):
        before = [] if result is None else [result]
        tokens, width = act.shape
        token, result = pl.pallas_call(
            output_kernel,
            grid=(1,),
            out_shape=[shaped((8, LANES), F32), shaped((1, ticks, tokens, width))],
            in_specs=[ANY, whole(act.shape), whole(moved.shape)] + [ANY] * len(before),
            out_specs=[
                whole((8, LANES)),
                pl.BlockSpec((1, 1, tokens, width), lambda i: (0, tick, 0, 0)),
            ],
            input_output_aliases={3: 1} if before else {},
            compiler_params=pltpu.CompilerParams(vmem_limit_bytes=8 * 2**20),
            cost_estimate=SMALL,
        )(*self.token, act, moved, *before)
        self.token = [token]
        return result


def shaped(shape, dtype=BF16):
    return jax.ShapeDtypeStruct(tuple(shape), dtype)


def whole(shape):
    return pl.BlockSpec(tuple(shape), lambda i: (0,) * len(shape))


def cost_of(matmuls, rows, weight):
    size = weight.shape[0] * weight.shape[1]
    return pl.CostEstimate(
        flops=4 * matmuls * rows * size,
        bytes_accessed=4 * size,
        transcendentals=rows * weight.shape[1],
    )


def per_device(
    arrive, entering, stash, back_arrive, head_grad, norm_gain, router, w_up, w_down, routes
):
    section = lax.axis_index("section")
    last = lax.axis_size("section") - 1
    dp_count = lax.axis_size("dp")
    chips = dp_count // CORES
    up, down = w_up[0], w_down[0]
    slots = routes.shape[3]
    tokens, width = arrive.shape[1:]
    half = width // 2
    ticks = stash.shape[1]
    period = 2 * slots
    flags = jnp.stack(
        [
            (section == 0).astype(jnp.int32),
            (section == last).astype(jnp.int32),
            lax.axis_index("dp") // CORES,
        ]
    )

    packed = shaped((period, half))
    packed_sum = shaped((period, half), F32)
    packet = shaped((period, half + LANES))
    full = shaped((tokens, width))
    gate_shape = shaped((period, LANES), F32)
    part_outs = [shaped((chips, period, half)), shaped((chips, period, half), F32)]
    all_rows = dp_count * period
    scratch_rows = pltpu.VMEM((all_rows, half), BF16)
    scratch_total = pltpu.VMEM((all_rows, half), F32)
    run = Order()

    def stacked(blocks):
        return run(stack_kernel, shaped((len(blocks), *blocks[0].shape)), *blocks)

    def pair(own, crossed):
        outs = [packed_sum] + [packed] * (chips - 1)
        return collect(run(pair_kernel, outs, own, crossed))

    forward_in, backward_in = arrive[0], back_arrive[0]
    forward_normed, forward_rows, gate, place = run(
        first_forward_kernel,
        [packed, packed, gate_shape, shaped((8, LANES), jnp.int32)],
        flags,
        forward_in,
        routes,
        norm_gain,
        router,
        smem=1,
    )
    forward_blocks = spread(forward_normed)
    saved_first, backward_rows, saved = run(
        first_backward_kernel,
        [
            shaped((ticks + 1, period, half)),
            packed,
            shaped((ticks, period, half)),
        ],
        backward_in,
        stash[0],
        routes,
        norm_gain,
        limit=16,
    )
    backward_blocks = spread(saved_first)
    term = []
    forward_out = backward_out = None
    forward_base = shift_section(forward_in, 1)
    backward_base = shift_section(backward_in, -1)
    near_f = stacked(forward_blocks)
    far_f = swap_core(near_f)

    for k in range(ticks):
        more = k + 1 < ticks
        if k > 0:
            backward_in = run(
                functools.partial(land_kernel, 1), full, backward_in, backward_moved, place
            )
            if more:
                backward_base = shift_section(backward_in, -1)
            forward_in = run(
                functools.partial(land_kernel, 0), full, forward_in, forward_moved, place
            )
            if more:
                forward_base = shift_section(forward_in, 1)
        cross, own = run(
            forward_kernel,
            part_outs,
            near_f,
            far_f,
            up,
            down,
            limit=WEIGHTS_LIMIT,
            scratch=[scratch_rows, scratch_total],
            cost=cost_of(2, all_rows, up),
        )
        crossed = swap_core(cross)
        if k == 0:
            terms = pair(own, crossed)
            near_b, near_n = run(
                stack_first_kernel,
                [shaped((chips, 2, period, half)), shaped((chips, ticks - 1, period, half))],
                *backward_blocks,
            )
            far_b, far_n = swap_core(near_b), swap_core(near_n)
            rows_n = (near_b, far_b)
        else:
            near_b = stacked(backward_blocks)
            far_b = swap_core(near_b)
            terms = pair(own, crossed)
            rows_n = (near_n, far_n)

        cross, own, part = run(
            functools.partial(backward_kernel, (max(k - 1, 0),), () if k else (1,)),
            part_outs + [shaped((2, half), F32)],
            *rows_n,
            near_b,
            far_b,
            up,
            down,
            router,
            *term,
            limit=WEIGHTS_LIMIT,
            scratch=[scratch_rows, scratch_rows, scratch_total],
            cost=cost_of(3, all_rows, up),
        )
        term = [part]
        forward_new, cross = run(
            functools.partial(forward_end_kernel, k),
            [packet, shaped(cross.shape)],
            forward_rows,
            gate,
            routes,
            *terms,
            through=cross,
        )
        crossed = swap_core(cross)
        if more:
            forward_moved = shift_section(forward_new, 1)
            forward_next, forward_picked = run(
                functools.partial(source_kernel, k + 1, 0),
                [full, packed],
                place,
                forward_base,
                entering,
                routes,
            )
        else:
            total = run(term_pair_kernel, shaped((2, half), F32), part, swap_core(part))
        terms = pair(own, crossed)

        if more:
            backward_next, backward_picked = run(
                functools.partial(source_kernel, k + 1, 1),
                [full, packed],
                place,
                backward_base,
                head_grad,
                routes,
            )
            forward_normed, forward_rows, gate = run(
                functools.partial(next_forward_kernel, k + 1),
                [packed, packed, gate_shape],
                forward_picked,
                forward_moved,
                place,
                routes,
                norm_gain,
                router,
            )
            forward_blocks = spread(forward_normed)
        else:
            total_blocks = spread(total)
        forward_out = run.write(forward_out, k, ticks, forward_in, forward_new)

        backward_new = run(
            functools.partial(backward_end_kernel, k),
            packet,
            backward_rows,
            saved,
            norm_gain,
            routes,
            *terms,
        )
        if more:
            backward_moved = shift_section(backward_new, -1)
            backward_rows = run(
                functools.partial(next_backward_kernel, k + 1),
                packed,
                backward_picked,
                backward_moved,
                place,
                routes,
            )
            backward_blocks = spread(backward_rows)
            near_f = stacked(forward_blocks)
            far_f = swap_core(near_f)
        backward_out = run.write(backward_out, k, ticks, backward_in, backward_new)
        if more:
            forward_in, backward_in = forward_next, backward_next

    scale = 1.0 / float(ticks * slots * dp_count)
    router_grad = run(
        functools.partial(term_end_kernel, scale), shaped((1, width), F32), place, *total_blocks
    )
    return forward_out, backward_out, router_grad


def solution(mesh):
    in_specs = (
        P("section", "dp", None),
        P(None, "dp", None),
        P("section", None, "dp", None),
        P("section", "dp", None),
        P(None, "dp", None),
        P("section", None),
        P("section", None),
        P("section", None, "dp"),
        P("section", "dp", None),
        P("section", None, None, "dp"),
    )
    out_specs = (P("section", None, "dp", None), P("section", None, "dp", None), P("section", None))
    return jax.shard_map(
        per_device, mesh=mesh, in_specs=in_specs, out_specs=out_specs, check_vma=False
    )
```

```python
import functools

import jax
import jax.numpy as jnp
from jax import lax
from jax.experimental import pallas as pl
from jax.experimental.pallas import tpu as pltpu
from jax.sharding import PartitionSpec as P

EPS = 1e-05
CORES = 2
CHUNK = 256
LANES = 128
WEIGHTS_LIMIT = 26
BF16 = jnp.bfloat16
F32 = jnp.float32
NN = (((1,), (0,)), ((), ()))
NT = (((1,), (1,)), ((), ()))
VMEM = pl.BlockSpec(memory_space=pltpu.VMEM)
SMEM = pl.BlockSpec(memory_space=pltpu.SMEM)
ANY = pl.BlockSpec(memory_space=pl.ANY)
SMALL = pl.CostEstimate(flops=0, bytes_accessed=2 * 2**20, transcendentals=0)


def shift_section(block, step):
    count = lax.axis_size("section")
    route = [(i, (i + step) % count) for i in range(count) if step > 0 or i + step >= 0]
    return lax.ppermute(block, "section", route)


def swap_core(block):
    count = lax.axis_size("dp")
    return lax.ppermute(block, "dp", [(i, i ^ 1) for i in range(count)])


def in_pairs(chips):
    return chips & (chips - 1) == 0


def swap_chip(block, j, way):
    count = lax.axis_size("dp")
    chips = count // CORES
    route = []
    for chip in range(chips):
        target = chip ^ j if in_pairs(chips) else (chip + way * j) % chips
        route += [(chip * CORES + core, target * CORES + core) for core in range(CORES)]
    return lax.ppermute(block, "dp", route)


def spread(block):
    return [block] + [swap_chip(block, j, 1) for j in range(1, lax.axis_size("dp") // CORES)]


def collect(blocks):
    return [blocks[0]] + [swap_chip(b, j, -1) for j, b in enumerate(blocks) if j > 0]


def dot(a, b, dims=NN):
    return lax.dot_general(a, b, dims, preferred_element_type=F32)


def halves(column):
    rows = column.shape[0]
    wide = jnp.broadcast_to(column, (rows, 128))
    return (wide + pltpu.roll(wide, rows // 2, 0))[:, :1]


def column_of(route):
    slots = route.shape[1]
    row = lax.rem(lax.broadcasted_iota(jnp.int32, (2 * slots, slots), 0), slots)
    same = row == lax.broadcasted_iota(jnp.int32, (2 * slots, slots), 1)
    return jnp.sum(jnp.where(same, route, 0), axis=1, keepdims=True)


def row_of(column):
    count = column.shape[0]
    shape = (count, count)
    same = lax.broadcasted_iota(jnp.int32, shape, 0) == lax.broadcasted_iota(jnp.int32, shape, 1)
    return jnp.sum(jnp.where(same, column, 0), axis=0, keepdims=True)


def arrived(moved, at_end=None):
    half = moved.shape[1] - LANES
    place = row_of(moved[:, half : half + 1].astype(F32).astype(jnp.int32)) - 1
    none = place < 0
    if at_end is not None:
        none = none | (at_end == 1)
    return moved[:, :half], jnp.where(none, -2, place)


def send_off(out, rows, route):
    half = rows.shape[1]
    out[:, :half] = rows
    place = (column_of(route) + 1).astype(F32).astype(BF16)
    out[:, half:] = jnp.broadcast_to(place, (rows.shape[0], LANES))


def top_rows(rows, period):
    return lax.rem(lax.broadcasted_iota(jnp.int32, (rows, 1), 0), period) < period // 2


def pick(activity, route_column):
    rows, half = route_column.shape[0], activity.shape[1] // 2
    tokens = activity.shape[0]
    hit = route_column == lax.broadcasted_iota(jnp.int32, (rows, tokens), 1)
    top = top_rows(rows, rows)
    left = jnp.where(hit & top, 1.0, 0.0).astype(BF16)
    right = jnp.where(hit & jnp.logical_not(top), 1.0, 0.0).astype(BF16)
    return dot(left, activity[:, :half]) + dot(right, activity[:, half:])


def put(activity, rows, route_row):
    tokens, half = activity.shape[0], activity.shape[1] // 2
    count = route_row.shape[1]
    hit = route_row == lax.broadcasted_iota(jnp.int32, (tokens, count), 0)
    first = lax.broadcasted_iota(jnp.int32, (tokens, count), 1) < count // 2
    left = jnp.where(hit & first, 1.0, 0.0)
    right = jnp.where(hit & jnp.logical_not(first), 1.0, 0.0)
    taken = jnp.sum(left, axis=1, keepdims=True) > 0.5
    new_left = jnp.where(taken, dot(left.astype(BF16), rows), activity[:, :half].astype(F32))
    new_right = jnp.where(taken, dot(right.astype(BF16), rows), activity[:, half:].astype(F32))
    return new_left.astype(BF16), new_right.astype(BF16)


def by_half(vector, rows):
    half = vector.shape[1] // 2
    return jnp.where(top_rows(rows, rows), vector[:, :half], vector[:, half:])


def inverse_rms(rows):
    width = 2 * rows.shape[1]
    mean = halves(jnp.sum(rows * rows, axis=1, keepdims=True)) / width
    return lax.rsqrt(mean + EPS)


def normalize(rows, gain, router):
    normed = (rows * inverse_rms(rows) * by_half(gain, rows.shape[0])).astype(BF16)
    logit = jnp.sum(normed.astype(F32) * by_half(router, rows.shape[0]), axis=1, keepdims=True)
    return normed, jax.nn.sigmoid(halves(logit))


def stack_blocks(refs, place, out):
    blocks = [ref[(j, *place)].astype(F32) for ref in refs for j in range(ref.shape[0])]
    out[...] = jnp.concatenate(blocks, axis=0).astype(BF16)


def join_halves(left, right, period):
    rows = left.shape[0]
    top = top_rows(rows, period)
    return jnp.where(
        top,
        left + pltpu.roll(right, rows - period // 2, 0),
        right + pltpu.roll(left, period // 2, 0),
    )


def first_forward_kernel(flags, act, routes, gain, router, normed_out, rows_out, gate_out, where_out):
    rows = pick(act[...], column_of(routes[0, 0, 0:1]))
    normed, gate = normalize(rows, gain[...], router[...])
    rows_out[...] = rows.astype(BF16)
    normed_out[...] = normed
    gate_out[...] = jnp.broadcast_to(gate, gate_out.shape)
    line = lax.broadcasted_iota(jnp.int32, where_out.shape, 0)
    where_out[...] = jnp.where(line == 0, flags[0], jnp.where(line == 1, flags[1], flags[2]))


def first_backward_kernel(act, stash, routes, gain, first_out, later_out, rows_out, saved_out):
    ticks = stash.shape[0]
    upstream = pick(act[...], column_of(routes[0, 0, 1:2])).astype(BF16)
    rows_out[...] = upstream
    first_out[1] = upstream
    for k in range(ticks):
        rows = pick(stash[k], column_of(routes[0, k, 1:2]))
        saved_out[k] = rows.astype(BF16)
        count = rows.shape[0]
        normed = (rows * inverse_rms(rows) * by_half(gain[...], count)).astype(BF16)
        if k == 0:
            first_out[0] = normed
        else:
            later_out[k - 1] = normed


def source_kernel(tick, way, place, moved, fresh, routes, source_out, rows_out):
    source = jnp.where(place[way : way + 1, :1] == 1, fresh[tick - 1], moved[...])
    source_out[...] = source
    rows_out[...] = pick(source, column_of(routes[0, tick, way : way + 1])).astype(BF16)


def select(base, packet, route, at_end):
    moved, behind_row = arrived(packet, at_end)
    column = column_of(route)
    rows = column.shape[0]
    hit = column == behind_row
    same = top_rows(rows, rows) == (lax.broadcasted_iota(jnp.int32, (rows, rows), 1) < rows // 2)
    match = jnp.where(hit & same, 1.0, 0.0)
    found = jnp.max(match, axis=1, keepdims=True) > 0.5
    return jnp.where(found, dot(match.astype(BF16), moved), base.astype(F32))


def next_forward_kernel(
    tick, base, moved, place, routes, gain, router, normed_out, rows_out, gate_out
):
    rows = select(base[...], moved[...], routes[0, tick, 0:1], place[0:1, :1])
    normed, gate = normalize(rows, gain[...], router[...])
    rows_out[...] = rows.astype(BF16)
    normed_out[...] = normed
    gate_out[...] = jnp.broadcast_to(gate, gate_out.shape)


def next_backward_kernel(tick, base, moved, place, routes, rows_out):
    rows = select(base[...], moved[...], routes[0, tick, 1:2], place[1:2, :1])
    rows_out[...] = rows.astype(BF16)


def land_kernel(way, source, moved, place, out):
    half = source.shape[1] // 2
    rows, places = arrived(moved[...], place[way : way + 1, :1])
    left, right = put(source[...], rows, places)
    out[:, :half] = left
    out[:, half:] = right


def output_kernel(token, act, moved, *outs):
    done, out = outs[-2:]
    done[...] = jnp.zeros_like(done)
    half = act.shape[1] // 2
    rows, places = arrived(moved[...])
    left, right = put(act[...], rows, places)
    out[0, 0, :, :half] = left
    out[0, 0, :, half:] = right


def stack_kernel(*refs):
    for j, ref in enumerate(refs[:-1]):
        refs[-1][j] = ref[...]


def forward_kernel(near, far, up, down, cross_out, own_out, rows, total):
    period, half = near.shape[-2:]
    hidden_count = up.shape[1]
    chunk = min(CHUNK, hidden_count)
    stack_blocks([near, far], (), rows)
    x = rows[...]
    top = top_rows(x.shape[0], period)
    for low in range(0, hidden_count, chunk):
        n = slice(low, low + chunk)
        u = join_halves(dot(x, up[:half, n]), dot(x, up[half:, n]), period)
        hidden = u * jax.nn.sigmoid(u)
        left = jnp.where(top, hidden, 0.0).astype(BF16)
        right = jnp.where(top, 0.0, hidden).astype(BF16)
        part = dot(left, down[n, :half]) + dot(right, down[n, half:])
        total[...] = part if low == 0 else total[...] + part
    write_blocks(total, own_out, cross_out)


def write_blocks(total, own_out, cross_out):
    chips, period, _ = own_out.shape
    for j in range(chips):
        own_out[j] = total[j * period : (j + 1) * period, :]
        low = (chips + j) * period
        cross_out[j] = total[low : low + period, :].astype(BF16)


def backward_kernel(
    normed_place,
    grad_place,
    near_n,
    far_n,
    near_g,
    far_g,
    up,
    down,
    router,
    *refs,
):
    term_in = refs[:-6]
    cross_out, own_out, term_out, x_n, x_g, total = refs[-6:]
    period, half = own_out.shape[1:]
    all_rows = x_n.shape[0]
    hidden_count = up.shape[1]
    chunk = min(CHUNK, hidden_count)
    top = top_rows(all_rows, period)
    stack_blocks([near_n, far_n], normed_place, x_n)
    stack_blocks([near_g, far_g], grad_place, x_g)
    x = x_n[...]
    g = x_g[...]
    vector = jnp.where(top, router[:, :half], router[:, half:])
    logit = jnp.sum(x.astype(F32) * vector, axis=1, keepdims=True)
    wide = jnp.broadcast_to(logit, (all_rows, 128))
    gate = jax.nn.sigmoid(join_halves(wide, wide, period))
    inner = jnp.zeros((all_rows, 1), F32)
    for low in range(0, hidden_count, chunk):
        n = slice(low, low + chunk)
        u = join_halves(dot(x, up[:half, n]), dot(x, up[half:, n]), period)
        grad_hidden = join_halves(
            dot(g, down[n, :half], NT), dot(g, down[n, half:], NT), period
        )
        grad_hidden = grad_hidden * gate[:, :1]
        sig = jax.nn.sigmoid(u)
        hidden = (u * sig).astype(BF16).astype(F32)
        inner = inner + jnp.sum(grad_hidden * hidden, axis=1, keepdims=True)
        grad_up = grad_hidden * sig * (1.0 + u * (1.0 - sig))
        left = jnp.where(top, grad_up, 0.0).astype(BF16)
        right = jnp.where(top, 0.0, grad_up).astype(BF16)
        part = dot(left, up[:half, n], NT) + dot(right, up[half:, n], NT)
        total[...] = part if low == 0 else total[...] + part

    logit = inner * (1.0 - gate)
    total[...] += logit[:, :1] * vector
    write_blocks(total, own_out, cross_out)
    rest = logit.T[:1]
    first = lax.rem(lax.broadcasted_iota(jnp.int32, (1, all_rows), 1), period) < period // 2
    pieces = []
    for _ in range(3):
        piece = rest.astype(BF16).astype(F32)
        pieces.append(piece)
        rest = rest - piece
    sums = []
    for side in (first, jnp.logical_not(first)):
        stacked = jnp.concatenate(
            [jnp.where(side, p, 0.0) for p in pieces] + [jnp.zeros((5, all_rows), F32)], axis=0
        )
        sums.append(jnp.sum(dot(stacked.astype(BF16), x), axis=0, keepdims=True))
    term = jnp.concatenate(sums, axis=0)
    for before in term_in:
        term = term + before[...]
    term_out[...] = term


def pair_kernel(own, crossed, *outs):
    for j, out in enumerate(outs):
        out[...] = (own[j] + crossed[j].astype(F32)).astype(out.dtype)


def pair_and_saved_kernel(tick, own, crossed, later, *outs):
    for j, out in enumerate(outs):
        total = own[j] + crossed[j].astype(F32)
        if j == 0:
            out[...] = total
        else:
            out[0] = total.astype(BF16)
            out[1] = later[tick]


def stack_saved_kernel(tick, later, *refs):
    out = refs[-1]
    out[0] = later[tick]
    for j, ref in enumerate(refs[:-1]):
        out[j + 1] = ref[1]


def added(terms):
    total = terms[0][...]
    for term in terms[1:]:
        block = term[0] if len(term.shape) == 3 else term[...]
        total = total + block.astype(F32)
    return total


def forward_end_kernel(tick, rows, gate, routes, *refs):
    block = added(refs[:-1])
    renewed = (rows[...].astype(F32) + gate[:, :1] * block).astype(BF16)
    send_off(refs[-1], renewed, routes[0, tick, 0:1])


def backward_end_kernel(tick, upstream, saved, gain, routes, *refs):
    grad_normed = added(refs[:-1])
    picked = saved[tick].astype(F32)
    inv_rms = inverse_rms(picked)
    scaled_grad = grad_normed * by_half(gain[...], picked.shape[0])
    unit = picked * inv_rms
    mean = halves(jnp.sum(scaled_grad * unit, axis=1, keepdims=True)) / (2 * picked.shape[1])
    grad_rows = inv_rms * (scaled_grad - unit * mean)
    renewed = (upstream[...].astype(F32) + grad_rows).astype(BF16)
    send_off(refs[-1], renewed, routes[0, tick, 1:2])


def term_pair_kernel(near, far, out):
    out[...] = near[...] + far[...]


def term_end_kernel(scale, place, *refs):
    out = refs[-1]
    chips = len(refs) - 1
    chip = place[2:3, :1]
    total = jnp.zeros(refs[0].shape, F32)
    for low in range(chips):
        for j in range(chips):
            source = chip ^ j if in_pairs(chips) else lax.rem(chip - j + chips, chips)
            total = total + jnp.where(source == low, refs[j][...], 0.0)
    half = refs[0].shape[1]
    out[:, :half] = total[0:1] * scale
    out[:, half:] = total[1:2] * scale


class Order:
    def __init__(self):
        self.token = []

    def __call__(
        self, kernel, outs, *operands, smem=0, limit=8, scratch=(), cost=None, through=None
    ):
        count = len(self.token)
        passed = 0 if through is None else 1

        def body(*refs):
            kernel(*refs[count + passed : len(refs) - passed])

        in_specs = [ANY] * (count + passed)
        out_specs = jax.tree.map(lambda _: VMEM, outs)
        aliases = {}
        if passed:
            out_specs[-1] = ANY
            aliases = {count: len(outs) - 1}
            operands = (through, *operands)
        result = pl.pallas_call(
            body,
            out_shape=outs,
            in_specs=in_specs + [SMEM] * smem + [VMEM] * (len(operands) - smem - passed),
            out_specs=out_specs,
            input_output_aliases=aliases,
            scratch_shapes=scratch,
            compiler_params=pltpu.CompilerParams(vmem_limit_bytes=limit * 2**20),
            cost_estimate=cost or SMALL,
        )(*self.token, *operands)
        several = isinstance(result, (list, tuple))
        self.token = [result[-1 - passed] if several else result]
        return result

    def write(self, result, tick, ticks, act, moved):
        before = [] if result is None else [result]
        tokens, width = act.shape
        token, result = pl.pallas_call(
            output_kernel,
            grid=(1,),
            out_shape=[shaped((8, LANES), F32), shaped((1, ticks, tokens, width))],
            in_specs=[ANY, whole(act.shape), whole(moved.shape)] + [ANY] * len(before),
            out_specs=[
                whole((8, LANES)),
                pl.BlockSpec((1, 1, tokens, width), lambda i: (0, tick, 0, 0)),
            ],
            input_output_aliases={3: 1} if before else {},
            compiler_params=pltpu.CompilerParams(vmem_limit_bytes=8 * 2**20),
            cost_estimate=SMALL,
        )(*self.token, act, moved, *before)
        self.token = [token]
        return result


def shaped(shape, dtype=BF16):
    return jax.ShapeDtypeStruct(tuple(shape), dtype)


def whole(shape):
    return pl.BlockSpec(tuple(shape), lambda i: (0,) * len(shape))


def cost_of(matmuls, rows, weight):
    size = weight.shape[0] * weight.shape[1]
    return pl.CostEstimate(
        flops=4 * matmuls * rows * size,
        bytes_accessed=4 * size,
        transcendentals=rows * weight.shape[1],
    )


def per_device(
    arrive, entering, stash, back_arrive, head_grad, norm_gain, router, w_up, w_down, routes
):
    section = lax.axis_index("section")
    last = lax.axis_size("section") - 1
    dp_count = lax.axis_size("dp")
    chips = dp_count // CORES
    up, down = w_up[0], w_down[0]
    slots = routes.shape[3]
    tokens, width = arrive.shape[1:]
    half = width // 2
    ticks = stash.shape[1]
    period = 2 * slots
    flags = jnp.stack(
        [
            (section == 0).astype(jnp.int32),
            (section == last).astype(jnp.int32),
            lax.axis_index("dp") // CORES,
        ]
    )

    packed = shaped((period, half))
    packed_sum = shaped((period, half), F32)
    packet = shaped((period, half + LANES))
    full = shaped((tokens, width))
    gate_shape = shaped((period, LANES), F32)
    part_outs = [shaped((chips, period, half)), shaped((chips, period, half), F32)]
    all_rows = dp_count * period
    scratch_rows = pltpu.VMEM((all_rows, half), BF16)
    scratch_total = pltpu.VMEM((all_rows, half), F32)
    run = Order()

    def stacked(blocks):
        return run(stack_kernel, shaped((len(blocks), *blocks[0].shape)), *blocks)

    def pair(own, crossed):
        outs = [packed_sum] + [packed] * (chips - 1)
        return collect(run(pair_kernel, outs, own, crossed))

    forward_in, backward_in = arrive[0], back_arrive[0]
    forward_normed, forward_rows, gate, place = run(
        first_forward_kernel,
        [packed, packed, gate_shape, shaped((8, LANES), jnp.int32)],
        flags,
        forward_in,
        routes,
        norm_gain,
        router,
        smem=1,
    )
    forward_blocks = spread(forward_normed)
    saved_first, saved_later, backward_rows, saved = run(
        first_backward_kernel,
        [
            shaped((2, period, half)),
            shaped((ticks - 1, period, half)),
            packed,
            shaped((ticks, period, half)),
        ],
        backward_in,
        stash[0],
        routes,
        norm_gain,
        limit=16,
    )
    backward_blocks = spread(saved_first)
    term = []
    forward_out = backward_out = None
    forward_base = shift_section(forward_in, 1)
    backward_base = shift_section(backward_in, -1)
    near_f = stacked(forward_blocks)
    far_f = swap_core(near_f)

    for k in range(ticks):
        more = k + 1 < ticks
        if k > 0:
            forward_in = run(
                functools.partial(land_kernel, 0), full, forward_in, forward_moved, place
            )
            if more:
                forward_base = shift_section(forward_in, 1)
        cross, own = run(
            forward_kernel,
            part_outs,
            near_f,
            far_f,
            up,
            down,
            limit=WEIGHTS_LIMIT,
            scratch=[scratch_rows, scratch_total],
            cost=cost_of(2, all_rows, up),
        )
        crossed = swap_core(cross)
        near_b = stacked(backward_blocks)
        far_b = swap_core(near_b)
        if more:
            outs = [packed_sum] + [shaped((2, period, half))] * (chips - 1)
            terms = collect(
                run(
                    functools.partial(pair_and_saved_kernel, k), outs, own, crossed, saved_later
                )
            )
        else:
            terms = pair(own, crossed)
        if k > 0:
            backward_in = run(
                functools.partial(land_kernel, 1), full, backward_in, backward_moved, place
            )
            if more:
                backward_base = shift_section(backward_in, -1)

        near_n, far_n, normed_place = (near_s, far_s, ()) if k else (near_b, far_b, (0,))
        cross, own, part = run(
            functools.partial(backward_kernel, normed_place, () if k else (1,)),
            part_outs + [shaped((2, half), F32)],
            near_n,
            far_n,
            near_b,
            far_b,
            up,
            down,
            router,
            *term,
            limit=WEIGHTS_LIMIT,
            scratch=[scratch_rows, scratch_rows, scratch_total],
            cost=cost_of(3, all_rows, up),
        )
        term = [part]
        forward_new, cross = run(
            functools.partial(forward_end_kernel, k),
            [packet, shaped(cross.shape)],
            forward_rows,
            gate,
            routes,
            *terms,
            through=cross,
        )
        crossed = swap_core(cross)
        if more:
            forward_moved = shift_section(forward_new, 1)
            came = terms[1:] if in_pairs(chips) else terms[:0:-1]
            near_s = run(
                functools.partial(stack_saved_kernel, k),
                shaped((chips, period, half)),
                saved_later,
                *came,
            )
            far_s = swap_core(near_s)
            forward_next, forward_picked = run(
                functools.partial(source_kernel, k + 1, 0),
                [full, packed],
                place,
                forward_base,
                entering,
                routes,
            )
        else:
            total = run(term_pair_kernel, shaped((2, half), F32), part, swap_core(part))
        terms = pair(own, crossed)

        if more:
            forward_normed, forward_rows, gate = run(
                functools.partial(next_forward_kernel, k + 1),
                [packed, packed, gate_shape],
                forward_picked,
                forward_moved,
                place,
                routes,
                norm_gain,
                router,
            )
            forward_blocks = spread(forward_normed)
            backward_next, backward_picked = run(
                functools.partial(source_kernel, k + 1, 1),
                [full, packed],
                place,
                backward_base,
                head_grad,
                routes,
            )
        else:
            total_blocks = spread(total)
        forward_out = run.write(forward_out, k, ticks, forward_in, forward_new)

        backward_new = run(
            functools.partial(backward_end_kernel, k),
            packet,
            backward_rows,
            saved,
            norm_gain,
            routes,
            *terms,
        )
        if more:
            backward_moved = shift_section(backward_new, -1)
            backward_rows = run(
                functools.partial(next_backward_kernel, k + 1),
                packed,
                backward_picked,
                backward_moved,
                place,
                routes,
            )
            backward_blocks = spread(backward_rows)
            near_f = stacked(forward_blocks)
            far_f = swap_core(near_f)
        backward_out = run.write(backward_out, k, ticks, backward_in, backward_new)
        if more:
            forward_in, backward_in = forward_next, backward_next

    scale = 1.0 / float(ticks * slots * dp_count)
    router_grad = run(
        functools.partial(term_end_kernel, scale), shaped((1, width), F32), place, *total_blocks
    )
    return forward_out, backward_out, router_grad


def solution(mesh):
    in_specs = (
        P("section", "dp", None),
        P(None, "dp", None),
        P("section", None, "dp", None),
        P("section", "dp", None),
        P(None, "dp", None),
        P("section", None),
        P("section", None),
        P("section", None, "dp"),
        P("section", "dp", None),
        P("section", None, None, "dp"),
    )
    out_specs = (P("section", None, "dp", None), P("section", None, "dp", None), P("section", None))
    return jax.shard_map(
        per_device, mesh=mesh, in_specs=in_specs, out_specs=out_specs, check_vma=False
    )
```

```python
import functools

import jax
import jax.numpy as jnp
from jax import lax
from jax.experimental import pallas as pl
from jax.experimental.pallas import tpu as pltpu
from jax.sharding import PartitionSpec as P

EPS = 1e-05
CORES = 2
CHUNK = 256
LANES = 128
WEIGHTS_LIMIT = 26
BF16 = jnp.bfloat16
F32 = jnp.float32
NN = (((1,), (0,)), ((), ()))
NT = (((1,), (1,)), ((), ()))
VMEM = pl.BlockSpec(memory_space=pltpu.VMEM)
SMEM = pl.BlockSpec(memory_space=pltpu.SMEM)
ANY = pl.BlockSpec(memory_space=pl.ANY)
SMALL = pl.CostEstimate(flops=0, bytes_accessed=2 * 2**20, transcendentals=0)


def shift_section(block, step):
    count = lax.axis_size("section")
    return lax.ppermute(block, "section", [(i, (i + step) % count) for i in range(count)])


def swap_core(block):
    count = lax.axis_size("dp")
    return lax.ppermute(block, "dp", [(i, i ^ 1) for i in range(count)])


def shift_chip(block, step):
    count = lax.axis_size("dp")
    return lax.ppermute(block, "dp", [(i, (i + CORES * step) % count) for i in range(count)])


def spread(block):
    return [block] + [shift_chip(block, j) for j in range(1, lax.axis_size("dp") // CORES)]


def collect(blocks):
    return [blocks[0]] + [shift_chip(b, -j) for j, b in enumerate(blocks) if j > 0]


def dot(a, b, dims=NN):
    return lax.dot_general(a, b, dims, preferred_element_type=F32)


def halves(column):
    rows = column.shape[0]
    wide = jnp.broadcast_to(column, (rows, 128))
    return (wide + pltpu.roll(wide, rows // 2, 0))[:, :1]


def column_of(route):
    slots = route.shape[1]
    row = lax.rem(lax.broadcasted_iota(jnp.int32, (2 * slots, slots), 0), slots)
    same = row == lax.broadcasted_iota(jnp.int32, (2 * slots, slots), 1)
    return jnp.sum(jnp.where(same, route, 0), axis=1, keepdims=True)


def row_of(column):
    count = column.shape[0]
    shape = (count, count)
    same = lax.broadcasted_iota(jnp.int32, shape, 0) == lax.broadcasted_iota(jnp.int32, shape, 1)
    return jnp.sum(jnp.where(same, column, 0), axis=0, keepdims=True)


def arrived(moved, at_end=None):
    half = moved.shape[1] - LANES
    place = row_of(moved[:, half : half + 1].astype(F32).astype(jnp.int32)) - 1
    none = place < 0
    if at_end is not None:
        none = none | (at_end == 1)
    return moved[:, :half], jnp.where(none, -2, place)


def send_off(out, rows, route):
    half = rows.shape[1]
    out[:, :half] = rows
    place = (column_of(route) + 1).astype(F32).astype(BF16)
    out[:, half:] = jnp.broadcast_to(place, (rows.shape[0], LANES))


def top_rows(rows, period):
    return lax.rem(lax.broadcasted_iota(jnp.int32, (rows, 1), 0), period) < period // 2


def pick(activity, route_column):
    rows, half = route_column.shape[0], activity.shape[1] // 2
    tokens = activity.shape[0]
    hit = route_column == lax.broadcasted_iota(jnp.int32, (rows, tokens), 1)
    top = top_rows(rows, rows)
    left = jnp.where(hit & top, 1.0, 0.0).astype(BF16)
    right = jnp.where(hit & jnp.logical_not(top), 1.0, 0.0).astype(BF16)
    return dot(left, activity[:, :half]) + dot(right, activity[:, half:])


def put(activity, rows, route_row):
    tokens, half = activity.shape[0], activity.shape[1] // 2
    count = route_row.shape[1]
    hit = route_row == lax.broadcasted_iota(jnp.int32, (tokens, count), 0)
    first = lax.broadcasted_iota(jnp.int32, (tokens, count), 1) < count // 2
    left = jnp.where(hit & first, 1.0, 0.0)
    right = jnp.where(hit & jnp.logical_not(first), 1.0, 0.0)
    taken = jnp.sum(left, axis=1, keepdims=True) > 0.5
    new_left = jnp.where(taken, dot(left.astype(BF16), rows), activity[:, :half].astype(F32))
    new_right = jnp.where(taken, dot(right.astype(BF16), rows), activity[:, half:].astype(F32))
    return new_left.astype(BF16), new_right.astype(BF16)


def by_half(vector, rows):
    half = vector.shape[1] // 2
    return jnp.where(top_rows(rows, rows), vector[:, :half], vector[:, half:])


def inverse_rms(rows):
    width = 2 * rows.shape[1]
    mean = halves(jnp.sum(rows * rows, axis=1, keepdims=True)) / width
    return lax.rsqrt(mean + EPS)


def normalize(rows, gain, router):
    normed = (rows * inverse_rms(rows) * by_half(gain, rows.shape[0])).astype(BF16)
    logit = jnp.sum(normed.astype(F32) * by_half(router, rows.shape[0]), axis=1, keepdims=True)
    return normed, jax.nn.sigmoid(halves(logit))


def stack_blocks(refs, place, out):
    blocks = [ref[(j, *place)].astype(F32) for ref in refs for j in range(ref.shape[0])]
    out[...] = jnp.concatenate(blocks, axis=0).astype(BF16)


def join_halves(left, right, period):
    rows = left.shape[0]
    top = top_rows(rows, period)
    return jnp.where(
        top,
        left + pltpu.roll(right, rows - period // 2, 0),
        right + pltpu.roll(left, period // 2, 0),
    )


def first_forward_kernel(flags, act, routes, gain, router, normed_out, rows_out, gate_out, where_out):
    rows = pick(act[...], column_of(routes[0, 0, 0:1]))
    normed, gate = normalize(rows, gain[...], router[...])
    rows_out[...] = rows.astype(BF16)
    normed_out[...] = normed
    gate_out[...] = jnp.broadcast_to(gate, gate_out.shape)
    line = lax.broadcasted_iota(jnp.int32, where_out.shape, 0)
    where_out[...] = jnp.where(line == 0, flags[0], jnp.where(line == 1, flags[1], flags[2]))


def first_backward_kernel(act, stash, routes, gain, first_out, later_out, rows_out, saved_out):
    ticks = stash.shape[0]
    upstream = pick(act[...], column_of(routes[0, 0, 1:2])).astype(BF16)
    rows_out[...] = upstream
    first_out[1] = upstream
    for k in range(ticks):
        rows = pick(stash[k], column_of(routes[0, k, 1:2]))
        saved_out[k] = rows.astype(BF16)
        count = rows.shape[0]
        normed = (rows * inverse_rms(rows) * by_half(gain[...], count)).astype(BF16)
        if k == 0:
            first_out[0] = normed
        else:
            later_out[k - 1] = normed


def source_kernel(tick, way, place, moved, fresh, routes, source_out, rows_out):
    source = jnp.where(place[way : way + 1, :1] == 1, fresh[tick - 1], moved[...])
    source_out[...] = source
    rows_out[...] = pick(source, column_of(routes[0, tick, way : way + 1])).astype(BF16)


def select(base, packet, route, at_end):
    moved, behind_row = arrived(packet, at_end)
    column = column_of(route)
    rows = column.shape[0]
    hit = column == behind_row
    same = top_rows(rows, rows) == (lax.broadcasted_iota(jnp.int32, (rows, rows), 1) < rows // 2)
    match = jnp.where(hit & same, 1.0, 0.0)
    found = jnp.max(match, axis=1, keepdims=True) > 0.5
    return jnp.where(found, dot(match.astype(BF16), moved), base.astype(F32))


def next_forward_kernel(
    tick, base, moved, place, later, routes, gain, router, normed_out, rows_out, gate_out
):
    rows = select(base[...], moved[...], routes[0, tick, 0:1], place[0:1, :1])
    normed, gate = normalize(rows, gain[...], router[...])
    rows_out[...] = rows.astype(BF16)
    normed_out[0] = normed
    normed_out[1] = later[tick - 1]
    gate_out[...] = jnp.broadcast_to(gate, gate_out.shape)


def next_backward_kernel(tick, base, moved, place, routes, rows_out):
    rows = select(base[...], moved[...], routes[0, tick, 1:2], place[1:2, :1])
    rows_out[...] = rows.astype(BF16)


def land_kernel(way, source, moved, place, out):
    half = source.shape[1] // 2
    rows, places = arrived(moved[...], place[way : way + 1, :1])
    left, right = put(source[...], rows, places)
    out[:, :half] = left
    out[:, half:] = right


def output_kernel(token, act, moved, *outs):
    done, out = outs[-2:]
    done[...] = jnp.zeros_like(done)
    half = act.shape[1] // 2
    rows, places = arrived(moved[...])
    left, right = put(act[...], rows, places)
    out[0, 0, :, :half] = left
    out[0, 0, :, half:] = right


def stack_kernel(*refs):
    for j, ref in enumerate(refs[:-1]):
        refs[-1][j] = ref[...]


def forward_kernel(place, near, far, up, down, cross_out, own_out, rows, total):
    period, half = near.shape[-2:]
    hidden_count = up.shape[1]
    chunk = min(CHUNK, hidden_count)
    stack_blocks([near, far], place, rows)
    x = rows[...]
    top = top_rows(x.shape[0], period)
    for low in range(0, hidden_count, chunk):
        n = slice(low, low + chunk)
        u = join_halves(dot(x, up[:half, n]), dot(x, up[half:, n]), period)
        hidden = u * jax.nn.sigmoid(u)
        left = jnp.where(top, hidden, 0.0).astype(BF16)
        right = jnp.where(top, 0.0, hidden).astype(BF16)
        part = dot(left, down[n, :half]) + dot(right, down[n, half:])
        total[...] = part if low == 0 else total[...] + part
    write_blocks(total, own_out, cross_out)


def write_blocks(total, own_out, cross_out):
    chips, period, _ = own_out.shape
    for j in range(chips):
        own_out[j] = total[j * period : (j + 1) * period, :]
        low = (chips + j) * period
        cross_out[j] = total[low : low + period, :].astype(BF16)


def backward_kernel(
    normed_place,
    grad_place,
    near_n,
    far_n,
    near_g,
    far_g,
    up,
    down,
    router,
    *refs,
):
    term_in = refs[:-6]
    cross_out, own_out, term_out, x_n, x_g, total = refs[-6:]
    period, half = own_out.shape[1:]
    all_rows = x_n.shape[0]
    hidden_count = up.shape[1]
    chunk = min(CHUNK, hidden_count)
    top = top_rows(all_rows, period)
    stack_blocks([near_n, far_n], normed_place, x_n)
    stack_blocks([near_g, far_g], grad_place, x_g)
    x = x_n[...]
    g = x_g[...]
    vector = jnp.where(top, router[:, :half], router[:, half:])
    logit = jnp.sum(x.astype(F32) * vector, axis=1, keepdims=True)
    wide = jnp.broadcast_to(logit, (all_rows, 128))
    gate = jax.nn.sigmoid(join_halves(wide, wide, period))
    inner = jnp.zeros((all_rows, 1), F32)
    for low in range(0, hidden_count, chunk):
        n = slice(low, low + chunk)
        u = join_halves(dot(x, up[:half, n]), dot(x, up[half:, n]), period)
        grad_hidden = join_halves(
            dot(g, down[n, :half], NT), dot(g, down[n, half:], NT), period
        )
        grad_hidden = grad_hidden * gate[:, :1]
        sig = jax.nn.sigmoid(u)
        hidden = (u * sig).astype(BF16).astype(F32)
        inner = inner + jnp.sum(grad_hidden * hidden, axis=1, keepdims=True)
        grad_up = grad_hidden * sig * (1.0 + u * (1.0 - sig))
        left = jnp.where(top, grad_up, 0.0).astype(BF16)
        right = jnp.where(top, 0.0, grad_up).astype(BF16)
        part = dot(left, up[:half, n], NT) + dot(right, up[half:, n], NT)
        total[...] = part if low == 0 else total[...] + part

    logit = inner * (1.0 - gate)
    total[...] += logit[:, :1] * vector
    write_blocks(total, own_out, cross_out)
    rest = logit.T[:1]
    first = lax.rem(lax.broadcasted_iota(jnp.int32, (1, all_rows), 1), period) < period // 2
    pieces = []
    for _ in range(3):
        piece = rest.astype(BF16).astype(F32)
        pieces.append(piece)
        rest = rest - piece
    sums = []
    for side in (first, jnp.logical_not(first)):
        stacked = jnp.concatenate(
            [jnp.where(side, p, 0.0) for p in pieces] + [jnp.zeros((5, all_rows), F32)], axis=0
        )
        sums.append(jnp.sum(dot(stacked.astype(BF16), x), axis=0, keepdims=True))
    term = jnp.concatenate(sums, axis=0)
    for before in term_in:
        term = term + before[...]
    term_out[...] = term


def pair_kernel(own, crossed, *outs):
    for j, out in enumerate(outs):
        out[...] = (own[j] + crossed[j].astype(F32)).astype(out.dtype)


def added(terms):
    total = terms[0][...]
    for term in terms[1:]:
        total = total + term[...].astype(F32)
    return total


def forward_end_kernel(tick, rows, gate, routes, *refs):
    block = added(refs[:-1])
    renewed = (rows[...].astype(F32) + gate[:, :1] * block).astype(BF16)
    send_off(refs[-1], renewed, routes[0, tick, 0:1])


def backward_end_kernel(tick, upstream, saved, gain, routes, *refs):
    grad_normed = added(refs[:-1])
    picked = saved[tick].astype(F32)
    inv_rms = inverse_rms(picked)
    scaled_grad = grad_normed * by_half(gain[...], picked.shape[0])
    unit = picked * inv_rms
    mean = halves(jnp.sum(scaled_grad * unit, axis=1, keepdims=True)) / (2 * picked.shape[1])
    grad_rows = inv_rms * (scaled_grad - unit * mean)
    renewed = (upstream[...].astype(F32) + grad_rows).astype(BF16)
    send_off(refs[-1], renewed, routes[0, tick, 1:2])


def term_pair_kernel(near, far, out):
    out[...] = near[...] + far[...]


def term_end_kernel(scale, place, *refs):
    out = refs[-1]
    chips = len(refs) - 1
    chip = place[2:3, :1]
    total = jnp.zeros(refs[0].shape, F32)
    for low in range(chips):
        for j in range(chips):
            total = total + jnp.where(lax.rem(chip - j + chips, chips) == low, refs[j][...], 0.0)
    half = refs[0].shape[1]
    out[:, :half] = total[0:1] * scale
    out[:, half:] = total[1:2] * scale


class Order:
    def __init__(self):
        self.token = []

    def __call__(
        self, kernel, outs, *operands, smem=0, limit=8, scratch=(), cost=None, through=None
    ):
        count = len(self.token)
        passed = 0 if through is None else 1

        def body(*refs):
            kernel(*refs[count + passed : len(refs) - passed])

        in_specs = [ANY] * (count + passed)
        out_specs = jax.tree.map(lambda _: VMEM, outs)
        aliases = {}
        if passed:
            out_specs[-1] = ANY
            aliases = {count: len(outs) - 1}
            operands = (through, *operands)
        result = pl.pallas_call(
            body,
            out_shape=outs,
            in_specs=in_specs + [SMEM] * smem + [VMEM] * (len(operands) - smem - passed),
            out_specs=out_specs,
            input_output_aliases=aliases,
            scratch_shapes=scratch,
            compiler_params=pltpu.CompilerParams(vmem_limit_bytes=limit * 2**20),
            cost_estimate=cost or SMALL,
        )(*self.token, *operands)
        several = isinstance(result, (list, tuple))
        self.token = [result[-1 - passed] if several else result]
        return result

    def write(self, result, tick, ticks, act, moved):
        before = [] if result is None else [result]
        tokens, width = act.shape
        token, result = pl.pallas_call(
            output_kernel,
            grid=(1,),
            out_shape=[shaped((8, LANES), F32), shaped((1, ticks, tokens, width))],
            in_specs=[ANY, whole(act.shape), whole(moved.shape)] + [ANY] * len(before),
            out_specs=[
                whole((8, LANES)),
                pl.BlockSpec((1, 1, tokens, width), lambda i: (0, tick, 0, 0)),
            ],
            input_output_aliases={3: 1} if before else {},
            compiler_params=pltpu.CompilerParams(vmem_limit_bytes=8 * 2**20),
            cost_estimate=SMALL,
        )(*self.token, act, moved, *before)
        self.token = [token]
        return result


def shaped(shape, dtype=BF16):
    return jax.ShapeDtypeStruct(tuple(shape), dtype)


def whole(shape):
    return pl.BlockSpec(tuple(shape), lambda i: (0,) * len(shape))


def cost_of(matmuls, rows, weight):
    size = weight.shape[0] * weight.shape[1]
    return pl.CostEstimate(
        flops=4 * matmuls * rows * size,
        bytes_accessed=4 * size,
        transcendentals=rows * weight.shape[1],
    )


def per_device(
    arrive, entering, stash, back_arrive, head_grad, norm_gain, router, w_up, w_down, routes
):
    section = lax.axis_index("section")
    last = lax.axis_size("section") - 1
    dp_count = lax.axis_size("dp")
    chips = dp_count // CORES
    up, down = w_up[0], w_down[0]
    slots = routes.shape[3]
    tokens, width = arrive.shape[1:]
    half = width // 2
    ticks = stash.shape[1]
    period = 2 * slots
    flags = jnp.stack(
        [
            (section == 0).astype(jnp.int32),
            (section == last).astype(jnp.int32),
            lax.axis_index("dp") // CORES,
        ]
    )

    packed = shaped((period, half))
    packed_sum = shaped((period, half), F32)
    packet = shaped((period, half + LANES))
    full = shaped((tokens, width))
    gate_shape = shaped((period, LANES), F32)
    part_outs = [shaped((chips, period, half)), shaped((chips, period, half), F32)]
    all_rows = dp_count * period
    scratch_rows = pltpu.VMEM((all_rows, half), BF16)
    scratch_total = pltpu.VMEM((all_rows, half), F32)
    run = Order()

    def stacked(blocks):
        return run(stack_kernel, shaped((len(blocks), *blocks[0].shape)), *blocks)

    def pair(own, crossed):
        outs = [packed_sum] + [packed] * (chips - 1)
        return collect(run(pair_kernel, outs, own, crossed))

    forward_in, backward_in = arrive[0], back_arrive[0]
    forward_normed, forward_rows, gate, place = run(
        first_forward_kernel,
        [packed, packed, gate_shape, shaped((8, LANES), jnp.int32)],
        flags,
        forward_in,
        routes,
        norm_gain,
        router,
        smem=1,
    )
    forward_blocks = spread(forward_normed)
    saved_first, saved_later, backward_rows, saved = run(
        first_backward_kernel,
        [
            shaped((2, period, half)),
            shaped((ticks - 1, period, half)),
            packed,
            shaped((ticks, period, half)),
        ],
        backward_in,
        stash[0],
        routes,
        norm_gain,
        limit=16,
    )
    backward_blocks = spread(saved_first)
    term = []
    forward_out = backward_out = None
    forward_base = shift_section(forward_in, 1)
    backward_base = shift_section(backward_in, -1)
    near_f = stacked(forward_blocks)
    far_f = swap_core(near_f)

    for k in range(ticks):
        more = k + 1 < ticks
        if k > 0:
            forward_in = run(
                functools.partial(land_kernel, 0), full, forward_in, forward_moved, place
            )
            if more:
                forward_base = shift_section(forward_in, 1)
        cross, own = run(
            functools.partial(forward_kernel, (0,) if k else ()),
            part_outs,
            near_f,
            far_f,
            up,
            down,
            limit=WEIGHTS_LIMIT,
            scratch=[scratch_rows, scratch_total],
            cost=cost_of(2, all_rows, up),
        )
        crossed = swap_core(cross)
        near_b = stacked(backward_blocks)
        far_b = swap_core(near_b)
        terms = pair(own, crossed)
        if k > 0:
            backward_in = run(
                functools.partial(land_kernel, 1), full, backward_in, backward_moved, place
            )
            if more:
                backward_base = shift_section(backward_in, -1)

        near_n, far_n, normed_place = (near_f, far_f, (1,)) if k else (near_b, far_b, (0,))
        cross, own, part = run(
            functools.partial(backward_kernel, normed_place, () if k else (1,)),
            part_outs + [shaped((2, half), F32)],
            near_n,
            far_n,
            near_b,
            far_b,
            up,
            down,
            router,
            *term,
            limit=WEIGHTS_LIMIT,
            scratch=[scratch_rows, scratch_rows, scratch_total],
            cost=cost_of(3, all_rows, up),
        )
        term = [part]
        forward_new, cross = run(
            functools.partial(forward_end_kernel, k),
            [packet, shaped(cross.shape)],
            forward_rows,
            gate,
            routes,
            *terms,
            through=cross,
        )
        crossed = swap_core(cross)
        if more:
            forward_moved = shift_section(forward_new, 1)
            forward_next, forward_picked = run(
                functools.partial(source_kernel, k + 1, 0),
                [full, packed],
                place,
                forward_base,
                entering,
                routes,
            )
        else:
            total = run(term_pair_kernel, shaped((2, half), F32), part, swap_core(part))
        terms = pair(own, crossed)

        if more:
            forward_normed, forward_rows, gate = run(
                functools.partial(next_forward_kernel, k + 1),
                [shaped((2, period, half)), packed, gate_shape],
                forward_picked,
                forward_moved,
                place,
                saved_later,
                routes,
                norm_gain,
                router,
            )
            forward_blocks = spread(forward_normed)
            backward_next, backward_picked = run(
                functools.partial(source_kernel, k + 1, 1),
                [full, packed],
                place,
                backward_base,
                head_grad,
                routes,
            )
        else:
            total_blocks = spread(total)
        forward_out = run.write(forward_out, k, ticks, forward_in, forward_new)

        backward_new = run(
            functools.partial(backward_end_kernel, k),
            packet,
            backward_rows,
            saved,
            norm_gain,
            routes,
            *terms,
        )
        if more:
            backward_moved = shift_section(backward_new, -1)
            backward_rows = run(
                functools.partial(next_backward_kernel, k + 1),
                packed,
                backward_picked,
                backward_moved,
                place,
                routes,
            )
            backward_blocks = spread(backward_rows)
            near_f = stacked(forward_blocks)
            far_f = swap_core(near_f)
        backward_out = run.write(backward_out, k, ticks, backward_in, backward_new)
        if more:
            forward_in, backward_in = forward_next, backward_next

    scale = 1.0 / float(ticks * slots * dp_count)
    router_grad = run(
        functools.partial(term_end_kernel, scale), shaped((1, width), F32), place, *total_blocks
    )
    return forward_out, backward_out, router_grad


def solution(mesh):
    in_specs = (
        P("section", "dp", None),
        P(None, "dp", None),
        P("section", None, "dp", None),
        P("section", "dp", None),
        P(None, "dp", None),
        P("section", None),
        P("section", None),
        P("section", None, "dp"),
        P("section", "dp", None),
        P("section", None, None, "dp"),
    )
    out_specs = (P("section", None, "dp", None), P("section", None, "dp", None), P("section", None))
    return jax.shard_map(
        per_device, mesh=mesh, in_specs=in_specs, out_specs=out_specs, check_vma=False
    )
```
